32 devices in a mesh: rows: 16 (over z, x, core), cols: 2 (over y).
Axes of the slice: x: 2, y: 2, z: 4, core: 2. Of those that a mesh axis runs over, the one named last changes fastest.
Arguments:
- ancestor: bfloat16 [24576, 24576], P('rows', 'cols'), may hold values from -6 to 6
- panel_below: bfloat16 [2048, 512], P('rows'), may hold values from -0.0625 to 0.0625
- panel_beside: bfloat16 [2048, 512], P('rows'), may hold values from -0.0625 to 0.0625
- inverse_lower: bfloat16 [512, 512], replicated, may hold values from -3 to 3
- inverse_upper: bfloat16 [512, 512], replicated, may hold values from -3 to 3
- list_below: int32 [16], replicated, may hold values from 0 to 191, as said below
- list_beside: int32 [16], replicated, may hold values from 0 to 191, as said below
- second_below: bfloat16 [2048, 512], P('rows'), may hold values from -0.0625 to 0.0625
- second_beside: bfloat16 [2048, 512], P('rows'), may hold values from -0.0625 to 0.0625
- linked_below: bfloat16 [512, 512], replicated, may hold values from -0.0625 to 0.0625
- linked_beside: bfloat16 [512, 512], replicated, may hold values from -0.0625 to 0.0625
- second_lower: bfloat16 [512, 512], replicated, may hold values from -3 to 3
- second_upper: bfloat16 [512, 512], replicated, may hold values from -3 to 3
- blocks_below: int32 [16], replicated, may hold values from 0 to 191, as said below
- blocks_beside: int32 [16], replicated, may hold values from 0 to 191, as said below
Outputs:
- new_lower: bfloat16 [24576, 512], P('rows', 'cols')
- new_upper: bfloat16 [24576, 512], P(('cols', 'rows'))
- new_diagonal: bfloat16 [512, 512], P(None, 'cols')
- next_lower: bfloat16 [24576, 512], P('rows', 'cols')
- next_upper: bfloat16 [24576, 512], P(('cols', 'rows'))
- next_link: bfloat16 [512, 512], replicated
- next_diagonal: bfloat16 [512, 512], P(None, 'cols')
The draws below stay inside these ranges and needn't reach their ends.
Inputs may be any that keep to these rules, and one draw needn't show every extreme that they name: `list_below`: 16 distinct block numbers in ascending order; block 0 and block 191 are always listed. `list_beside`: 16 distinct block numbers in ascending order; block 0 and block 191 are always listed. `blocks_below`: 16 distinct block numbers in ascending order; block 0 and block 191 are always listed. `blocks_beside`: 16 distinct block numbers in ascending order; block 0 and block 191 are always listed.
All inputs are finite; a program needn't handle non-finite values.
Results may differ from the reference program's by a relative error of at most 0.0077.
Values may be sent and summed in bfloat16 or wider, within the bound.
No kernel may reach another device: no remote copies, remote signals or barrier semaphores. Data moves between devices by JAX's collectives and lax.ppermute only.
A program may use at most 256 MiB of HBM per device.

```python
import jax
import jax.numpy as jnp

M = 24576
W = 512
BLK = 128
R = 16
P_SIZE = 2048


def pick_blocks(key, salt_value):
    folded = jax.random.fold_in(key, salt_value)
    shuffled = jax.random.permutation(folded, M // BLK - 2) + 1
    chosen = shuffled[:R - 2].astype(jnp.int32)
    listed = jnp.concatenate([jnp.zeros((1,), jnp.int32), chosen, jnp.full((1,), M // BLK - 1, jnp.int32)])
    return jnp.sort(listed)


def draw_list_below(key, part):
    return pick_blocks(key, 11)


def draw_list_beside(key, part):
    return pick_blocks(key, 23)


def draw_blocks_below(key, part):
    return pick_blocks(key, 37)


def draw_blocks_beside(key, part):
    return pick_blocks(key, 41)


def level_of(key, shape, split, low, top_value):
    loudness = 1.0
    for axis_at, shards_of in split:
        draws = jax.random.uniform(jax.random.fold_in(jax.random.fold_in(key, 6), axis_at), (shards_of,), jnp.float32, low / len(split), top_value / len(split))
        loudness = loudness * jnp.repeat(jnp.exp(draws), shape[axis_at] // shards_of).reshape((-1,) + (1,) * (len(shape) - 1 - axis_at))
    return loudness


def normal_values(own_key, dims, deviation, limit, cuts=(), dtype=jnp.bfloat16):
    drawn = deviation * jax.random.normal(own_key, dims, jnp.float32)
    if cuts:
        drawn = drawn * level_of(own_key, dims, cuts, -0.22, 0.18)
    return jnp.clip(drawn, -limit, limit).astype(dtype)


def setup_inputs(seed: int = 0) -> dict:
    keys = jax.random.split(jax.random.key(seed), 16)
    return {
        "ancestor": normal_values(keys[0], (M, M), 1.0, 6.0, ((0, 16), (1, 2))),
        "panel_below": normal_values(keys[1], (P_SIZE, W), ((R * BLK) ** -0.5 * W ** -0.25), 0.0625, ((0, 16),)),
        "panel_beside": normal_values(keys[2], (P_SIZE, W), ((R * BLK) ** -0.5 * W ** -0.25), 0.0625, ((0, 16),)),
        "inverse_lower": normal_values(keys[3], (W, W), (W ** -0.25), 3.0),
        "inverse_upper": normal_values(keys[4], (W, W), (W ** -0.25), 3.0),
        "list_below": draw_list_below(jax.random.fold_in(keys[15], 71), 0),
        "list_beside": draw_list_beside(jax.random.fold_in(keys[15], 71), 0),
        "second_below": normal_values(keys[7], (P_SIZE, W), ((R * BLK) ** -0.5 * W ** -0.25), 0.0625, ((0, 16),)),
        "second_beside": normal_values(keys[8], (P_SIZE, W), ((R * BLK) ** -0.5 * W ** -0.25), 0.0625, ((0, 16),)),
        "linked_below": normal_values(keys[9], (W, W), ((R * BLK) ** -0.5 * W ** -0.25), 0.0625),
        "linked_beside": normal_values(keys[10], (W, W), ((R * BLK) ** -0.5 * W ** -0.25), 0.0625),
        "second_lower": normal_values(keys[11], (W, W), (W ** -0.25), 3.0),
        "second_upper": normal_values(keys[12], (W, W), (W ** -0.25), 3.0),
        "blocks_below": draw_blocks_below(jax.random.fold_in(keys[15], 71), 0),
        "blocks_beside": draw_blocks_beside(jax.random.fold_in(keys[15], 71), 0),
    }


def normalise(panel, inverse):
    return jnp.dot(panel, inverse, preferred_element_type=jnp.float32).astype(jnp.bfloat16)


def normalise_by_rows(panel, inverse):
    return jnp.dot(panel, inverse.T, preferred_element_type=jnp.float32).astype(jnp.bfloat16)


def rows_from(matrix, blocks):
    shaped = matrix.reshape(M // BLK, BLK, matrix.shape[1])
    return jnp.take(shaped, blocks, axis=0).reshape(R * BLK, matrix.shape[1])


def columns_of(matrix, blocks):
    shaped = matrix.reshape(matrix.shape[0], M // BLK, BLK)
    return jnp.take(shaped, blocks, axis=1).reshape(matrix.shape[0], R * BLK)


def reference(ancestor, panel_below, panel_beside, inverse_lower, inverse_upper, list_below, list_beside, second_below, second_beside, linked_below, linked_beside, second_lower, second_upper, blocks_below, blocks_beside):
    unit_below = normalise(panel_below, inverse_lower)
    unit_beside = normalise_by_rows(panel_beside, inverse_upper)
    new_lower = (-jnp.dot(columns_of(ancestor, list_below), unit_below, preferred_element_type=jnp.float32)).astype(jnp.bfloat16)
    new_upper = (-jnp.dot(rows_from(ancestor, list_beside).T, unit_beside, preferred_element_type=jnp.float32)).astype(jnp.bfloat16)
    new_diagonal = (jnp.dot(inverse_upper, inverse_lower, preferred_element_type=jnp.float32)
                    - jnp.dot(unit_beside.T, rows_from(new_lower, list_beside), preferred_element_type=jnp.float32)).astype(jnp.bfloat16)
    below_next = normalise(second_below, second_lower)
    link_below = normalise(linked_below, second_lower)
    beside_next = normalise_by_rows(second_beside, second_upper)
    link_beside = normalise_by_rows(linked_beside, second_upper)
    next_lower = (-(jnp.dot(columns_of(ancestor, blocks_below), below_next, preferred_element_type=jnp.float32)
                    + jnp.dot(new_lower, link_below, preferred_element_type=jnp.float32))).astype(jnp.bfloat16)
    next_link = (-(jnp.dot(rows_from(new_upper, blocks_below).T, below_next, preferred_element_type=jnp.float32)
                   + jnp.dot(new_diagonal, link_below, preferred_element_type=jnp.float32))).astype(jnp.bfloat16)
    next_upper = (-(jnp.dot(rows_from(ancestor, blocks_beside).T, beside_next, preferred_element_type=jnp.float32)
                    + jnp.dot(new_upper, link_beside, preferred_element_type=jnp.float32))).astype(jnp.bfloat16)
    next_diagonal = (jnp.dot(second_upper, second_lower, preferred_element_type=jnp.float32)
                     - jnp.dot(beside_next.T, rows_from(next_lower, blocks_beside), preferred_element_type=jnp.float32)
                     - jnp.dot(link_beside.T, next_link, preferred_element_type=jnp.float32)).astype(jnp.bfloat16)
    return new_lower, new_upper, new_diagonal, next_lower, next_upper, next_link, next_diagonal
```

```python
import functools

import jax
import jax.numpy as jnp
from jax import lax
from jax.experimental import pallas as pl
from jax.experimental.pallas import tpu as pltpu
from jax.sharding import PartitionSpec as P

BLK = 128
F32 = jnp.float32
BF16 = jnp.bfloat16


def mm(left, right):
    return jnp.dot(left, right, preferred_element_type=F32)


def mm_rows(left, right):
    return lax.dot_general(left, right, (((1,), (1,)), ((), ())), preferred_element_type=F32)


def mm_first(left, right):
    return lax.dot_general(left, right, (((0,), (0,)), ((), ())), preferred_element_type=F32)


def largest_tile(size, limit):
    tile = min(limit, size)
    while size % tile:
        tile -= BLK
    return tile


def gather_pair(first, second, product):
    cols = lax.axis_size("cols")
    if cols == 2:
        at_first = lax.axis_index("cols") == 0
        mine = product(
            jnp.where(at_first, first[0], second[0]), jnp.where(at_first, first[1], second[1])
        ).astype(BF16)
        return lax.all_gather(mine, ("cols", "rows"), axis=0, tiled=True)
    return jnp.concatenate(
        [
            lax.all_gather(product(*each).astype(BF16), "rows", axis=0, tiled=True)
            for each in (first, second)
        ]
    )


def place_body(pos1, in1, pos2, in2, u1_ref, u2_ref, link_ref, out_ref):
    at = pl.program_id(0)
    width = u1_ref.shape[1]
    keep1 = in1[at].astype(F32)
    keep2 = in2[at].astype(F32)
    u1 = u1_ref[...]
    linked = mm(u1, link_ref[...])
    out_ref[:width, :] = (-u1.astype(F32) * keep1).T.astype(BF16)
    out_ref[width:, :] = (linked * keep1 - u2_ref[...].astype(F32) * keep2).T.astype(BF16)


def blocks_in_tile(blocks, first_block, block_count):
    ids = first_block + jnp.arange(block_count, dtype=jnp.int32)
    matches = ids[:, None] == blocks[None, :]
    places = jnp.sum(
        jnp.where(matches, jnp.arange(blocks.shape[0], dtype=jnp.int32)[None, :], 0), axis=1
    )
    return places.astype(jnp.int32), jnp.any(matches, axis=1).astype(jnp.int32)


def rows_onto(panel, blocks, first_row, row_count):
    global_rows = first_row + jnp.arange(row_count, dtype=jnp.int32)
    matches = (global_rows // BLK)[:, None] == blocks[None, :]
    places = jnp.sum(
        jnp.where(matches, jnp.arange(blocks.shape[0], dtype=jnp.int32)[None, :], 0), axis=1
    )
    picked = jnp.take(panel, places * BLK + global_rows % BLK, axis=0)
    return jnp.where(jnp.any(matches, axis=1)[:, None], picked, jnp.zeros_like(picked))


def place_panels(both, link, list1, list2, first_row, row_count):
    width = both.shape[1]
    listed = list1.shape[0]
    if row_count % BLK:
        u1 = rows_onto(both[: listed * BLK], list1, first_row, row_count)
        u2 = rows_onto(both[listed * BLK :], list2, first_row, row_count)
        joined = jnp.concatenate([-u1.astype(F32), mm(u1, link) - u2.astype(F32)], axis=1)
        return joined.T.astype(BF16)
    first_block = first_row // BLK
    block_count = row_count // BLK
    pos1, in1 = blocks_in_tile(list1, first_block, block_count)
    pos2, in2 = blocks_in_tile(list2, first_block, block_count)
    return pl.pallas_call(
        place_body,
        out_shape=jax.ShapeDtypeStruct((2 * width, block_count * BLK), BF16),
        grid_spec=pltpu.PrefetchScalarGridSpec(
            num_scalar_prefetch=4,
            grid=(block_count,),
            in_specs=[
                pl.BlockSpec((BLK, width), lambda b, p1, i1, p2, i2: (p1[b], 0)),
                pl.BlockSpec((BLK, width), lambda b, p1, i1, p2, i2: (listed + p2[b], 0)),
                pl.BlockSpec((width, width), lambda b, p1, i1, p2, i2: (0, 0)),
            ],
            out_specs=pl.BlockSpec((2 * width, BLK), lambda b, p1, i1, p2, i2: (0, b)),
        ),
        compiler_params=pltpu.CompilerParams(vmem_limit_bytes=24 * 2**20),
        cost_estimate=pl.CostEstimate(
            flops=2 * block_count * BLK * width * width,
            bytes_accessed=8 * block_count * BLK * width,
            transcendentals=0,
        ),
        name="place_panels",
    )(pos1, in1, pos2, in2, both, both, link)


def lower_body(listed, loc1, in1, loc2, in2, part, *refs):
    tiles1, tiles2 = refs[:listed], refs[listed : 2 * listed]
    l1_ref, v1_ref, l2_ref, out_ref = refs[2 * listed :]
    half = l1_ref.shape[1]
    picked1 = jnp.concatenate(
        [tiles1[k][...] * in1[k].astype(F32).astype(BF16) for k in range(listed)], axis=1
    )
    picked2 = jnp.concatenate(
        [tiles2[k][...] * in2[k].astype(F32).astype(BF16) for k in range(listed)], axis=1
    )
    out_ref[:, :half] = (-mm(picked1, l1_ref[...])).astype(BF16)
    out_ref[:, half:] = (mm(picked1, v1_ref[...]) - mm(picked2, l2_ref[...])).astype(BF16)


def lower_partial(ancestor, both, linked, list1, list2, first_block, part, parts):
    rows, columns = ancestor.shape
    width = both.shape[1]
    half = width // parts
    listed = list1.shape[0]
    depth = listed * BLK
    block_count = columns // BLK
    tile = largest_tile(rows, 512)

    def local(blocks):
        at = blocks - first_block
        inside = jnp.logical_and(at >= 0, at < block_count)
        return jnp.clip(at, 0, block_count - 1), inside.astype(jnp.int32)

    loc1, in1 = local(list1)
    loc2, in2 = local(list2)
    specs = [
        pl.BlockSpec((tile, BLK), functools.partial(lambda k, i, l1, i1, l2, i2, p: (i, l1[k]), k))
        for k in range(listed)
    ] + [
        pl.BlockSpec((tile, BLK), functools.partial(lambda k, i, l1, i1, l2, i2, p: (i, l2[k]), k))
        for k in range(listed)
    ]
    specs += [
        pl.BlockSpec((depth, half), lambda i, l1, i1, l2, i2, p: (0, p[0])),
        pl.BlockSpec((depth, half), lambda i, l1, i1, l2, i2, p: (0, p[0])),
        pl.BlockSpec((depth, half), lambda i, l1, i1, l2, i2, p: (1, p[0])),
    ]
    return pl.pallas_call(
        functools.partial(lower_body, listed),
        out_shape=jax.ShapeDtypeStruct((rows, 2 * half), BF16),
        grid_spec=pltpu.PrefetchScalarGridSpec(
            num_scalar_prefetch=5,
            grid=(rows // tile,),
            in_specs=specs,
            out_specs=pl.BlockSpec((tile, 2 * half), lambda i, l1, i1, l2, i2, p: (i, 0)),
        ),
        compiler_params=pltpu.CompilerParams(vmem_limit_bytes=40 * 2**20),
        cost_estimate=pl.CostEstimate(
            flops=6 * rows * depth * half,
            bytes_accessed=4 * rows * depth + 6 * depth * half,
            transcendentals=0,
        ),
        name="lower_partial",
    )(
        loc1, in1, loc2, in2, jnp.reshape(part, (1,)).astype(jnp.int32),
        *([ancestor] * (2 * listed)), both, linked, both,
    )


def strip_body(strip, w_ref, a_ref, *refs):
    total = mm(w_ref[...], a_ref[...])
    for ref in refs[:-1]:
        total = total + ref[...].astype(F32)
    refs[-1][...] = total.astype(BF16)


def strip_product(ancestor, placed, strip, strips, *added):
    rows, columns = ancestor.shape
    strip_width = columns // strips
    height = placed.shape[0]
    if strip_width % BLK:
        total = mm(
            placed, lax.dynamic_slice_in_dim(ancestor, strip * strip_width, strip_width, 1)
        )
        for each in added:
            total = total + each.astype(F32)
        return total.astype(BF16)
    tile = largest_tile(strip_width, 256)
    per = strip_width // tile
    return pl.pallas_call(
        strip_body,
        out_shape=jax.ShapeDtypeStruct((height, strip_width), BF16),
        grid_spec=pltpu.PrefetchScalarGridSpec(
            num_scalar_prefetch=1,
            grid=(per,),
            in_specs=[
                pl.BlockSpec((height, rows), lambda j, s: (0, 0)),
                pl.BlockSpec((rows, tile), lambda j, s: (0, s[0] * per + j)),
            ]
            + [pl.BlockSpec((height, tile), lambda j, s: (0, j))] * len(added),
            out_specs=pl.BlockSpec((height, tile), lambda j, s: (0, j)),
        ),
        compiler_params=pltpu.CompilerParams(vmem_limit_bytes=40 * 2**20),
        cost_estimate=pl.CostEstimate(
            flops=2 * height * rows * strip_width,
            bytes_accessed=2 * (rows * strip_width + height * rows)
            + 2 * (1 + len(added)) * height * strip_width,
            transcendentals=0,
        ),
        name="strip_product",
    )(jnp.reshape(strip, (1,)).astype(jnp.int32), placed, ancestor, *added)


def add_pair(left, right):
    return (left.astype(F32) + right.astype(F32)).astype(BF16)


def upper_sums(ancestor, placed):
    strips = lax.axis_size("rows")
    row_at = lax.axis_index("rows")
    inner = 4 if strips % 4 == 0 else 1
    if inner == 1:
        whole = strip_product(ancestor, placed, 0, 1)
        return lax.psum_scatter(whole.astype(F32), "rows", scatter_dimension=1, tiled=True)
    depth = strips // inner
    core, side, level = row_at % 2, (row_at // 2) % 2, row_at // 4
    to_core = [(i, i ^ 1) for i in range(strips)]
    to_side = [(i, i ^ 2) for i in range(strips)]
    order = [sorted(range(depth), key=lambda d: (-abs(d - z), d)) for z in range(depth)]
    place = [[order[z].index(d) for d in range(depth)] for z in range(depth)]
    order_table = jnp.array(order, jnp.int32)

    def strip_of(target, x, c):
        return (target * 2 + x) * 2 + c

    layer = []
    for turn in range(depth):
        target = order_table[level, turn]
        far = strip_product(ancestor, placed, strip_of(target, 1 - side, 1 - core), strips)
        far = lax.ppermute(far, "rows", to_core)
        near = strip_product(ancestor, placed, strip_of(target, side, 1 - core), strips)
        near = lax.ppermute(near, "rows", to_core)
        far = strip_product(ancestor, placed, strip_of(target, 1 - side, core), strips, far)
        far = lax.ppermute(far, "rows", to_side)
        layer.append(
            strip_product(ancestor, placed, strip_of(target, side, core), strips, near, far)
        )

    def own_part(step, way):
        gap = depth - 1 - step
        chosen = None
        for z in range(depth):
            target = z + way * gap
            if 0 <= target < depth:
                value = layer[place[z][target]]
                chosen = value if chosen is None else jnp.where(level == z, value, chosen)
        return chosen

    arrived = {1: None, -1: None}
    for step in range(depth - 1):
        gap = depth - 1 - step
        for way in (1, -1):
            senders = [z for z in range(depth) if 0 <= z + way * gap < depth]
            pairs = [
                (z * inner + i, (z + way) * inner + i) for z in senders for i in range(inner)
            ]
            value = own_part(step, way)
            if arrived[way] is not None:
                value = add_pair(value, arrived[way])
            arrived[way] = lax.ppermute(value, "rows", pairs)
    total = layer[-1].astype(F32)
    for way in (1, -1):
        if arrived[way] is not None:
            total = total + arrived[way].astype(F32)
    return total


def body(
    ancestor,
    panel_below,
    panel_beside,
    inverse_lower,
    inverse_upper,
    list_below,
    list_beside,
    second_below,
    second_beside,
    linked_below,
    linked_beside,
    second_lower,
    second_upper,
    blocks_below,
    blocks_beside,
):
    row_at = lax.axis_index("rows")
    col_at = lax.axis_index("cols")
    cols = lax.axis_size("cols")
    tile_rows, tile_cols = ancestor.shape
    width = inverse_lower.shape[0]
    half = width // cols

    beside = gather_pair((panel_beside, inverse_upper), (second_beside, second_upper), mm_rows)
    below = gather_pair((panel_below, inverse_lower), (second_below, second_lower), mm)
    link_below = mm(linked_below, second_lower).astype(BF16)
    link_beside = mm_rows(linked_beside, second_upper).astype(BF16)

    placed = place_panels(
        beside, link_beside, list_beside, blocks_beside,
        row_at * tile_rows, tile_rows,
    )
    upper = upper_sums(ancestor, placed)
    new_upper = upper[:width].T.astype(BF16)
    next_upper = upper[width:].T.astype(BF16)

    depth = below.shape[0] // 2
    linked = mm(below[:depth], link_below).astype(BF16)
    lower_total = None
    sums_total = None
    for shift in reversed(range(cols)):
        part = (col_at + shift) % cols
        piece = lower_partial(
            ancestor, below, linked, list_below, blocks_below,
            col_at * (tile_cols // BLK), part, cols,
        )
        sums = jnp.concatenate(
            [mm(placed[:width], piece), mm(placed[width:], piece[:, half:])], axis=1
        )
        if shift:
            pairs = [(i, (i + shift) % cols) for i in range(cols)]
            piece = lax.ppermute(piece, "cols", pairs)
            sums = lax.ppermute(sums, "cols", pairs)
        piece = piece.astype(F32)
        lower_total = piece if lower_total is None else lower_total + piece
        sums_total = sums if sums_total is None else sums_total + sums
    new_lower = lower_total[:, :half].astype(BF16)
    next_lower = lower_total[:, half:].astype(BF16)

    sums = lax.psum(sums_total, "rows")

    def own(matrix):
        return lax.dynamic_slice_in_dim(matrix, col_at * half, half, 1)

    base = mm(inverse_upper, inverse_lower).astype(BF16)
    base_link = mm(base, own(link_below))
    new_diagonal = (mm(inverse_upper, own(inverse_lower)) + sums[:, :half]).astype(BF16)
    link_part = (sums[:, half : 2 * half] - base_link).astype(BF16)
    next_link = lax.all_gather(link_part, "cols", axis=1, tiled=True)
    next_diagonal = (
        mm(second_upper, own(second_lower))
        + mm_first(link_beside, base_link.astype(BF16))
        + sums[:, 2 * half :]
    ).astype(BF16)
    return (new_lower, new_upper, new_diagonal, next_lower, next_upper, next_link, next_diagonal)


def solution(mesh):
    return jax.shard_map(
        body,
        mesh=mesh,
        in_specs=(
            P("rows", "cols"),
            P("rows", None),
            P("rows", None),
            P(),
            P(),
            P(),
            P(),
            P("rows", None),
            P("rows", None),
            P(),
            P(),
            P(),
            P(),
            P(),
            P(),
        ),
        out_specs=(
            P("rows", "cols"),
            P(("cols", "rows"), None),
            P(None, "cols"),
            P("rows", "cols"),
            P(("cols", "rows"), None),
            P(),
            P(None, "cols"),
        ),
        check_vma=False,
    )
```

```python
import functools

import jax
import jax.numpy as jnp
from jax import lax
from jax.experimental import pallas as pl
from jax.experimental.pallas import tpu as pltpu
from jax.sharding import PartitionSpec as P

BLK = 128
F32 = jnp.float32
BF16 = jnp.bfloat16


def mm(left, right):
    return jnp.dot(left, right, preferred_element_type=F32)


def mm_rows(left, right):
    return lax.dot_general(left, right, (((1,), (1,)), ((), ())), preferred_element_type=F32)


def mm_first(left, right):
    return lax.dot_general(left, right, (((0,), (0,)), ((), ())), preferred_element_type=F32)


def largest_tile(size, limit):
    tile = min(limit, size)
    while size % tile:
        tile -= BLK
    return tile


def gather_pair(first, second, product):
    cols = lax.axis_size("cols")
    if cols == 2:
        at_first = lax.axis_index("cols") == 0
        mine = product(
            jnp.where(at_first, first[0], second[0]), jnp.where(at_first, first[1], second[1])
        ).astype(BF16)
        return lax.all_gather(mine, ("cols", "rows"), axis=0, tiled=True)
    return jnp.concatenate(
        [
            lax.all_gather(product(*each).astype(BF16), "rows", axis=0, tiled=True)
            for each in (first, second)
        ]
    )


def place_body(pos1, in1, pos2, in2, u1_ref, u2_ref, link_ref, out_ref):
    at = pl.program_id(0)
    width = u1_ref.shape[1]
    keep1 = in1[at].astype(F32)
    keep2 = in2[at].astype(F32)
    u1 = u1_ref[...]
    linked = mm(u1, link_ref[...])
    out_ref[:width, :] = (-u1.astype(F32) * keep1).T.astype(BF16)
    out_ref[width:, :] = (linked * keep1 - u2_ref[...].astype(F32) * keep2).T.astype(BF16)


def blocks_in_tile(blocks, first_block, block_count):
    ids = first_block + jnp.arange(block_count, dtype=jnp.int32)
    matches = ids[:, None] == blocks[None, :]
    places = jnp.sum(
        jnp.where(matches, jnp.arange(blocks.shape[0], dtype=jnp.int32)[None, :], 0), axis=1
    )
    return places.astype(jnp.int32), jnp.any(matches, axis=1).astype(jnp.int32)


def rows_onto(panel, blocks, first_row, row_count):
    global_rows = first_row + jnp.arange(row_count, dtype=jnp.int32)
    matches = (global_rows // BLK)[:, None] == blocks[None, :]
    places = jnp.sum(
        jnp.where(matches, jnp.arange(blocks.shape[0], dtype=jnp.int32)[None, :], 0), axis=1
    )
    picked = jnp.take(panel, places * BLK + global_rows % BLK, axis=0)
    return jnp.where(jnp.any(matches, axis=1)[:, None], picked, jnp.zeros_like(picked))


def place_panels(both, link, list1, list2, first_row, row_count):
    width = both.shape[1]
    listed = list1.shape[0]
    if row_count % BLK:
        u1 = rows_onto(both[: listed * BLK], list1, first_row, row_count)
        u2 = rows_onto(both[listed * BLK :], list2, first_row, row_count)
        joined = jnp.concatenate([-u1.astype(F32), mm(u1, link) - u2.astype(F32)], axis=1)
        return joined.T.astype(BF16)
    first_block = first_row // BLK
    block_count = row_count // BLK
    pos1, in1 = blocks_in_tile(list1, first_block, block_count)
    pos2, in2 = blocks_in_tile(list2, first_block, block_count)
    return pl.pallas_call(
        place_body,
        out_shape=jax.ShapeDtypeStruct((2 * width, block_count * BLK), BF16),
        grid_spec=pltpu.PrefetchScalarGridSpec(
            num_scalar_prefetch=4,
            grid=(block_count,),
            in_specs=[
                pl.BlockSpec((BLK, width), lambda b, p1, i1, p2, i2: (p1[b], 0)),
                pl.BlockSpec((BLK, width), lambda b, p1, i1, p2, i2: (listed + p2[b], 0)),
                pl.BlockSpec((width, width), lambda b, p1, i1, p2, i2: (0, 0)),
            ],
            out_specs=pl.BlockSpec((2 * width, BLK), lambda b, p1, i1, p2, i2: (0, b)),
        ),
        compiler_params=pltpu.CompilerParams(vmem_limit_bytes=24 * 2**20),
        cost_estimate=pl.CostEstimate(
            flops=2 * block_count * BLK * width * width,
            bytes_accessed=8 * block_count * BLK * width,
            transcendentals=0,
        ),
        name="place_panels",
    )(pos1, in1, pos2, in2, both, both, link)


def lower_body(listed, loc1, in1, loc2, in2, part, *refs):
    tiles1, tiles2 = refs[:listed], refs[listed : 2 * listed]
    l1_ref, v1_ref, l2_ref, out_ref = refs[2 * listed :]
    half = l1_ref.shape[1]
    picked1 = jnp.concatenate(
        [tiles1[k][...] * in1[k].astype(F32).astype(BF16) for k in range(listed)], axis=1
    )
    picked2 = jnp.concatenate(
        [tiles2[k][...] * in2[k].astype(F32).astype(BF16) for k in range(listed)], axis=1
    )
    out_ref[:, :half] = (-mm(picked1, l1_ref[...])).astype(BF16)
    out_ref[:, half:] = (mm(picked1, v1_ref[...]) - mm(picked2, l2_ref[...])).astype(BF16)


def lower_partial(ancestor, both, linked, list1, list2, first_block, part, parts):
    rows, columns = ancestor.shape
    width = both.shape[1]
    half = width // parts
    listed = list1.shape[0]
    depth = listed * BLK
    block_count = columns // BLK
    tile = largest_tile(rows, 512)

    def local(blocks):
        at = blocks - first_block
        inside = jnp.logical_and(at >= 0, at < block_count)
        return jnp.clip(at, 0, block_count - 1), inside.astype(jnp.int32)

    loc1, in1 = local(list1)
    loc2, in2 = local(list2)
    specs = [
        pl.BlockSpec((tile, BLK), functools.partial(lambda k, i, l1, i1, l2, i2, p: (i, l1[k]), k))
        for k in range(listed)
    ] + [
        pl.BlockSpec((tile, BLK), functools.partial(lambda k, i, l1, i1, l2, i2, p: (i, l2[k]), k))
        for k in range(listed)
    ]
    specs += [
        pl.BlockSpec((depth, half), lambda i, l1, i1, l2, i2, p: (0, p[0])),
        pl.BlockSpec((depth, half), lambda i, l1, i1, l2, i2, p: (0, p[0])),
        pl.BlockSpec((depth, half), lambda i, l1, i1, l2, i2, p: (1, p[0])),
    ]
    return pl.pallas_call(
        functools.partial(lower_body, listed),
        out_shape=jax.ShapeDtypeStruct((rows, 2 * half), BF16),
        grid_spec=pltpu.PrefetchScalarGridSpec(
            num_scalar_prefetch=5,
            grid=(rows // tile,),
            in_specs=specs,
            out_specs=pl.BlockSpec((tile, 2 * half), lambda i, l1, i1, l2, i2, p: (i, 0)),
        ),
        compiler_params=pltpu.CompilerParams(vmem_limit_bytes=40 * 2**20),
        cost_estimate=pl.CostEstimate(
            flops=6 * rows * depth * half,
            bytes_accessed=4 * rows * depth + 6 * depth * half,
            transcendentals=0,
        ),
        name="lower_partial",
    )(
        loc1, in1, loc2, in2, jnp.reshape(part, (1,)).astype(jnp.int32),
        *([ancestor] * (2 * listed)), both, linked, both,
    )


def strip_body(strip, w_ref, a_ref, *refs):
    total = mm(w_ref[...], a_ref[...])
    for ref in refs[:-1]:
        total = total + ref[...].astype(F32)
    refs[-1][...] = total.astype(BF16)


def strip_product(ancestor, placed, strip, strips, *added):
    rows, columns = ancestor.shape
    strip_width = columns // strips
    height = placed.shape[0]
    if strip_width % BLK:
        total = mm(
            placed, lax.dynamic_slice_in_dim(ancestor, strip * strip_width, strip_width, 1)
        )
        for each in added:
            total = total + each.astype(F32)
        return total.astype(BF16)
    tile = largest_tile(strip_width, 256)
    per = strip_width // tile
    return pl.pallas_call(
        strip_body,
        out_shape=jax.ShapeDtypeStruct((height, strip_width), BF16),
        grid_spec=pltpu.PrefetchScalarGridSpec(
            num_scalar_prefetch=1,
            grid=(per,),
            in_specs=[
                pl.BlockSpec((height, rows), lambda j, s: (0, 0)),
                pl.BlockSpec((rows, tile), lambda j, s: (0, s[0] * per + j)),
            ]
            + [pl.BlockSpec((height, tile), lambda j, s: (0, j))] * len(added),
            out_specs=pl.BlockSpec((height, tile), lambda j, s: (0, j)),
        ),
        compiler_params=pltpu.CompilerParams(vmem_limit_bytes=40 * 2**20),
        cost_estimate=pl.CostEstimate(
            flops=2 * height * rows * strip_width,
            bytes_accessed=2 * (rows * strip_width + height * rows)
            + 2 * (1 + len(added)) * height * strip_width,
            transcendentals=0,
        ),
        name="strip_product",
    )(jnp.reshape(strip, (1,)).astype(jnp.int32), placed, ancestor, *added)


def add_pair(left, right):
    return (left.astype(F32) + right.astype(F32)).astype(BF16)


def upper_sums(ancestor, placed):
    strips = lax.axis_size("rows")
    row_at = lax.axis_index("rows")
    inner = 4 if strips % 4 == 0 else 1
    if inner == 1:
        whole = strip_product(ancestor, placed, 0, 1)
        return lax.psum_scatter(whole.astype(F32), "rows", scatter_dimension=1, tiled=True)
    depth = strips // inner
    core, side, level = row_at % 2, (row_at // 2) % 2, row_at // 4
    to_core = [(i, i ^ 1) for i in range(strips)]
    to_side = [(i, i ^ 2) for i in range(strips)]
    order = [sorted(range(depth), key=lambda d: (-abs(d - z), d)) for z in range(depth)]
    place = [[order[z].index(d) for d in range(depth)] for z in range(depth)]
    order_table = jnp.array(order, jnp.int32)

    def strip_of(target, x, c):
        return (target * 2 + x) * 2 + c

    layer = []
    for turn in range(depth):
        target = order_table[level, turn]
        far = strip_product(ancestor, placed, strip_of(target, 1 - side, 1 - core), strips)
        far = lax.ppermute(far, "rows", to_core)
        near = strip_product(ancestor, placed, strip_of(target, side, 1 - core), strips)
        near = lax.ppermute(near, "rows", to_core)
        far = strip_product(ancestor, placed, strip_of(target, 1 - side, core), strips, far)
        far = lax.ppermute(far, "rows", to_side)
        layer.append(
            strip_product(ancestor, placed, strip_of(target, side, core), strips, near, far)
        )

    def own_part(step, way):
        gap = depth - 1 - step
        chosen = None
        for z in range(depth):
            target = z + way * gap
            if 0 <= target < depth:
                value = layer[place[z][target]]
                chosen = value if chosen is None else jnp.where(level == z, value, chosen)
        return chosen

    arrived = {1: None, -1: None}
    for step in range(depth - 1):
        gap = depth - 1 - step
        for way in (1, -1):
            senders = [z for z in range(depth) if 0 <= z + way * gap < depth]
            pairs = [
                (z * inner + i, (z + way) * inner + i) for z in senders for i in range(inner)
            ]
            value = own_part(step, way)
            if arrived[way] is not None:
                value = add_pair(value, arrived[way])
            arrived[way] = lax.ppermute(value, "rows", pairs)
    total = layer[-1].astype(F32)
    for way in (1, -1):
        if arrived[way] is not None:
            total = total + arrived[way].astype(F32)
    return total


def body_general(
    ancestor,
    panel_below,
    panel_beside,
    inverse_lower,
    inverse_upper,
    list_below,
    list_beside,
    second_below,
    second_beside,
    linked_below,
    linked_beside,
    second_lower,
    second_upper,
    blocks_below,
    blocks_beside,
):
    row_at = lax.axis_index("rows")
    col_at = lax.axis_index("cols")
    cols = lax.axis_size("cols")
    tile_rows, tile_cols = ancestor.shape
    width = inverse_lower.shape[0]
    half = width // cols

    beside = gather_pair((panel_beside, inverse_upper), (second_beside, second_upper), mm_rows)
    below = gather_pair((panel_below, inverse_lower), (second_below, second_lower), mm)
    link_below = mm(linked_below, second_lower).astype(BF16)
    link_beside = mm_rows(linked_beside, second_upper).astype(BF16)

    placed = place_panels(
        beside, link_beside, list_beside, blocks_beside,
        row_at * tile_rows, tile_rows,
    )
    upper = upper_sums(ancestor, placed)
    new_upper = upper[:width].T.astype(BF16)
    next_upper = upper[width:].T.astype(BF16)

    depth = below.shape[0] // 2
    linked = mm(below[:depth], link_below).astype(BF16)
    lower_total = None
    sums_total = None
    for shift in reversed(range(cols)):
        part = (col_at + shift) % cols
        piece = lower_partial(
            ancestor, below, linked, list_below, blocks_below,
            col_at * (tile_cols // BLK), part, cols,
        )
        sums = jnp.concatenate(
            [mm(placed[:width], piece), mm(placed[width:], piece[:, half:])], axis=1
        )
        if shift:
            pairs = [(i, (i + shift) % cols) for i in range(cols)]
            piece = lax.ppermute(piece, "cols", pairs)
            sums = lax.ppermute(sums, "cols", pairs)
        piece = piece.astype(F32)
        lower_total = piece if lower_total is None else lower_total + piece
        sums_total = sums if sums_total is None else sums_total + sums
    new_lower = lower_total[:, :half].astype(BF16)
    next_lower = lower_total[:, half:].astype(BF16)

    sums = lax.psum(sums_total, "rows")

    def own(matrix):
        return lax.dynamic_slice_in_dim(matrix, col_at * half, half, 1)

    base = mm(inverse_upper, inverse_lower).astype(BF16)
    base_link = mm(base, own(link_below))
    new_diagonal = (mm(inverse_upper, own(inverse_lower)) + sums[:, :half]).astype(BF16)
    link_part = (sums[:, half : 2 * half] - base_link).astype(BF16)
    next_link = lax.all_gather(link_part, "cols", axis=1, tiled=True)
    next_diagonal = (
        mm(second_upper, own(second_lower))
        + mm_first(link_beside, base_link.astype(BF16))
        + sums[:, 2 * half :]
    ).astype(BF16)
    return (new_lower, new_upper, new_diagonal, next_lower, next_upper, next_link, next_diagonal)


SLOTS = 4


def swapped(value, axis, bit):
    size = lax.axis_size(axis)
    return lax.ppermute(value, axis, [(i, i ^ bit) for i in range(size)])


def from_levels(value, shift):
    size = lax.axis_size("rows")
    return lax.ppermute(value, "rows", [(i, (i + 4 * shift) % size) for i in range(size)])


class Seat:
    def __init__(self):
        row_at = lax.axis_index("rows")
        self.row = row_at
        self.core, self.side, self.level = row_at % 2, (row_at // 2) % 2, row_at // 4
        self.depth = lax.axis_size("rows") // 4
        self.col = lax.axis_index("cols")


def spread(item, depth):
    pair = jnp.concatenate([item, swapped(item, "rows", 2)])
    near = [pair] + [from_levels(pair, shift) for shift in range(1, depth)]
    beyond = [swapped(each, "cols", 1) for each in near]
    both = [swapped(jnp.stack(each), "rows", 1) for each in zip(near, beyond)]
    return jnp.concatenate(
        near + [each[0] for each in both] + beyond + [each[1] for each in both]
    )


def spread_order(seat):
    at = jnp.arange(4 * seat.depth, dtype=jnp.int32)
    apart_core, rest = at // (2 * seat.depth), at % (2 * seat.depth)
    level = (seat.level - rest // 2) % seat.depth
    side = seat.side ^ (rest % 2)
    core = seat.core ^ apart_core
    return (level * 2 + side) * 2 + core


def spread_place(seat, listed, which):
    at = jnp.arange(listed, dtype=jnp.int32)
    core, side, level = at % 2, (at // 2) % 2, at // 4
    apart = (seat.col ^ which) * 2 + (seat.core ^ core)
    return (apart * seat.depth + (seat.level - level) % seat.depth) * 2 + (seat.side ^ side)


def tile_slots(tile, block_count, marked):
    flags = lax.dynamic_slice_in_dim(marked, tile * block_count, block_count, 0)
    at = jnp.arange(block_count, dtype=jnp.int32)
    rank = jnp.sum(jnp.where(at[None, :] < at[:, None], flags[None, :], 0), axis=1)
    hit = jnp.logical_and(rank[None, :] == at[:, None], flags[None, :] > 0)
    ids = jnp.sum(jnp.where(hit, at[None, :], 0), axis=1)
    return ids.astype(jnp.int32), jnp.sum(flags).astype(jnp.int32)


def sent_slots(own, own_count, other, other_count, own_tile, other_tile, block_count):
    at = jnp.arange(SLOTS, dtype=jnp.int32)
    behind = jnp.clip(SLOTS + at - own_count, 0, block_count - 1)
    mine = at < own_count
    ids = jnp.where(
        mine, own_tile * block_count + own[:SLOTS], other_tile * block_count + other[behind]
    )
    return ids, jnp.logical_or(mine, SLOTS + at - own_count < other_count)


def place_slots_body(b1, m1, b2, m2, u1_ref, u2_ref, link_ref, out_ref):
    at = pl.program_id(0)
    width = u1_ref.shape[1]
    used = m1[at] + m2[at] > 0

    @pl.when(used)
    def _():
        keep1 = m1[at].astype(F32)
        keep2 = m2[at].astype(F32)
        u1 = u1_ref[...]
        linked = mm(u1, link_ref[...])
        out_ref[:width, :] = (-u1.astype(F32) * keep1).T.astype(BF16)
        out_ref[width:, :] = (linked * keep1 - u2_ref[...].astype(F32) * keep2).T.astype(BF16)

    @pl.when(jnp.logical_not(used))
    def _():
        out_ref[...] = jnp.zeros_like(out_ref)


def place_slots(gathered, link, list1, list2, place1, place2, ids, valid):
    width = gathered.shape[1]
    count = ids.shape[0]

    def find(blocks, places):
        matches = jnp.logical_and(ids[:, None] == blocks[None, :], valid[:, None])
        return (
            jnp.sum(jnp.where(matches, places[None, :], 0), axis=1).astype(jnp.int32),
            jnp.any(matches, axis=1).astype(jnp.int32),
        )

    b1, m1 = find(list1, place1)
    b2, m2 = find(list2, place2)
    return pl.pallas_call(
        place_slots_body,
        out_shape=jax.ShapeDtypeStruct((2 * width, count * BLK), BF16),
        grid_spec=pltpu.PrefetchScalarGridSpec(
            num_scalar_prefetch=4,
            grid=(count,),
            in_specs=[
                pl.BlockSpec((BLK, width), lambda s, p1, i1, p2, i2: (p1[s], 0)),
                pl.BlockSpec((BLK, width), lambda s, p1, i1, p2, i2: (p2[s], 0)),
                pl.BlockSpec((width, width), lambda s, p1, i1, p2, i2: (0, 0)),
            ],
            out_specs=pl.BlockSpec((2 * width, BLK), lambda s, p1, i1, p2, i2: (0, s)),
        ),
        compiler_params=pltpu.CompilerParams(vmem_limit_bytes=24 * 2**20),
        cost_estimate=pl.CostEstimate(
            flops=2 * count * BLK * width * width // 4,
            bytes_accessed=4 * count * BLK * width,
            transcendentals=0,
        ),
        name="place_slots",
    )(b1, m1, b2, m2, gathered, gathered, link)


def pack_body(local, strip, a_ref, out_ref):
    out_ref[...] = a_ref[...]


def pack(ancestor, local, pair, pairs):
    wide = ancestor.shape[1] // pairs
    count = local.shape[0]
    return pl.pallas_call(
        pack_body,
        out_shape=jax.ShapeDtypeStruct((count * BLK, wide), BF16),
        grid_spec=pltpu.PrefetchScalarGridSpec(
            num_scalar_prefetch=2,
            grid=(count,),
            in_specs=[pl.BlockSpec((BLK, wide), lambda s, l, p: (l[s], p[0]))],
            out_specs=pl.BlockSpec((BLK, wide), lambda s, l, p: (s, 0)),
        ),
        cost_estimate=pl.CostEstimate(
            flops=0, bytes_accessed=4 * count * BLK * wide, transcendentals=0
        ),
        name="pack_slots",
    )(local, jnp.reshape(pair, (1,)).astype(jnp.int32), ancestor)


def merge_body(local, behind, own_count, strip, a_ref, got_ref, out_ref):
    mine = pl.program_id(0) < own_count[0]

    @pl.when(mine)
    def _():
        out_ref[...] = a_ref[...]

    @pl.when(jnp.logical_not(mine))
    def _():
        out_ref[...] = got_ref[...]


def merge(ancestor, got, local, own_count, pair, pairs):
    wide = ancestor.shape[1] // pairs
    at = jnp.arange(SLOTS, dtype=jnp.int32)
    behind = jnp.clip(at - own_count, 0, SLOTS - 1)
    return pl.pallas_call(
        merge_body,
        out_shape=jax.ShapeDtypeStruct((SLOTS * BLK, wide), BF16),
        grid_spec=pltpu.PrefetchScalarGridSpec(
            num_scalar_prefetch=4,
            grid=(SLOTS,),
            in_specs=[
                pl.BlockSpec((BLK, wide), lambda s, l, b, n, p: (l[s], p[0])),
                pl.BlockSpec((BLK, wide), lambda s, l, b, n, p: (b[s], 0)),
            ],
            out_specs=pl.BlockSpec((BLK, wide), lambda s, l, b, n, p: (s, 0)),
        ),
        cost_estimate=pl.CostEstimate(
            flops=0, bytes_accessed=6 * SLOTS * BLK * wide, transcendentals=0
        ),
        name="merge_slots",
    )(
        local[:SLOTS], behind, jnp.reshape(own_count, (1,)),
        jnp.reshape(pair, (1,)).astype(jnp.int32), ancestor, got,
    )


def slots_body(units, local, count, at, *refs):
    w_refs, arrived_ref = refs[:units], refs[units]
    tiles = refs[units + 1 : units + 1 + (units - 1) * SLOTS]
    added = refs[units + 1 + (units - 1) * SLOTS : -1]
    out_ref = refs[-1]

    def own(unit):
        group = tiles[(unit - 1) * SLOTS : unit * SLOTS]
        return mm(w_refs[unit][...], jnp.concatenate([ref[...] for ref in group], axis=0))

    def store(more):
        total = mm(w_refs[0][...], arrived_ref[...]) + own(1)
        for unit in more:
            total = total + own(unit)
        for ref in added:
            total = total + ref[...].astype(F32)
        out_ref[...] = total.astype(BF16)

    @pl.when(count[0] <= SLOTS)
    def _():
        store(())

    @pl.when(count[0] > SLOTS)
    def _():
        store(range(2, units))


def slots_product(ancestor, placed, arrived, local, count, strip, within, strips, *added):
    columns = ancestor.shape[1]
    strip_width = columns // strips
    height = placed.shape[0]
    tile = largest_tile(strip_width, 256)
    per = strip_width // tile
    unit_width = SLOTS * BLK
    units = placed.shape[1] // unit_width
    where_at = jnp.stack([strip * per, within * per]).astype(jnp.int32)

    def own_block(slot):
        if slot < SLOTS:
            return lambda j, l, n, p: (l[slot], p[0] + j)
        return lambda j, l, n, p: (l[slot], jnp.where(n[0] > SLOTS, p[0] + j, 0))

    def unit_block(unit):
        if unit < 2:
            return lambda j, l, n, p: (0, unit)
        return lambda j, l, n, p: (0, jnp.where(n[0] > SLOTS, unit, 0))

    own_slots = (units - 1) * SLOTS
    return pl.pallas_call(
        functools.partial(slots_body, units),
        out_shape=jax.ShapeDtypeStruct((height, strip_width), BF16),
        grid_spec=pltpu.PrefetchScalarGridSpec(
            num_scalar_prefetch=3,
            grid=(per,),
            in_specs=[pl.BlockSpec((height, unit_width), unit_block(u)) for u in range(units)]
            + [pl.BlockSpec((unit_width, tile), lambda j, l, n, p: (0, p[1] + j))]
            + [pl.BlockSpec((BLK, tile), own_block(slot)) for slot in range(own_slots)]
            + [pl.BlockSpec((height, tile), lambda j, l, n, p: (0, j))] * len(added),
            out_specs=pl.BlockSpec((height, tile), lambda j, l, n, p: (0, j)),
        ),
        compiler_params=pltpu.CompilerParams(vmem_limit_bytes=40 * 2**20),
        cost_estimate=pl.CostEstimate(
            flops=4 * height * unit_width * strip_width,
            bytes_accessed=4 * unit_width * (height + strip_width)
            + 2 * (1 + len(added)) * height * strip_width,
            transcendentals=0,
        ),
        name="slots_product",
    )(
        local, jnp.reshape(count, (1,)), where_at,
        *([placed] * units), arrived, *([ancestor] * own_slots), *added,
    )


def small_sums_body(local, count, w_ref, x_ref, out_ref, total_ref):
    at = pl.program_id(0)
    width = w_ref.shape[0] // 2
    half = x_ref.shape[1] // 2

    @pl.when(at == 0)
    def _():
        total_ref[...] = jnp.zeros_like(total_ref)

    @pl.when(at < count[0])
    def _():
        total_ref[:, : 2 * half] += mm(w_ref[:width, :], x_ref[...])
        total_ref[:, 2 * half :] += mm(w_ref[width:, :], x_ref[:, half:])

    @pl.when(at == pl.num_programs(0) - 1)
    def _():
        out_ref[...] = total_ref[...].astype(BF16)


def small_sums(placed, piece, local, count):
    width = placed.shape[0] // 2
    half = piece.shape[1] // 2
    slots = local.shape[0]
    return pl.pallas_call(
        small_sums_body,
        out_shape=jax.ShapeDtypeStruct((width, 3 * half), BF16),
        grid_spec=pltpu.PrefetchScalarGridSpec(
            num_scalar_prefetch=2,
            grid=(slots,),
            in_specs=[
                pl.BlockSpec((2 * width, BLK), lambda s, l, n: (0, SLOTS + s)),
                pl.BlockSpec((BLK, 2 * half), lambda s, l, n: (l[s], 0)),
            ],
            out_specs=pl.BlockSpec((width, 3 * half), lambda s, l, n: (0, 0)),
            scratch_shapes=[pltpu.VMEM((width, 3 * half), F32)],
        ),
        compiler_params=pltpu.CompilerParams(vmem_limit_bytes=24 * 2**20),
        cost_estimate=pl.CostEstimate(
            flops=2 * SLOTS * BLK * width * 3 * half,
            bytes_accessed=4 * slots * BLK * width,
            transcendentals=0,
        ),
        name="small_sums",
    )(local, jnp.reshape(count, (1,)), placed, piece)


def level_chain(seat, layer, place):
    depth = seat.depth
    arrived = {1: None, -1: None}
    for step in range(depth - 1):
        gap = depth - 1 - step
        for way in (1, -1):
            senders = [z for z in range(depth) if 0 <= z + way * gap < depth]
            pairs = [(z * 4 + i, (z + way) * 4 + i) for z in senders for i in range(4)]
            value = None
            for z in senders:
                each = layer[place[z][z + way * gap]]
                value = each if value is None else jnp.where(seat.level == z, each, value)
            if arrived[way] is not None:
                value = add_pair(value, arrived[way])
            arrived[way] = lax.ppermute(value, "rows", pairs)
    total = layer[-1].astype(F32)
    for way in (1, -1):
        total = total + arrived[way].astype(F32)
    return total


def upper_by_slots(seat, ancestor, placed, local, count):
    depth = seat.depth
    strips = 4 * depth
    order = [sorted(range(depth), key=lambda d: (-abs(d - z), d)) for z in range(depth)]
    place = [[order[z].index(d) for d in range(depth)] for z in range(depth)]
    order_table = jnp.array(order, jnp.int32)
    arrived = []
    for turn in range(depth):
        pair = order_table[seat.level, turn] * 2 + (1 - seat.side)
        passed = swapped(pack(ancestor, local[SLOTS : 2 * SLOTS], pair, strips // 2), "rows", 1)
        leaving = merge(ancestor, passed, local, count, pair, strips // 2)
        arrived.append(swapped(leaving, "rows", 2))
    layer = []
    for turn in range(depth):
        pair = order_table[seat.level, turn] * 2 + seat.side
        parts = (ancestor, placed, arrived[turn], local, count)
        far = slots_product(*parts, pair * 2 + 1 - seat.core, 1 - seat.core, strips)
        far = swapped(far, "rows", 1)
        layer.append(slots_product(*parts, pair * 2 + seat.core, seat.core, strips, far))
    return level_chain(seat, layer, place)


def left_over(seat, ancestor, gathered, link, lists, places, dropped):
    block_rows, columns = ancestor.shape
    first_row = seat.row * block_rows
    shaped = gathered.reshape(-1, BLK, gathered.shape[1])
    u1, u2 = (
        rows_onto(
            jnp.take(shaped, place, axis=0).reshape(-1, gathered.shape[1]),
            blocks, first_row, block_rows,
        )
        for blocks, place in zip(lists, places)
    )
    joined = jnp.concatenate([-u1.astype(F32), mm(u1, link) - u2.astype(F32)], axis=1)
    joined = jnp.where(jnp.repeat(dropped, BLK)[:, None], joined, 0.0).astype(BF16)
    strip_width = columns // (4 * seat.depth)
    side = (jnp.arange(columns, dtype=jnp.int32) // strip_width // 2) % 2
    partial = jnp.where((side != seat.side)[None, :], mm_first(joined, ancestor), 0.0)
    return lax.psum_scatter(partial, "rows", scatter_dimension=1, tiled=True)


def sum_small(seat, sums):
    rows = sums.shape[0]

    def halves(value, bit):
        size = value.shape[0] // 2
        kept = lax.dynamic_slice_in_dim(value, bit * size, size, 0)
        given = lax.dynamic_slice_in_dim(value, (1 - bit) * size, size, 0)
        return kept, given

    kept, given = halves(sums, seat.core)
    sums = add_pair(kept, swapped(given, "rows", 1))
    kept, given = halves(sums, seat.side)
    sums = add_pair(kept, swapped(given, "rows", 2))
    size = rows // (4 * seat.depth)

    def level_rows(level):
        return lax.dynamic_slice_in_dim(sums, level * size, size, 0)

    total = level_rows(seat.level).astype(F32)
    for shift in range(1, seat.depth):
        given = level_rows((seat.level + shift) % seat.depth)
        total = total + from_levels(given, shift).astype(F32)
    return total


def gather_small(seat, mine):
    levels = [mine] + [from_levels(mine, shift) for shift in range(1, seat.depth)]
    value = jnp.concatenate(
        [
            lax.select_n((seat.level - z) % seat.depth, *levels)
            if seat.depth > 2
            else jnp.where(seat.level == z, levels[0], levels[-1])
            for z in range(seat.depth)
        ]
    )
    for bit, at in ((2, seat.side), (1, seat.core)):
        other = swapped(value, "rows", bit)
        value = jnp.concatenate(
            [jnp.where(at == 0, value, other), jnp.where(at == 0, other, value)]
        )
    return value


def body_by_slots(
    ancestor,
    panel_below,
    panel_beside,
    inverse_lower,
    inverse_upper,
    list_below,
    list_beside,
    second_below,
    second_beside,
    linked_below,
    linked_beside,
    second_lower,
    second_upper,
    blocks_below,
    blocks_beside,
):
    seat = Seat()
    tile_rows, tile_cols = ancestor.shape
    block_count = tile_rows // BLK
    width = inverse_lower.shape[0]
    half = width // 2
    listed = list_below.shape[0]
    rows = 4 * seat.depth
    at_first = seat.col == 0

    def either(first, second):
        return jnp.where(at_first, first, second)

    beside = mm_rows(either(panel_beside, second_beside), either(inverse_upper, second_upper))
    below = mm(either(panel_below, second_below), either(inverse_lower, second_lower))
    beside = spread(beside.astype(BF16), seat.depth)
    below = spread(below.astype(BF16), seat.depth)
    link_below = mm(linked_below, second_lower).astype(BF16)
    link_beside = mm_rows(linked_beside, second_upper).astype(BF16)

    all_blocks = jnp.arange(rows * block_count, dtype=jnp.int32)[:, None]
    marked = jnp.logical_or(
        jnp.any(all_blocks == list_beside[None, :], axis=1),
        jnp.any(all_blocks == blocks_beside[None, :], axis=1),
    ).astype(jnp.int32)
    full = jnp.max(jnp.sum(marked.reshape(rows // 2, 2 * block_count), axis=1)) > 2 * SLOTS

    def slots_of(tile):
        return tile_slots(tile, block_count, marked)

    local, count = slots_of(seat.row)
    _, other_count = slots_of(seat.row ^ 1)
    facing, beyond = seat.row ^ 2, seat.row ^ 3
    ids, valid = sent_slots(*slots_of(facing), *slots_of(beyond), facing, beyond, block_count)
    own_at = jnp.arange(block_count, dtype=jnp.int32)
    ids = jnp.concatenate([ids, seat.row * block_count + local])
    valid = jnp.concatenate([valid, own_at < count])
    lists = (list_beside, blocks_beside)
    places = (spread_place(seat, listed, 0), spread_place(seat, listed, 1))
    placed = place_slots(beside, link_beside, *lists, *places, ids, valid)
    upper = upper_by_slots(seat, ancestor, placed, local, count)

    slot_dropped = jnp.logical_and(
        own_at < count, own_at >= 2 * SLOTS - jnp.minimum(other_count, SLOTS)
    )
    dropped = jnp.any(
        jnp.logical_and(slot_dropped[:, None], local[:, None] == own_at[None, :]), axis=0
    )

    def with_rest(total):
        return total + left_over(seat, ancestor, beside, link_beside, lists, places, dropped)

    upper = lax.cond(full, with_rest, lambda total: total, upper)
    new_upper = upper[:width].T.astype(BF16)
    next_upper = upper[width:].T.astype(BF16)

    order = spread_order(seat)
    below = jnp.concatenate(
        [
            lax.dynamic_slice_in_dim(below, (seat.col ^ which) * listed * BLK, listed * BLK, 0)
            for which in (0, 1)
        ]
    )
    linked = mm(below[: listed * BLK], link_below).astype(BF16)
    pieces, sums = [], []
    for shift in (1, 0):
        piece = lower_partial(
            ancestor, below, linked, list_below[order], blocks_below[order],
            seat.col * (tile_cols // BLK), seat.col ^ shift, 2,
        )
        pieces.append(piece)
        sums.append(small_sums(placed, piece, local, count))
    piece = pieces[1].astype(F32) + swapped(pieces[0], "cols", 1).astype(F32)
    new_lower = piece[:, :half].astype(BF16)
    next_lower = piece[:, half:].astype(BF16)
    mine = sum_small(seat, add_pair(sums[1], swapped(sums[0], "cols", 1)))

    def own(matrix):
        return lax.dynamic_slice_in_dim(matrix, seat.col * half, half, 1)

    base = mm(inverse_upper, inverse_lower).astype(BF16)
    base_link = mm(base, own(link_below))
    added = jnp.concatenate(
        [
            mm(inverse_upper, own(inverse_lower)),
            -base_link,
            mm(second_upper, own(second_lower)) + mm_first(link_beside, base_link.astype(BF16)),
        ],
        axis=1,
    )
    size = width // rows
    first = (seat.core * 2 + seat.side) * (width // 4) + seat.level * size
    mine = mine + lax.dynamic_slice_in_dim(added, first, size, 0)
    whole = gather_small(seat, mine.astype(BF16))
    link_part = whole[:, half : 2 * half]
    link_other = swapped(link_part, "cols", 1)
    next_link = jnp.concatenate(
        [either(link_part, link_other), either(link_other, link_part)], axis=1
    )
    return (
        new_lower, new_upper, whole[:, :half], next_lower, next_upper, next_link,
        whole[:, 2 * half :],
    )


def body(*arrays):
    ancestor, panel = arrays[0], arrays[1]
    rows, cols = lax.axis_size("rows"), lax.axis_size("cols")
    by_slots = (
        cols == 2
        and rows % 4 == 0
        and rows > 4
        and panel.shape[0] == BLK
        and ancestor.shape[0] % BLK == 0
        and ancestor.shape[0] // BLK >= 2 * SLOTS
        and ancestor.shape[0] // BLK % SLOTS == 0
        and ancestor.shape[1] % (rows * BLK) == 0
        and panel.shape[1] % (2 * rows) == 0
    )
    return (body_by_slots if by_slots else body_general)(*arrays)


def solution(mesh):
    return jax.shard_map(
        body,
        mesh=mesh,
        in_specs=(
            P("rows", "cols"),
            P("rows", None),
            P("rows", None),
            P(),
            P(),
            P(),
            P(),
            P("rows", None),
            P("rows", None),
            P(),
            P(),
            P(),
            P(),
            P(),
            P(),
        ),
        out_specs=(
            P("rows", "cols"),
            P(("cols", "rows"), None),
            P(None, "cols"),
            P("rows", "cols"),
            P(("cols", "rows"), None),
            P(),
            P(None, "cols"),
        ),
        check_vma=False,
    )
```

```python
import functools

import jax
import jax.numpy as jnp
from jax import lax
from jax.experimental import pallas as pl
from jax.experimental.pallas import tpu as pltpu
from jax.sharding import PartitionSpec as P

BLK = 128
F32 = jnp.float32
BF16 = jnp.bfloat16


def mm(left, right):
    return jnp.dot(left, right, preferred_element_type=F32)


def mm_rows(left, right):
    return lax.dot_general(left, right, (((1,), (1,)), ((), ())), preferred_element_type=F32)


def mm_first(left, right):
    return lax.dot_general(left, right, (((0,), (0,)), ((), ())), preferred_element_type=F32)


def largest_tile(size, limit):
    tile = min(limit, size)
    while size % tile:
        tile -= BLK
    return tile


def gather_pair(first, second, product):
    cols = lax.axis_size("cols")
    if cols == 2:
        at_first = lax.axis_index("cols") == 0
        mine = product(
            jnp.where(at_first, first[0], second[0]), jnp.where(at_first, first[1], second[1])
        ).astype(BF16)
        return lax.all_gather(mine, ("cols", "rows"), axis=0, tiled=True)
    return jnp.concatenate(
        [
            lax.all_gather(product(*each).astype(BF16), "rows", axis=0, tiled=True)
            for each in (first, second)
        ]
    )


def place_body(pos1, in1, pos2, in2, u1_ref, u2_ref, link_ref, out_ref):
    at = pl.program_id(0)
    width = u1_ref.shape[1]
    keep1 = in1[at].astype(F32)
    keep2 = in2[at].astype(F32)
    u1 = u1_ref[...]
    linked = mm(u1, link_ref[...])
    out_ref[:width, :] = (-u1.astype(F32) * keep1).T.astype(BF16)
    out_ref[width:, :] = (linked * keep1 - u2_ref[...].astype(F32) * keep2).T.astype(BF16)


def blocks_in_tile(blocks, first_block, block_count):
    ids = first_block + jnp.arange(block_count, dtype=jnp.int32)
    matches = ids[:, None] == blocks[None, :]
    places = jnp.sum(
        jnp.where(matches, jnp.arange(blocks.shape[0], dtype=jnp.int32)[None, :], 0), axis=1
    )
    return places.astype(jnp.int32), jnp.any(matches, axis=1).astype(jnp.int32)


def rows_onto(panel, blocks, first_row, row_count):
    global_rows = first_row + jnp.arange(row_count, dtype=jnp.int32)
    matches = (global_rows // BLK)[:, None] == blocks[None, :]
    places = jnp.sum(
        jnp.where(matches, jnp.arange(blocks.shape[0], dtype=jnp.int32)[None, :], 0), axis=1
    )
    picked = jnp.take(panel, places * BLK + global_rows % BLK, axis=0)
    return jnp.where(jnp.any(matches, axis=1)[:, None], picked, jnp.zeros_like(picked))


def place_panels(both, link, list1, list2, first_row, row_count):
    width = both.shape[1]
    listed = list1.shape[0]
    if row_count % BLK:
        u1 = rows_onto(both[: listed * BLK], list1, first_row, row_count)
        u2 = rows_onto(both[listed * BLK :], list2, first_row, row_count)
        joined = jnp.concatenate([-u1.astype(F32), mm(u1, link) - u2.astype(F32)], axis=1)
        return joined.T.astype(BF16)
    first_block = first_row // BLK
    block_count = row_count // BLK
    pos1, in1 = blocks_in_tile(list1, first_block, block_count)
    pos2, in2 = blocks_in_tile(list2, first_block, block_count)
    return pl.pallas_call(
        place_body,
        out_shape=jax.ShapeDtypeStruct((2 * width, block_count * BLK), BF16),
        grid_spec=pltpu.PrefetchScalarGridSpec(
            num_scalar_prefetch=4,
            grid=(block_count,),
            in_specs=[
                pl.BlockSpec((BLK, width), lambda b, p1, i1, p2, i2: (p1[b], 0)),
                pl.BlockSpec((BLK, width), lambda b, p1, i1, p2, i2: (listed + p2[b], 0)),
                pl.BlockSpec((width, width), lambda b, p1, i1, p2, i2: (0, 0)),
            ],
            out_specs=pl.BlockSpec((2 * width, BLK), lambda b, p1, i1, p2, i2: (0, b)),
        ),
        compiler_params=pltpu.CompilerParams(vmem_limit_bytes=24 * 2**20),
        cost_estimate=pl.CostEstimate(
            flops=2 * block_count * BLK * width * width,
            bytes_accessed=8 * block_count * BLK * width,
            transcendentals=0,
        ),
        name="place_panels",
    )(pos1, in1, pos2, in2, both, both, link)


def lower_body(listed, loc1, in1, loc2, in2, part, *refs):
    tiles1, tiles2 = refs[:listed], refs[listed : 2 * listed]
    l1_ref, v1_ref, l2_ref, out_ref = refs[2 * listed :]
    half = l1_ref.shape[1]
    picked1 = jnp.concatenate(
        [tiles1[k][...] * in1[k].astype(F32).astype(BF16) for k in range(listed)], axis=1
    )
    picked2 = jnp.concatenate(
        [tiles2[k][...] * in2[k].astype(F32).astype(BF16) for k in range(listed)], axis=1
    )
    out_ref[:, :half] = (-mm(picked1, l1_ref[...])).astype(BF16)
    out_ref[:, half:] = (mm(picked1, v1_ref[...]) - mm(picked2, l2_ref[...])).astype(BF16)


def lower_partial(ancestor, both, linked, list1, list2, first_block, part, parts):
    rows, columns = ancestor.shape
    width = both.shape[1]
    half = width // parts
    listed = list1.shape[0]
    depth = listed * BLK
    block_count = columns // BLK
    tile = largest_tile(rows, 512)

    def local(blocks):
        at = blocks - first_block
        inside = jnp.logical_and(at >= 0, at < block_count)
        return jnp.clip(at, 0, block_count - 1), inside.astype(jnp.int32)

    loc1, in1 = local(list1)
    loc2, in2 = local(list2)
    specs = [
        pl.BlockSpec((tile, BLK), functools.partial(lambda k, i, l1, i1, l2, i2, p: (i, l1[k]), k))
        for k in range(listed)
    ] + [
        pl.BlockSpec((tile, BLK), functools.partial(lambda k, i, l1, i1, l2, i2, p: (i, l2[k]), k))
        for k in range(listed)
    ]
    specs += [
        pl.BlockSpec((depth, half), lambda i, l1, i1, l2, i2, p: (0, p[0])),
        pl.BlockSpec((depth, half), lambda i, l1, i1, l2, i2, p: (0, p[0])),
        pl.BlockSpec((depth, half), lambda i, l1, i1, l2, i2, p: (1, p[0])),
    ]
    return pl.pallas_call(
        functools.partial(lower_body, listed),
        out_shape=jax.ShapeDtypeStruct((rows, 2 * half), BF16),
        grid_spec=pltpu.PrefetchScalarGridSpec(
            num_scalar_prefetch=5,
            grid=(rows // tile,),
            in_specs=specs,
            out_specs=pl.BlockSpec((tile, 2 * half), lambda i, l1, i1, l2, i2, p: (i, 0)),
        ),
        compiler_params=pltpu.CompilerParams(vmem_limit_bytes=40 * 2**20),
        cost_estimate=pl.CostEstimate(
            flops=6 * rows * depth * half,
            bytes_accessed=4 * rows * depth + 6 * depth * half,
            transcendentals=0,
        ),
        name="lower_partial",
    )(
        loc1, in1, loc2, in2, jnp.reshape(part, (1,)).astype(jnp.int32),
        *([ancestor] * (2 * listed)), both, linked, both,
    )


def strip_body(strip, w_ref, a_ref, *refs):
    total = mm(w_ref[...], a_ref[...])
    for ref in refs[:-1]:
        total = total + ref[...].astype(F32)
    refs[-1][...] = total.astype(BF16)


def strip_product(ancestor, placed, strip, strips, *added):
    rows, columns = ancestor.shape
    strip_width = columns // strips
    height = placed.shape[0]
    if strip_width % BLK:
        total = mm(
            placed, lax.dynamic_slice_in_dim(ancestor, strip * strip_width, strip_width, 1)
        )
        for each in added:
            total = total + each.astype(F32)
        return total.astype(BF16)
    tile = largest_tile(strip_width, 256)
    per = strip_width // tile
    return pl.pallas_call(
        strip_body,
        out_shape=jax.ShapeDtypeStruct((height, strip_width), BF16),
        grid_spec=pltpu.PrefetchScalarGridSpec(
            num_scalar_prefetch=1,
            grid=(per,),
            in_specs=[
                pl.BlockSpec((height, rows), lambda j, s: (0, 0)),
                pl.BlockSpec((rows, tile), lambda j, s: (0, s[0] * per + j)),
            ]
            + [pl.BlockSpec((height, tile), lambda j, s: (0, j))] * len(added),
            out_specs=pl.BlockSpec((height, tile), lambda j, s: (0, j)),
        ),
        compiler_params=pltpu.CompilerParams(vmem_limit_bytes=40 * 2**20),
        cost_estimate=pl.CostEstimate(
            flops=2 * height * rows * strip_width,
            bytes_accessed=2 * (rows * strip_width + height * rows)
            + 2 * (1 + len(added)) * height * strip_width,
            transcendentals=0,
        ),
        name="strip_product",
    )(jnp.reshape(strip, (1,)).astype(jnp.int32), placed, ancestor, *added)


def add_pair(left, right):
    return (left.astype(F32) + right.astype(F32)).astype(BF16)


def upper_sums(ancestor, placed):
    strips = lax.axis_size("rows")
    row_at = lax.axis_index("rows")
    inner = 4 if strips % 4 == 0 else 1
    if inner == 1:
        whole = strip_product(ancestor, placed, 0, 1)
        return lax.psum_scatter(whole.astype(F32), "rows", scatter_dimension=1, tiled=True)
    depth = strips // inner
    core, side, level = row_at % 2, (row_at // 2) % 2, row_at // 4
    to_core = [(i, i ^ 1) for i in range(strips)]
    to_side = [(i, i ^ 2) for i in range(strips)]
    order = [sorted(range(depth), key=lambda d: (-abs(d - z), d)) for z in range(depth)]
    place = [[order[z].index(d) for d in range(depth)] for z in range(depth)]
    order_table = jnp.array(order, jnp.int32)

    def strip_of(target, x, c):
        return (target * 2 + x) * 2 + c

    layer = []
    for turn in range(depth):
        target = order_table[level, turn]
        far = strip_product(ancestor, placed, strip_of(target, 1 - side, 1 - core), strips)
        far = lax.ppermute(far, "rows", to_core)
        near = strip_product(ancestor, placed, strip_of(target, side, 1 - core), strips)
        near = lax.ppermute(near, "rows", to_core)
        far = strip_product(ancestor, placed, strip_of(target, 1 - side, core), strips, far)
        far = lax.ppermute(far, "rows", to_side)
        layer.append(
            strip_product(ancestor, placed, strip_of(target, side, core), strips, near, far)
        )

    def own_part(step, way):
        gap = depth - 1 - step
        chosen = None
        for z in range(depth):
            target = z + way * gap
            if 0 <= target < depth:
                value = layer[place[z][target]]
                chosen = value if chosen is None else jnp.where(level == z, value, chosen)
        return chosen

    arrived = {1: None, -1: None}
    for step in range(depth - 1):
        gap = depth - 1 - step
        for way in (1, -1):
            senders = [z for z in range(depth) if 0 <= z + way * gap < depth]
            pairs = [
                (z * inner + i, (z + way) * inner + i) for z in senders for i in range(inner)
            ]
            value = own_part(step, way)
            if arrived[way] is not None:
                value = add_pair(value, arrived[way])
            arrived[way] = lax.ppermute(value, "rows", pairs)
    total = layer[-1].astype(F32)
    for way in (1, -1):
        if arrived[way] is not None:
            total = total + arrived[way].astype(F32)
    return total


def body_general(
    ancestor,
    panel_below,
    panel_beside,
    inverse_lower,
    inverse_upper,
    list_below,
    list_beside,
    second_below,
    second_beside,
    linked_below,
    linked_beside,
    second_lower,
    second_upper,
    blocks_below,
    blocks_beside,
):
    row_at = lax.axis_index("rows")
    col_at = lax.axis_index("cols")
    cols = lax.axis_size("cols")
    tile_rows, tile_cols = ancestor.shape
    width = inverse_lower.shape[0]
    half = width // cols

    beside = gather_pair((panel_beside, inverse_upper), (second_beside, second_upper), mm_rows)
    below = gather_pair((panel_below, inverse_lower), (second_below, second_lower), mm)
    link_below = mm(linked_below, second_lower).astype(BF16)
    link_beside = mm_rows(linked_beside, second_upper).astype(BF16)

    placed = place_panels(
        beside, link_beside, list_beside, blocks_beside,
        row_at * tile_rows, tile_rows,
    )
    upper = upper_sums(ancestor, placed)
    new_upper = upper[:width].T.astype(BF16)
    next_upper = upper[width:].T.astype(BF16)

    depth = below.shape[0] // 2
    linked = mm(below[:depth], link_below).astype(BF16)
    lower_total = None
    sums_total = None
    for shift in reversed(range(cols)):
        part = (col_at + shift) % cols
        piece = lower_partial(
            ancestor, below, linked, list_below, blocks_below,
            col_at * (tile_cols // BLK), part, cols,
        )
        sums = jnp.concatenate(
            [mm(placed[:width], piece), mm(placed[width:], piece[:, half:])], axis=1
        )
        if shift:
            pairs = [(i, (i + shift) % cols) for i in range(cols)]
            piece = lax.ppermute(piece, "cols", pairs)
            sums = lax.ppermute(sums, "cols", pairs)
        piece = piece.astype(F32)
        lower_total = piece if lower_total is None else lower_total + piece
        sums_total = sums if sums_total is None else sums_total + sums
    new_lower = lower_total[:, :half].astype(BF16)
    next_lower = lower_total[:, half:].astype(BF16)

    sums = lax.psum(sums_total, "rows")

    def own(matrix):
        return lax.dynamic_slice_in_dim(matrix, col_at * half, half, 1)

    base = mm(inverse_upper, inverse_lower).astype(BF16)
    base_link = mm(base, own(link_below))
    new_diagonal = (mm(inverse_upper, own(inverse_lower)) + sums[:, :half]).astype(BF16)
    link_part = (sums[:, half : 2 * half] - base_link).astype(BF16)
    next_link = lax.all_gather(link_part, "cols", axis=1, tiled=True)
    next_diagonal = (
        mm(second_upper, own(second_lower))
        + mm_first(link_beside, base_link.astype(BF16))
        + sums[:, 2 * half :]
    ).astype(BF16)
    return (new_lower, new_upper, new_diagonal, next_lower, next_upper, next_link, next_diagonal)


SLOTS = 4
ANY = pl.BlockSpec(memory_space=pl.ANY)
SCALARS = pl.BlockSpec(memory_space=pltpu.SMEM)


def swapped(value, axis, bit):
    size = lax.axis_size(axis)
    return lax.ppermute(value, axis, [(i, i ^ bit) for i in range(size)])


def from_levels(value, shift):
    size = lax.axis_size("rows")
    return lax.ppermute(value, "rows", [(i, (i + 4 * shift) % size) for i in range(size)])


class Seat:
    def __init__(self):
        row_at = lax.axis_index("rows")
        self.row = row_at
        self.core, self.side, self.level = row_at % 2, (row_at // 2) % 2, row_at // 4
        self.depth = lax.axis_size("rows") // 4
        self.col = lax.axis_index("cols")


def plan_body(block_count, row, l1, l2, local, meta, b1, m1, b2, m2, at1, at2):
    listed = l1.shape[0]
    tiles = at1.shape[0] // block_count
    own = row[0]

    @pl.loop(0, at1.shape[0])
    def _(i):
        at1[i] = 0
        at2[i] = 0

    @pl.loop(0, listed)
    def _(k):
        at1[l1[k]] = k + 1
        at2[l2[k]] = k + 1

    @pl.loop(0, b1.shape[0])
    def _(s):
        b1[s] = 0
        m1[s] = 0
        b2[s] = 0
        m2[s] = 0

    def scan(tile, put):
        def step(b, rank):
            g = tile * block_count + b
            here = jnp.where(at1[g] + at2[g] > 0, 1, 0)
            put(rank, b, g, here)
            return rank + here

        return lax.fori_loop(0, block_count, step, jnp.int32(0))

    def place(slot, g):
        b1[slot] = 2 * jnp.maximum(at1[g] - 1, 0)
        m1[slot] = jnp.where(at1[g] > 0, 1, 0)
        b2[slot] = 2 * (listed + jnp.maximum(at2[g] - 1, 0))
        m2[slot] = jnp.where(at2[g] > 0, 1, 0)

    def put_own(rank, b, g, here):
        local[rank] = b
        place(SLOTS + rank, g)

    def put_facing(rank, b, g, here):
        @pl.when(jnp.logical_and(here > 0, rank < SLOTS))
        def _():
            place(rank, g)

    def nothing(rank, b, g, here):
        return None

    @pl.loop(0, block_count)
    def _(s):
        local[s] = 0

    meta[0] = scan(own, put_own)
    meta[1] = scan(own ^ 1, nothing)
    facing = scan(own ^ 2, put_facing)

    def put_beyond(rank, b, g, here):
        slot = facing + rank - SLOTS

        @pl.when(jnp.logical_and(here > 0, jnp.logical_and(rank >= SLOTS, slot < SLOTS)))
        def _():
            place(slot, g)

    scan(own ^ 3, put_beyond)

    def most(chip, found):
        count = scan(2 * chip, nothing) + scan(2 * chip + 1, nothing)
        return jnp.maximum(found, count)

    meta[2] = lax.fori_loop(0, tiles // 2, most, jnp.int32(0))


def plan_slots(row, list1, list2, block_count, tiles):
    def numbers(count):
        return jax.ShapeDtypeStruct((count,), jnp.int32)

    slots = SLOTS + block_count
    return pl.pallas_call(
        functools.partial(plan_body, block_count),
        out_shape=(numbers(block_count), numbers(3)) + (numbers(slots),) * 4,
        in_specs=[SCALARS] * 3,
        out_specs=(SCALARS,) * 6,
        scratch_shapes=[pltpu.SMEM((tiles * block_count,), jnp.int32)] * 2,
        name="plan_slots",
    )(jnp.reshape(row, (1,)).astype(jnp.int32), list1, list2)


def place_slots_body(b1, m1, b2, m2, u1_ref, u2_ref, link_ref, *refs):
    out_ref = refs[-1]
    at = pl.program_id(0)
    width = u1_ref.shape[1]
    used = m1[at] + m2[at] > 0

    @pl.when(used)
    def _():
        keep1 = m1[at].astype(F32)
        keep2 = m2[at].astype(F32)
        u1 = u1_ref[...]
        linked = mm(u1, link_ref[...])
        out_ref[:width, :] = (-u1.astype(F32) * keep1).T.astype(BF16)
        out_ref[width:, :] = (linked * keep1 - u2_ref[...].astype(F32) * keep2).T.astype(BF16)

    @pl.when(jnp.logical_not(used))
    def _():
        out_ref[...] = jnp.zeros_like(out_ref)


def place_slots(gathered, link, tables, first):
    width = gathered.shape[1]
    count = tables[0].shape[0]
    return pl.pallas_call(
        place_slots_body,
        out_shape=jax.ShapeDtypeStruct((2 * width, count * BLK), BF16),
        grid_spec=pltpu.PrefetchScalarGridSpec(
            num_scalar_prefetch=4,
            grid=(count,),
            in_specs=[
                pl.BlockSpec((BLK, width), lambda s, p1, i1, p2, i2: (p1[s], 0)),
                pl.BlockSpec((BLK, width), lambda s, p1, i1, p2, i2: (p2[s], 0)),
                pl.BlockSpec((width, width), lambda s, p1, i1, p2, i2: (0, 0)),
            ]
            + [ANY] * len(first),
            out_specs=pl.BlockSpec((2 * width, BLK), lambda s, p1, i1, p2, i2: (0, s)),
        ),
        compiler_params=pltpu.CompilerParams(vmem_limit_bytes=24 * 2**20),
        cost_estimate=pl.CostEstimate(
            flops=2 * count * BLK * width * width // 4,
            bytes_accessed=4 * count * BLK * width,
            transcendentals=0,
        ),
        name="place_slots",
    )(*tables, gathered, gathered, link, *first)


def pack_body(local, pair, a_ref, out_ref, sems):
    wide = out_ref.shape[1]
    column = pl.multiple_of(pair[0] * wide, BLK)

    def copy(s):
        row = pl.multiple_of(local[SLOTS + s] * BLK, BLK)
        return pltpu.make_async_copy(
            a_ref.at[pl.ds(row, BLK), pl.ds(column, wide)],
            out_ref.at[pl.ds(s * BLK, BLK), :],
            sems.at[s],
        )

    for s in range(SLOTS):
        copy(s).start()
    for s in range(SLOTS):
        copy(s).wait()


def pack(ancestor, local, pair, pairs):
    wide = ancestor.shape[1] // pairs
    return pl.pallas_call(
        pack_body,
        out_shape=jax.ShapeDtypeStruct((SLOTS * BLK, wide), BF16),
        grid_spec=pltpu.PrefetchScalarGridSpec(
            num_scalar_prefetch=2,
            grid=(1,),
            in_specs=[ANY],
            out_specs=ANY,
            scratch_shapes=[pltpu.SemaphoreType.DMA((SLOTS,))],
        ),
        cost_estimate=pl.CostEstimate(
            flops=0, bytes_accessed=4 * SLOTS * BLK * wide, transcendentals=0
        ),
        name="pack_slots",
    )(local, jnp.reshape(pair, (1,)).astype(jnp.int32), ancestor)


def merge_body(local, meta, pair, a_ref, got_ref, *refs):
    out_ref, sems = refs[-2:]
    wide = out_ref.shape[1]
    column = pl.multiple_of(pair[0] * wide, BLK)
    count = meta[0]

    def own(s):
        row = pl.multiple_of(local[s] * BLK, BLK)
        return pltpu.make_async_copy(
            a_ref.at[pl.ds(row, BLK), pl.ds(column, wide)],
            out_ref.at[pl.ds(s * BLK, BLK), :],
            sems.at[s],
        )

    def passed(s):
        row = pl.multiple_of(jnp.clip(s - count, 0, SLOTS - 1) * BLK, BLK)
        return pltpu.make_async_copy(
            got_ref.at[pl.ds(row, BLK), :],
            out_ref.at[pl.ds(s * BLK, BLK), :],
            sems.at[s],
        )

    for act in ("start", "wait"):
        for s in range(SLOTS):

            @pl.when(s < count)
            def _():
                getattr(own(s), act)()

            @pl.when(s >= count)
            def _():
                getattr(passed(s), act)()


def merge(ancestor, got, local, meta, pair, pairs, first):
    wide = ancestor.shape[1] // pairs
    return pl.pallas_call(
        merge_body,
        out_shape=jax.ShapeDtypeStruct((SLOTS * BLK, wide), BF16),
        grid_spec=pltpu.PrefetchScalarGridSpec(
            num_scalar_prefetch=3,
            grid=(1,),
            in_specs=[ANY] * (2 + len(first)),
            out_specs=ANY,
            scratch_shapes=[pltpu.SemaphoreType.DMA((SLOTS,))],
        ),
        cost_estimate=pl.CostEstimate(
            flops=0, bytes_accessed=4 * SLOTS * BLK * wide, transcendentals=0
        ),
        name="merge_slots",
    )(local, meta, jnp.reshape(pair, (1,)).astype(jnp.int32), ancestor, got, *first)


def lower_slots_body(listed, block_count, l1, l2, at, *refs):
    tiles1, tiles2 = refs[:listed], refs[listed : 2 * listed]
    own1_ref, whole1_ref, own2_ref, link_ref = refs[2 * listed : 2 * listed + 4]
    out_ref, linked_ref = refs[-2:]
    half = link_ref.shape[1]
    depth = listed * BLK

    @pl.when(pl.program_id(0) == 0)
    def _():
        whole = whole1_ref[...].reshape(depth, whole1_ref.shape[2])
        linked_ref[...] = mm(whole, link_ref[...]).astype(BF16)

    def picked(tiles, blocks):
        kept = []
        for k in range(listed):
            place = blocks[k] - at[0]
            inside = jnp.logical_and(place >= 0, place < block_count)
            kept.append(tiles[k][...] * jnp.where(inside, 1.0, 0.0).astype(BF16))
        return jnp.concatenate(kept, axis=1)

    picked1 = picked(tiles1, l1)
    out_ref[:, :half] = (-mm(picked1, own1_ref[...].reshape(depth, half))).astype(BF16)
    second = mm(picked1, linked_ref[...])
    second = second - mm(picked(tiles2, l2), own2_ref[...].reshape(depth, half))
    out_ref[:, half:] = second.astype(BF16)


def lower_slots(ancestor, gathered, link, list1, list2, first_block, part, first):
    rows, columns = ancestor.shape
    listed, width = list1.shape[0], link.shape[0]
    half = width // 2
    block_count = columns // BLK
    tile = largest_tile(rows, 512)
    shaped = gathered.reshape(2 * listed, 2, BLK, width)
    at = jnp.stack([first_block, part]).astype(jnp.int32)

    def column(which, k):
        def index(i, l1, l2, at):
            return i, jnp.clip((l1, l2)[which][k] - at[0], 0, block_count - 1)

        return pl.BlockSpec((tile, BLK), index)

    specs = [column(which, k) for which in (0, 1) for k in range(listed)]
    specs += [
        pl.BlockSpec((listed, None, BLK, half), lambda i, l1, l2, at: (0, 1, 0, at[1])),
        pl.BlockSpec((listed, None, BLK, width), lambda i, l1, l2, at: (0, 1, 0, 0)),
        pl.BlockSpec((listed, None, BLK, half), lambda i, l1, l2, at: (1, 1, 0, at[1])),
        pl.BlockSpec((width, half), lambda i, l1, l2, at: (0, at[1])),
    ]
    return pl.pallas_call(
        functools.partial(lower_slots_body, listed, block_count),
        out_shape=jax.ShapeDtypeStruct((rows, 2 * half), BF16),
        grid_spec=pltpu.PrefetchScalarGridSpec(
            num_scalar_prefetch=3,
            grid=(rows // tile,),
            in_specs=specs + [ANY] * len(first),
            out_specs=pl.BlockSpec((tile, 2 * half), lambda i, l1, l2, at: (i, 0)),
            scratch_shapes=[pltpu.VMEM((listed * BLK, half), BF16)],
        ),
        compiler_params=pltpu.CompilerParams(vmem_limit_bytes=48 * 2**20),
        cost_estimate=pl.CostEstimate(
            flops=6 * rows * listed * BLK * half,
            bytes_accessed=4 * rows * listed * BLK + 8 * listed * BLK * width,
            transcendentals=0,
        ),
        name="lower_slots",
    )(
        list1, list2, at, *([ancestor] * (2 * listed)), shaped, shaped, shaped, link, *first
    )


def slots_body(units, local, count, at, *refs):
    w_refs, arrived_ref = refs[:units], refs[units]
    tiles = refs[units + 1 : units + 1 + (units - 1) * SLOTS]
    added = refs[units + 1 + (units - 1) * SLOTS : -1]
    out_ref = refs[-1]

    def own(unit):
        group = tiles[(unit - 1) * SLOTS : unit * SLOTS]
        return mm(w_refs[unit][...], jnp.concatenate([ref[...] for ref in group], axis=0))

    def store(more):
        total = mm(w_refs[0][...], arrived_ref[...]) + own(1)
        for unit in more:
            total = total + own(unit)
        for ref in added:
            total = total + ref[...].astype(F32)
        out_ref[...] = total.astype(BF16)

    @pl.when(count[0] <= SLOTS)
    def _():
        store(())

    @pl.when(count[0] > SLOTS)
    def _():
        store(range(2, units))


def slots_product(ancestor, placed, arrived, local, count, strip, within, strips, *added):
    columns = ancestor.shape[1]
    strip_width = columns // strips
    height = placed.shape[0]
    tile = largest_tile(strip_width, 384)
    per = strip_width // tile
    unit_width = SLOTS * BLK
    units = placed.shape[1] // unit_width
    where_at = jnp.stack([strip * per, within * per]).astype(jnp.int32)

    def own_block(slot):
        if slot < SLOTS:
            return lambda j, l, n, p: (l[slot], p[0] + j)
        return lambda j, l, n, p: (l[slot], jnp.where(n[0] > SLOTS, p[0] + j, 0))

    def unit_block(unit):
        if unit < 2:
            return lambda j, l, n, p: (0, unit)
        return lambda j, l, n, p: (0, jnp.where(n[0] > SLOTS, unit, 0))

    own_slots = (units - 1) * SLOTS
    return pl.pallas_call(
        functools.partial(slots_body, units),
        out_shape=jax.ShapeDtypeStruct((height, strip_width), BF16),
        grid_spec=pltpu.PrefetchScalarGridSpec(
            num_scalar_prefetch=3,
            grid=(per,),
            in_specs=[pl.BlockSpec((height, unit_width), unit_block(u)) for u in range(units)]
            + [pl.BlockSpec((unit_width, tile), lambda j, l, n, p: (0, p[1] + j))]
            + [pl.BlockSpec((BLK, tile), own_block(slot)) for slot in range(own_slots)]
            + [pl.BlockSpec((height, tile), lambda j, l, n, p: (0, j))] * len(added),
            out_specs=pl.BlockSpec((height, tile), lambda j, l, n, p: (0, j)),
        ),
        compiler_params=pltpu.CompilerParams(vmem_limit_bytes=40 * 2**20),
        cost_estimate=pl.CostEstimate(
            flops=4 * height * unit_width * strip_width,
            bytes_accessed=4 * unit_width * (height + strip_width)
            + 2 * (1 + len(added)) * height * strip_width,
            transcendentals=0,
        ),
        name="slots_product",
    )(
        local, jnp.reshape(count, (1,)), where_at,
        *([placed] * units), arrived, *([ancestor] * own_slots), *added,
    )


def small_sums_body(local, count, w_ref, x_ref, out_ref, total_ref):
    at = pl.program_id(0)
    width = w_ref.shape[0] // 2
    half = x_ref.shape[1] // 2

    @pl.when(at == 0)
    def _():
        total_ref[...] = jnp.zeros_like(total_ref)

    @pl.when(at < count[0])
    def _():
        total_ref[:, : 2 * half] += mm(w_ref[:width, :], x_ref[...])
        total_ref[:, 2 * half :] += mm(w_ref[width:, :], x_ref[:, half:])

    @pl.when(at == pl.num_programs(0) - 1)
    def _():
        out_ref[...] = total_ref[...].astype(BF16)


def small_sums(placed, piece, local, count):
    width = placed.shape[0] // 2
    half = piece.shape[1] // 2
    slots = local.shape[0]
    return pl.pallas_call(
        small_sums_body,
        out_shape=jax.ShapeDtypeStruct((width, 3 * half), BF16),
        grid_spec=pltpu.PrefetchScalarGridSpec(
            num_scalar_prefetch=2,
            grid=(slots,),
            in_specs=[
                pl.BlockSpec((2 * width, BLK), lambda s, l, n: (0, SLOTS + s)),
                pl.BlockSpec((BLK, 2 * half), lambda s, l, n: (l[s], 0)),
            ],
            out_specs=pl.BlockSpec((width, 3 * half), lambda s, l, n: (0, 0)),
            scratch_shapes=[pltpu.VMEM((width, 3 * half), F32)],
        ),
        compiler_params=pltpu.CompilerParams(vmem_limit_bytes=24 * 2**20),
        cost_estimate=pl.CostEstimate(
            flops=2 * SLOTS * BLK * width * 3 * half,
            bytes_accessed=4 * slots * BLK * width,
            transcendentals=0,
        ),
        name="small_sums",
    )(local, jnp.reshape(count, (1,)), placed, piece)


def level_chain(seat, layer, place):
    depth = seat.depth
    arrived = {1: None, -1: None}
    for step in range(depth - 1):
        gap = depth - 1 - step
        for way in (1, -1):
            senders = [z for z in range(depth) if 0 <= z + way * gap < depth]
            pairs = [(z * 4 + i, (z + way) * 4 + i) for z in senders for i in range(4)]
            value = None
            for z in senders:
                each = layer[place[z][z + way * gap]]
                value = each if value is None else jnp.where(seat.level == z, each, value)
            if arrived[way] is not None:
                value = add_pair(value, arrived[way])
            arrived[way] = lax.ppermute(value, "rows", pairs)
    total = layer[-1].astype(F32)
    for way in (1, -1):
        total = total + arrived[way].astype(F32)
    return total


def left_over(seat, ancestor, gathered, link, lists, places, dropped):
    block_rows, columns = ancestor.shape
    first_row = seat.row * block_rows
    shaped = gathered.reshape(-1, BLK, gathered.shape[1])
    u1, u2 = (
        rows_onto(
            jnp.take(shaped, place, axis=0).reshape(-1, gathered.shape[1]),
            blocks, first_row, block_rows,
        )
        for blocks, place in zip(lists, places)
    )
    joined = jnp.concatenate([-u1.astype(F32), mm(u1, link) - u2.astype(F32)], axis=1)
    joined = jnp.where(jnp.repeat(dropped, BLK)[:, None], joined, 0.0).astype(BF16)
    strip_width = columns // (4 * seat.depth)
    side = (jnp.arange(columns, dtype=jnp.int32) // strip_width // 2) % 2
    partial = jnp.where((side != seat.side)[None, :], mm_first(joined, ancestor), 0.0)
    return lax.psum_scatter(partial, "rows", scatter_dimension=1, tiled=True)


def sum_small(seat, sums):
    rows = sums.shape[0]

    def halves(value, bit):
        size = value.shape[0] // 2
        kept = lax.dynamic_slice_in_dim(value, bit * size, size, 0)
        given = lax.dynamic_slice_in_dim(value, (1 - bit) * size, size, 0)
        return kept, given

    kept, given = halves(sums, seat.core)
    sums = add_pair(kept, swapped(given, "rows", 1))
    kept, given = halves(sums, seat.side)
    sums = add_pair(kept, swapped(given, "rows", 2))
    size = rows // (4 * seat.depth)

    def level_rows(level):
        return lax.dynamic_slice_in_dim(sums, level * size, size, 0)

    total = level_rows(seat.level).astype(F32)
    for shift in range(1, seat.depth):
        given = level_rows((seat.level + shift) % seat.depth)
        total = total + from_levels(given, shift).astype(F32)
    return total


def gather_small(seat, mine):
    levels = [mine] + [from_levels(mine, shift) for shift in range(1, seat.depth)]
    value = jnp.concatenate(
        [
            lax.select_n((seat.level - z) % seat.depth, *levels)
            if seat.depth > 2
            else jnp.where(seat.level == z, levels[0], levels[-1])
            for z in range(seat.depth)
        ]
    )
    for bit, at in ((2, seat.side), (1, seat.core)):
        other = swapped(value, "rows", bit)
        value = jnp.concatenate(
            [jnp.where(at == 0, value, other), jnp.where(at == 0, other, value)]
        )
    return value


def body_by_slots(
    ancestor,
    panel_below,
    panel_beside,
    inverse_lower,
    inverse_upper,
    list_below,
    list_beside,
    second_below,
    second_beside,
    linked_below,
    linked_beside,
    second_lower,
    second_upper,
    blocks_below,
    blocks_beside,
):
    seat = Seat()
    tile_rows, tile_cols = ancestor.shape
    block_count = tile_rows // BLK
    width = inverse_lower.shape[0]
    half = width // 2
    listed = list_below.shape[0]
    depth = seat.depth
    rows = 4 * depth
    pairs = 2 * depth
    at_first = seat.col == 0

    def either(first, second):
        return jnp.where(at_first, first, second)

    beside = mm_rows(either(panel_beside, second_beside), either(inverse_upper, second_upper))
    below = mm(either(panel_below, second_below), either(inverse_lower, second_lower))
    gathered = lax.all_gather(
        jnp.concatenate([beside, below]).astype(BF16), ("cols", "rows"), axis=0, tiled=True
    )
    link_below = mm(linked_below, second_lower).astype(BF16)
    link_beside = mm_rows(linked_beside, second_upper).astype(BF16)

    local, meta, *tables = plan_slots(
        seat.row, list_beside, blocks_beside, block_count, rows
    )
    count = meta[0]
    order = [sorted(range(depth), key=lambda d: (-abs(d - z), d)) for z in range(depth)]
    place = [[order[z].index(d) for d in range(depth)] for z in range(depth)]
    order_table = jnp.array(order, jnp.int32)
    targets = [order_table[seat.level, turn] for turn in range(depth)]

    passed = [
        swapped(pack(ancestor, local, target * 2 + 1 - seat.side, pairs), "rows", 1)
        for target in targets
    ]
    leaving, arrived = [], []
    for target, got in zip(targets, passed):
        leaving.append(
            merge(
                ancestor, got, local, meta, target * 2 + 1 - seat.side, pairs, leaving[-1:]
            )
        )
        arrived.append(swapped(leaving[-1], "rows", 2))

    placed = place_slots(gathered, link_beside, tables, leaving)

    def lower(shift, first):
        return lower_slots(
            ancestor, gathered, link_below, list_below, blocks_below,
            seat.col * (tile_cols // BLK), seat.col ^ shift, first,
        )

    def strip(turn, part, *added):
        pair = targets[turn] * 2 + seat.side
        return slots_product(
            ancestor, placed, arrived[turn], local, count, pair * 2 + part, part, rows, *added
        )

    layer = []
    for turn in range(depth):
        far = strip(turn, 1 - seat.core)
        if turn == 0:
            given = lower(1, [far])
        layer.append(strip(turn, seat.core, swapped(far, "rows", 1)))
    kept = lower(0, [given, layer[0]])
    given_sums = small_sums(placed, given, local, count)
    kept_sums = small_sums(placed, kept, local, count)
    got_sums = swapped(given_sums, "cols", 1)
    upper = level_chain(seat, layer, place)

    def with_rest(total):
        own_at = jnp.arange(block_count, dtype=jnp.int32)
        slot_dropped = jnp.logical_and(
            own_at < count, own_at >= 2 * SLOTS - jnp.minimum(meta[1], SLOTS)
        )
        dropped = jnp.any(
            jnp.logical_and(slot_dropped[:, None], local[:, None] == own_at[None, :]), axis=0
        )
        at = 2 * jnp.arange(listed, dtype=jnp.int32)
        return total + left_over(
            seat, ancestor, gathered, link_beside, (list_beside, blocks_beside),
            (at, at + 2 * listed), dropped,
        )

    upper = lax.cond(meta[2] > 2 * SLOTS, with_rest, lambda total: total, upper)
    new_upper = upper[:width].T.astype(BF16)
    next_upper = upper[width:].T.astype(BF16)

    given, _ = lax.optimization_barrier((given, got_sums))
    piece = kept.astype(F32) + swapped(given, "cols", 1).astype(F32)
    new_lower = piece[:, :half].astype(BF16)
    next_lower = piece[:, half:].astype(BF16)
    mine = sum_small(seat, add_pair(kept_sums, got_sums))

    def own(matrix):
        return lax.dynamic_slice_in_dim(matrix, seat.col * half, half, 1)

    base = mm(inverse_upper, inverse_lower).astype(BF16)
    base_link = mm(base, own(link_below))
    added = jnp.concatenate(
        [
            mm(inverse_upper, own(inverse_lower)),
            -base_link,
            mm(second_upper, own(second_lower)) + mm_first(link_beside, base_link.astype(BF16)),
        ],
        axis=1,
    )
    size = width // rows
    first = (seat.core * 2 + seat.side) * (width // 4) + seat.level * size
    mine = mine + lax.dynamic_slice_in_dim(added, first, size, 0)
    whole = gather_small(seat, mine.astype(BF16))
    link_part = whole[:, half : 2 * half]
    link_other = swapped(link_part, "cols", 1)
    next_link = jnp.concatenate(
        [either(link_part, link_other), either(link_other, link_part)], axis=1
    )
    return (
        new_lower, new_upper, whole[:, :half], next_lower, next_upper, next_link,
        whole[:, 2 * half :],
    )


def body(*arrays):
    ancestor, panel, list_beside = arrays[0], arrays[1], arrays[6]
    rows, cols = lax.axis_size("rows"), lax.axis_size("cols")
    by_slots = (
        cols == 2
        and rows % 4 == 0
        and rows > 4
        and panel.shape[0] == BLK
        and list_beside.shape[0] == rows
        and ancestor.shape[0] % BLK == 0
        and ancestor.shape[0] // BLK >= 2 * SLOTS
        and ancestor.shape[0] // BLK % SLOTS == 0
        and ancestor.shape[1] % (rows * BLK) == 0
        and panel.shape[1] % (2 * rows) == 0
    )
    return (body_by_slots if by_slots else body_general)(*arrays)


def solution(mesh):
    return jax.shard_map(
        body,
        mesh=mesh,
        in_specs=(
            P("rows", "cols"),
            P("rows", None),
            P("rows", None),
            P(),
            P(),
            P(),
            P(),
            P("rows", None),
            P("rows", None),
            P(),
            P(),
            P(),
            P(),
            P(),
            P(),
        ),
        out_specs=(
            P("rows", "cols"),
            P(("cols", "rows"), None),
            P(None, "cols"),
            P("rows", "cols"),
            P(("cols", "rows"), None),
            P(),
            P(None, "cols"),
        ),
        check_vma=False,
    )
```

```python
import functools

import jax
import jax.numpy as jnp
from jax import lax
from jax.experimental import pallas as pl
from jax.experimental.pallas import tpu as pltpu
from jax.sharding import PartitionSpec as P

BLK = 128
F32 = jnp.float32
BF16 = jnp.bfloat16


def mm(left, right):
    return jnp.dot(left, right, preferred_element_type=F32)


def mm_rows(left, right):
    return lax.dot_general(left, right, (((1,), (1,)), ((), ())), preferred_element_type=F32)


def mm_first(left, right):
    return lax.dot_general(left, right, (((0,), (0,)), ((), ())), preferred_element_type=F32)


def largest_tile(size, limit):
    tile = min(limit, size)
    while size % tile:
        tile -= BLK
    return tile


def gather_pair(first, second, product):
    cols = lax.axis_size("cols")
    if cols == 2:
        at_first = lax.axis_index("cols") == 0
        mine = product(
            jnp.where(at_first, first[0], second[0]), jnp.where(at_first, first[1], second[1])
        ).astype(BF16)
        return lax.all_gather(mine, ("cols", "rows"), axis=0, tiled=True)
    return jnp.concatenate(
        [
            lax.all_gather(product(*each).astype(BF16), "rows", axis=0, tiled=True)
            for each in (first, second)
        ]
    )


def place_body(pos1, in1, pos2, in2, u1_ref, u2_ref, link_ref, out_ref):
    at = pl.program_id(0)
    width = u1_ref.shape[1]
    keep1 = in1[at].astype(F32)
    keep2 = in2[at].astype(F32)
    u1 = u1_ref[...]
    linked = mm(u1, link_ref[...])
    out_ref[:width, :] = (-u1.astype(F32) * keep1).T.astype(BF16)
    out_ref[width:, :] = (linked * keep1 - u2_ref[...].astype(F32) * keep2).T.astype(BF16)


def blocks_in_tile(blocks, first_block, block_count):
    ids = first_block + jnp.arange(block_count, dtype=jnp.int32)
    matches = ids[:, None] == blocks[None, :]
    places = jnp.sum(
        jnp.where(matches, jnp.arange(blocks.shape[0], dtype=jnp.int32)[None, :], 0), axis=1
    )
    return places.astype(jnp.int32), jnp.any(matches, axis=1).astype(jnp.int32)


def rows_onto(panel, blocks, first_row, row_count):
    global_rows = first_row + jnp.arange(row_count, dtype=jnp.int32)
    matches = (global_rows // BLK)[:, None] == blocks[None, :]
    places = jnp.sum(
        jnp.where(matches, jnp.arange(blocks.shape[0], dtype=jnp.int32)[None, :], 0), axis=1
    )
    picked = jnp.take(panel, places * BLK + global_rows % BLK, axis=0)
    return jnp.where(jnp.any(matches, axis=1)[:, None], picked, jnp.zeros_like(picked))


def place_panels(both, link, list1, list2, first_row, row_count):
    width = both.shape[1]
    listed = list1.shape[0]
    if row_count % BLK:
        u1 = rows_onto(both[: listed * BLK], list1, first_row, row_count)
        u2 = rows_onto(both[listed * BLK :], list2, first_row, row_count)
        joined = jnp.concatenate([-u1.astype(F32), mm(u1, link) - u2.astype(F32)], axis=1)
        return joined.T.astype(BF16)
    first_block = first_row // BLK
    block_count = row_count // BLK
    pos1, in1 = blocks_in_tile(list1, first_block, block_count)
    pos2, in2 = blocks_in_tile(list2, first_block, block_count)
    return pl.pallas_call(
        place_body,
        out_shape=jax.ShapeDtypeStruct((2 * width, block_count * BLK), BF16),
        grid_spec=pltpu.PrefetchScalarGridSpec(
            num_scalar_prefetch=4,
            grid=(block_count,),
            in_specs=[
                pl.BlockSpec((BLK, width), lambda b, p1, i1, p2, i2: (p1[b], 0)),
                pl.BlockSpec((BLK, width), lambda b, p1, i1, p2, i2: (listed + p2[b], 0)),
                pl.BlockSpec((width, width), lambda b, p1, i1, p2, i2: (0, 0)),
            ],
            out_specs=pl.BlockSpec((2 * width, BLK), lambda b, p1, i1, p2, i2: (0, b)),
        ),
        compiler_params=pltpu.CompilerParams(vmem_limit_bytes=24 * 2**20),
        cost_estimate=pl.CostEstimate(
            flops=2 * block_count * BLK * width * width,
            bytes_accessed=8 * block_count * BLK * width,
            transcendentals=0,
        ),
        name="place_panels",
    )(pos1, in1, pos2, in2, both, both, link)


def lower_body(listed, loc1, in1, loc2, in2, part, *refs):
    tiles1, tiles2 = refs[:listed], refs[listed : 2 * listed]
    l1_ref, v1_ref, l2_ref, out_ref = refs[2 * listed :]
    half = l1_ref.shape[1]
    picked1 = jnp.concatenate(
        [tiles1[k][...] * in1[k].astype(F32).astype(BF16) for k in range(listed)], axis=1
    )
    picked2 = jnp.concatenate(
        [tiles2[k][...] * in2[k].astype(F32).astype(BF16) for k in range(listed)], axis=1
    )
    out_ref[:, :half] = (-mm(picked1, l1_ref[...])).astype(BF16)
    out_ref[:, half:] = (mm(picked1, v1_ref[...]) - mm(picked2, l2_ref[...])).astype(BF16)


def lower_partial(ancestor, both, linked, list1, list2, first_block, part, parts):
    rows, columns = ancestor.shape
    width = both.shape[1]
    half = width // parts
    listed = list1.shape[0]
    depth = listed * BLK
    block_count = columns // BLK
    tile = largest_tile(rows, 512)

    def local(blocks):
        at = blocks - first_block
        inside = jnp.logical_and(at >= 0, at < block_count)
        return jnp.clip(at, 0, block_count - 1), inside.astype(jnp.int32)

    loc1, in1 = local(list1)
    loc2, in2 = local(list2)
    specs = [
        pl.BlockSpec((tile, BLK), functools.partial(lambda k, i, l1, i1, l2, i2, p: (i, l1[k]), k))
        for k in range(listed)
    ] + [
        pl.BlockSpec((tile, BLK), functools.partial(lambda k, i, l1, i1, l2, i2, p: (i, l2[k]), k))
        for k in range(listed)
    ]
    specs += [
        pl.BlockSpec((depth, half), lambda i, l1, i1, l2, i2, p: (0, p[0])),
        pl.BlockSpec((depth, half), lambda i, l1, i1, l2, i2, p: (0, p[0])),
        pl.BlockSpec((depth, half), lambda i, l1, i1, l2, i2, p: (1, p[0])),
    ]
    return pl.pallas_call(
        functools.partial(lower_body, listed),
        out_shape=jax.ShapeDtypeStruct((rows, 2 * half), BF16),
        grid_spec=pltpu.PrefetchScalarGridSpec(
            num_scalar_prefetch=5,
            grid=(rows // tile,),
            in_specs=specs,
            out_specs=pl.BlockSpec((tile, 2 * half), lambda i, l1, i1, l2, i2, p: (i, 0)),
        ),
        compiler_params=pltpu.CompilerParams(vmem_limit_bytes=40 * 2**20),
        cost_estimate=pl.CostEstimate(
            flops=6 * rows * depth * half,
            bytes_accessed=4 * rows * depth + 6 * depth * half,
            transcendentals=0,
        ),
        name="lower_partial",
    )(
        loc1, in1, loc2, in2, jnp.reshape(part, (1,)).astype(jnp.int32),
        *([ancestor] * (2 * listed)), both, linked, both,
    )


def strip_body(strip, w_ref, a_ref, *refs):
    total = mm(w_ref[...], a_ref[...])
    for ref in refs[:-1]:
        total = total + ref[...].astype(F32)
    refs[-1][...] = total.astype(BF16)


def strip_product(ancestor, placed, strip, strips, *added):
    rows, columns = ancestor.shape
    strip_width = columns // strips
    height = placed.shape[0]
    if strip_width % BLK:
        total = mm(
            placed, lax.dynamic_slice_in_dim(ancestor, strip * strip_width, strip_width, 1)
        )
        for each in added:
            total = total + each.astype(F32)
        return total.astype(BF16)
    tile = largest_tile(strip_width, 256)
    per = strip_width // tile
    return pl.pallas_call(
        strip_body,
        out_shape=jax.ShapeDtypeStruct((height, strip_width), BF16),
        grid_spec=pltpu.PrefetchScalarGridSpec(
            num_scalar_prefetch=1,
            grid=(per,),
            in_specs=[
                pl.BlockSpec((height, rows), lambda j, s: (0, 0)),
                pl.BlockSpec((rows, tile), lambda j, s: (0, s[0] * per + j)),
            ]
            + [pl.BlockSpec((height, tile), lambda j, s: (0, j))] * len(added),
            out_specs=pl.BlockSpec((height, tile), lambda j, s: (0, j)),
        ),
        compiler_params=pltpu.CompilerParams(vmem_limit_bytes=40 * 2**20),
        cost_estimate=pl.CostEstimate(
            flops=2 * height * rows * strip_width,
            bytes_accessed=2 * (rows * strip_width + height * rows)
            + 2 * (1 + len(added)) * height * strip_width,
            transcendentals=0,
        ),
        name="strip_product",
    )(jnp.reshape(strip, (1,)).astype(jnp.int32), placed, ancestor, *added)


def add_pair(left, right):
    return (left.astype(F32) + right.astype(F32)).astype(BF16)


def upper_sums(ancestor, placed):
    strips = lax.axis_size("rows")
    row_at = lax.axis_index("rows")
    inner = 4 if strips % 4 == 0 else 1
    if inner == 1:
        whole = strip_product(ancestor, placed, 0, 1)
        return lax.psum_scatter(whole.astype(F32), "rows", scatter_dimension=1, tiled=True)
    depth = strips // inner
    core, side, level = row_at % 2, (row_at // 2) % 2, row_at // 4
    to_core = [(i, i ^ 1) for i in range(strips)]
    to_side = [(i, i ^ 2) for i in range(strips)]
    order = [sorted(range(depth), key=lambda d: (-abs(d - z), d)) for z in range(depth)]
    place = [[order[z].index(d) for d in range(depth)] for z in range(depth)]
    order_table = jnp.array(order, jnp.int32)

    def strip_of(target, x, c):
        return (target * 2 + x) * 2 + c

    layer = []
    for turn in range(depth):
        target = order_table[level, turn]
        far = strip_product(ancestor, placed, strip_of(target, 1 - side, 1 - core), strips)
        far = lax.ppermute(far, "rows", to_core)
        near = strip_product(ancestor, placed, strip_of(target, side, 1 - core), strips)
        near = lax.ppermute(near, "rows", to_core)
        far = strip_product(ancestor, placed, strip_of(target, 1 - side, core), strips, far)
        far = lax.ppermute(far, "rows", to_side)
        layer.append(
            strip_product(ancestor, placed, strip_of(target, side, core), strips, near, far)
        )

    def own_part(step, way):
        gap = depth - 1 - step
        chosen = None
        for z in range(depth):
            target = z + way * gap
            if 0 <= target < depth:
                value = layer[place[z][target]]
                chosen = value if chosen is None else jnp.where(level == z, value, chosen)
        return chosen

    arrived = {1: None, -1: None}
    for step in range(depth - 1):
        gap = depth - 1 - step
        for way in (1, -1):
            senders = [z for z in range(depth) if 0 <= z + way * gap < depth]
            pairs = [
                (z * inner + i, (z + way) * inner + i) for z in senders for i in range(inner)
            ]
            value = own_part(step, way)
            if arrived[way] is not None:
                value = add_pair(value, arrived[way])
            arrived[way] = lax.ppermute(value, "rows", pairs)
    total = layer[-1].astype(F32)
    for way in (1, -1):
        if arrived[way] is not None:
            total = total + arrived[way].astype(F32)
    return total


def body_general(
    ancestor,
    panel_below,
    panel_beside,
    inverse_lower,
    inverse_upper,
    list_below,
    list_beside,
    second_below,
    second_beside,
    linked_below,
    linked_beside,
    second_lower,
    second_upper,
    blocks_below,
    blocks_beside,
):
    row_at = lax.axis_index("rows")
    col_at = lax.axis_index("cols")
    cols = lax.axis_size("cols")
    tile_rows, tile_cols = ancestor.shape
    width = inverse_lower.shape[0]
    half = width // cols

    beside = gather_pair((panel_beside, inverse_upper), (second_beside, second_upper), mm_rows)
    below = gather_pair((panel_below, inverse_lower), (second_below, second_lower), mm)
    link_below = mm(linked_below, second_lower).astype(BF16)
    link_beside = mm_rows(linked_beside, second_upper).astype(BF16)

    placed = place_panels(
        beside, link_beside, list_beside, blocks_beside,
        row_at * tile_rows, tile_rows,
    )
    upper = upper_sums(ancestor, placed)
    new_upper = upper[:width].T.astype(BF16)
    next_upper = upper[width:].T.astype(BF16)

    depth = below.shape[0] // 2
    linked = mm(below[:depth], link_below).astype(BF16)
    lower_total = None
    sums_total = None
    for shift in reversed(range(cols)):
        part = (col_at + shift) % cols
        piece = lower_partial(
            ancestor, below, linked, list_below, blocks_below,
            col_at * (tile_cols // BLK), part, cols,
        )
        sums = jnp.concatenate(
            [mm(placed[:width], piece), mm(placed[width:], piece[:, half:])], axis=1
        )
        if shift:
            pairs = [(i, (i + shift) % cols) for i in range(cols)]
            piece = lax.ppermute(piece, "cols", pairs)
            sums = lax.ppermute(sums, "cols", pairs)
        piece = piece.astype(F32)
        lower_total = piece if lower_total is None else lower_total + piece
        sums_total = sums if sums_total is None else sums_total + sums
    new_lower = lower_total[:, :half].astype(BF16)
    next_lower = lower_total[:, half:].astype(BF16)

    sums = lax.psum(sums_total, "rows")

    def own(matrix):
        return lax.dynamic_slice_in_dim(matrix, col_at * half, half, 1)

    base = mm(inverse_upper, inverse_lower).astype(BF16)
    base_link = mm(base, own(link_below))
    new_diagonal = (mm(inverse_upper, own(inverse_lower)) + sums[:, :half]).astype(BF16)
    link_part = (sums[:, half : 2 * half] - base_link).astype(BF16)
    next_link = lax.all_gather(link_part, "cols", axis=1, tiled=True)
    next_diagonal = (
        mm(second_upper, own(second_lower))
        + mm_first(link_beside, base_link.astype(BF16))
        + sums[:, 2 * half :]
    ).astype(BF16)
    return (new_lower, new_upper, new_diagonal, next_lower, next_upper, next_link, next_diagonal)


SLOTS = 4
ANY = pl.BlockSpec(memory_space=pl.ANY)
SCALARS = pl.BlockSpec(memory_space=pltpu.SMEM)


def swapped(value, axis, bit):
    size = lax.axis_size(axis)
    return lax.ppermute(value, axis, [(i, i ^ bit) for i in range(size)])


def from_levels(value, shift):
    size = lax.axis_size("rows")
    return lax.ppermute(value, "rows", [(i, (i + 4 * shift) % size) for i in range(size)])


class Seat:
    def __init__(self):
        row_at = lax.axis_index("rows")
        self.row = row_at
        self.core, self.side, self.level = row_at % 2, (row_at // 2) % 2, row_at // 4
        self.depth = lax.axis_size("rows") // 4
        self.col = lax.axis_index("cols")


def plan_body(block_count, row, l1, l2, local, meta, b1, m1, b2, m2, at1, at2):
    listed = l1.shape[0]
    tiles = at1.shape[0] // block_count
    own = row[0]

    @pl.loop(0, at1.shape[0])
    def _(i):
        at1[i] = 0
        at2[i] = 0

    @pl.loop(0, listed)
    def _(k):
        at1[l1[k]] = k + 1
        at2[l2[k]] = k + 1

    @pl.loop(0, b1.shape[0])
    def _(s):
        b1[s] = 0
        m1[s] = 0
        b2[s] = 0
        m2[s] = 0

    def scan(tile, put):
        def step(b, rank):
            g = tile * block_count + b
            here = jnp.where(at1[g] + at2[g] > 0, 1, 0)
            put(rank, b, g, here)
            return rank + here

        return lax.fori_loop(0, block_count, step, jnp.int32(0))

    def place(slot, g):
        b1[slot] = 2 * jnp.maximum(at1[g] - 1, 0)
        m1[slot] = jnp.where(at1[g] > 0, 1, 0)
        b2[slot] = 2 * (listed + jnp.maximum(at2[g] - 1, 0))
        m2[slot] = jnp.where(at2[g] > 0, 1, 0)

    def put_own(rank, b, g, here):
        local[rank] = b
        place(SLOTS + rank, g)

    def put_facing(rank, b, g, here):
        @pl.when(jnp.logical_and(here > 0, rank < SLOTS))
        def _():
            place(rank, g)

    def nothing(rank, b, g, here):
        return None

    @pl.loop(0, block_count)
    def _(s):
        local[s] = 0

    meta[0] = scan(own, put_own)
    meta[1] = scan(own ^ 1, nothing)
    facing = scan(own ^ 2, put_facing)

    def put_beyond(rank, b, g, here):
        slot = facing + rank - SLOTS

        @pl.when(jnp.logical_and(here > 0, jnp.logical_and(rank >= SLOTS, slot < SLOTS)))
        def _():
            place(slot, g)

    scan(own ^ 3, put_beyond)

    def most(chip, found):
        count = scan(2 * chip, nothing) + scan(2 * chip + 1, nothing)
        return jnp.maximum(found, count)

    meta[2] = lax.fori_loop(0, tiles // 2, most, jnp.int32(0))


def plan_slots(row, list1, list2, block_count, tiles):
    def numbers(count):
        return jax.ShapeDtypeStruct((count,), jnp.int32)

    slots = SLOTS + block_count
    return pl.pallas_call(
        functools.partial(plan_body, block_count),
        out_shape=(numbers(block_count), numbers(3)) + (numbers(slots),) * 4,
        in_specs=[SCALARS] * 3,
        out_specs=(SCALARS,) * 6,
        scratch_shapes=[pltpu.SMEM((tiles * block_count,), jnp.int32)] * 2,
        name="plan_slots",
    )(jnp.reshape(row, (1,)).astype(jnp.int32), list1, list2)


def place_slots_body(b1, m1, b2, m2, u1_ref, u2_ref, link_ref, *refs):
    out_ref = refs[-1]
    at = pl.program_id(0)
    width = u1_ref.shape[1]
    used = m1[at] + m2[at] > 0

    @pl.when(used)
    def _():
        keep1 = m1[at].astype(F32)
        keep2 = m2[at].astype(F32)
        u1 = u1_ref[...]
        linked = mm(u1, link_ref[...])
        out_ref[:width, :] = (-u1.astype(F32) * keep1).T.astype(BF16)
        out_ref[width:, :] = (linked * keep1 - u2_ref[...].astype(F32) * keep2).T.astype(BF16)

    @pl.when(jnp.logical_not(used))
    def _():
        out_ref[...] = jnp.zeros_like(out_ref)


def place_slots(gathered, link, tables, first):
    width = gathered.shape[1]
    count = tables[0].shape[0]
    return pl.pallas_call(
        place_slots_body,
        out_shape=jax.ShapeDtypeStruct((2 * width, count * BLK), BF16),
        grid_spec=pltpu.PrefetchScalarGridSpec(
            num_scalar_prefetch=4,
            grid=(count,),
            in_specs=[
                pl.BlockSpec((BLK, width), lambda s, p1, i1, p2, i2: (p1[s], 0)),
                pl.BlockSpec((BLK, width), lambda s, p1, i1, p2, i2: (p2[s], 0)),
                pl.BlockSpec((width, width), lambda s, p1, i1, p2, i2: (0, 0)),
            ]
            + [ANY] * len(first),
            out_specs=pl.BlockSpec((2 * width, BLK), lambda s, p1, i1, p2, i2: (0, s)),
        ),
        compiler_params=pltpu.CompilerParams(vmem_limit_bytes=24 * 2**20),
        cost_estimate=pl.CostEstimate(
            flops=2 * count * BLK * width * width // 4,
            bytes_accessed=4 * count * BLK * width,
            transcendentals=0,
        ),
        name="place_slots",
    )(*tables, gathered, gathered, link, *first)


def pack_body(local, pair, a_ref, *refs):
    refs[-1][...] = a_ref[...]


def pack(ancestor, local, pair, pairs, first):
    wide = ancestor.shape[1] // pairs
    return pl.pallas_call(
        pack_body,
        out_shape=jax.ShapeDtypeStruct((SLOTS * BLK, wide), BF16),
        grid_spec=pltpu.PrefetchScalarGridSpec(
            num_scalar_prefetch=2,
            grid=(SLOTS,),
            in_specs=[pl.BlockSpec((BLK, wide), lambda s, l, p: (l[SLOTS + s], p[0]))]
            + [ANY] * len(first),
            out_specs=pl.BlockSpec((BLK, wide), lambda s, l, p: (s, 0)),
        ),
        cost_estimate=pl.CostEstimate(
            flops=0, bytes_accessed=4 * SLOTS * BLK * wide, transcendentals=0
        ),
        name="pack_slots",
    )(local, jnp.reshape(pair, (1,)).astype(jnp.int32), ancestor, *first)


def merge_body(local, meta, pair, a_ref, got_ref, *refs):
    mine = pl.program_id(0) < meta[0]
    out_ref = refs[-1]

    @pl.when(mine)
    def _():
        out_ref[...] = a_ref[...]

    @pl.when(jnp.logical_not(mine))
    def _():
        out_ref[...] = got_ref[...]


def merge(ancestor, got, local, meta, pair, pairs, first):
    wide = ancestor.shape[1] // pairs
    return pl.pallas_call(
        merge_body,
        out_shape=jax.ShapeDtypeStruct((SLOTS * BLK, wide), BF16),
        grid_spec=pltpu.PrefetchScalarGridSpec(
            num_scalar_prefetch=3,
            grid=(SLOTS,),
            in_specs=[
                pl.BlockSpec((BLK, wide), lambda s, l, n, p: (l[s], p[0])),
                pl.BlockSpec(
                    (BLK, wide), lambda s, l, n, p: (jnp.clip(s - n[0], 0, SLOTS - 1), 0)
                ),
            ]
            + [ANY] * len(first),
            out_specs=pl.BlockSpec((BLK, wide), lambda s, l, n, p: (s, 0)),
        ),
        cost_estimate=pl.CostEstimate(
            flops=0, bytes_accessed=4 * SLOTS * BLK * wide, transcendentals=0
        ),
        name="merge_slots",
    )(local, meta, jnp.reshape(pair, (1,)).astype(jnp.int32), ancestor, got, *first)


def lower_slots_body(listed, block_count, l1, l2, at, *refs):
    tiles1, tiles2 = refs[:listed], refs[listed : 2 * listed]
    own1_ref, whole1_ref, own2_ref, link_ref = refs[2 * listed : 2 * listed + 4]
    out_ref, linked_ref = refs[-2:]
    half = link_ref.shape[1]
    depth = listed * BLK

    @pl.when(pl.program_id(0) == 0)
    def _():
        whole = whole1_ref[...].reshape(depth, whole1_ref.shape[2])
        linked_ref[...] = mm(whole, link_ref[...]).astype(BF16)

    def picked(tiles, blocks):
        kept = []
        for k in range(listed):
            place = blocks[k] - at[0]
            inside = jnp.logical_and(place >= 0, place < block_count)
            kept.append(tiles[k][...] * jnp.where(inside, 1.0, 0.0).astype(BF16))
        return jnp.concatenate(kept, axis=1)

    picked1 = picked(tiles1, l1)
    out_ref[:, :half] = (-mm(picked1, own1_ref[...].reshape(depth, half))).astype(BF16)
    second = mm(picked1, linked_ref[...])
    second = second - mm(picked(tiles2, l2), own2_ref[...].reshape(depth, half))
    out_ref[:, half:] = second.astype(BF16)


def lower_slots(ancestor, gathered, link, list1, list2, first_block, part, first):
    rows, columns = ancestor.shape
    listed, width = list1.shape[0], link.shape[0]
    half = width // 2
    block_count = columns // BLK
    tile = largest_tile(rows, 512)
    shaped = gathered.reshape(2 * listed, 2, BLK, width)
    at = jnp.stack([first_block, part]).astype(jnp.int32)

    def column(which, k):
        def index(i, l1, l2, at):
            return i, jnp.clip((l1, l2)[which][k] - at[0], 0, block_count - 1)

        return pl.BlockSpec((tile, BLK), index)

    specs = [column(which, k) for which in (0, 1) for k in range(listed)]
    specs += [
        pl.BlockSpec((listed, None, BLK, half), lambda i, l1, l2, at: (0, 1, 0, at[1])),
        pl.BlockSpec((listed, None, BLK, width), lambda i, l1, l2, at: (0, 1, 0, 0)),
        pl.BlockSpec((listed, None, BLK, half), lambda i, l1, l2, at: (1, 1, 0, at[1])),
        pl.BlockSpec((width, half), lambda i, l1, l2, at: (0, at[1])),
    ]
    return pl.pallas_call(
        functools.partial(lower_slots_body, listed, block_count),
        out_shape=jax.ShapeDtypeStruct((rows, 2 * half), BF16),
        grid_spec=pltpu.PrefetchScalarGridSpec(
            num_scalar_prefetch=3,
            grid=(rows // tile,),
            in_specs=specs + [ANY] * len(first),
            out_specs=pl.BlockSpec((tile, 2 * half), lambda i, l1, l2, at: (i, 0)),
            scratch_shapes=[pltpu.VMEM((listed * BLK, half), BF16)],
        ),
        compiler_params=pltpu.CompilerParams(vmem_limit_bytes=48 * 2**20),
        cost_estimate=pl.CostEstimate(
            flops=6 * rows * listed * BLK * half,
            bytes_accessed=4 * rows * listed * BLK + 8 * listed * BLK * width,
            transcendentals=0,
        ),
        name="lower_slots",
    )(
        list1, list2, at, *([ancestor] * (2 * listed)), shaped, shaped, shaped, link, *first
    )


def slots_body(units, adds, local, count, at, *refs):
    w_refs, arrived_ref = refs[: units - 1], refs[units - 1]
    tiles = refs[units : units + (units - 1) * SLOTS]
    added = refs[units + (units - 1) * SLOTS :][:adds]
    out_ref = refs[-1]

    def store(more):
        first = [arrived_ref[...]] + [ref[...] for ref in tiles[:SLOTS]]
        total = mm(w_refs[0][...], jnp.concatenate(first, axis=0))
        for unit in more:
            group = tiles[(unit - 1) * SLOTS : unit * SLOTS]
            own = jnp.concatenate([ref[...] for ref in group], axis=0)
            total = total + mm(w_refs[unit - 1][...], own)
        for ref in added:
            total = total + ref[...].astype(F32)
        out_ref[...] = total.astype(BF16)

    @pl.when(count[0] <= SLOTS)
    def _():
        store(())

    @pl.when(count[0] > SLOTS)
    def _():
        store(range(2, units))


def slots_product(
    ancestor, placed, arrived, local, count, strip, within, strips, added, first
):
    columns = ancestor.shape[1]
    strip_width = columns // strips
    height = placed.shape[0]
    tile = largest_tile(strip_width, 384)
    per = strip_width // tile
    unit_width = SLOTS * BLK
    units = placed.shape[1] // unit_width
    where_at = jnp.stack([strip * per, within * per]).astype(jnp.int32)

    def own_block(slot):
        if slot < SLOTS:
            return lambda j, l, n, p: (l[slot], p[0] + j)
        return lambda j, l, n, p: (l[slot], jnp.where(n[0] > SLOTS, p[0] + j, 0))

    def unit_block(unit):
        return lambda j, l, n, p: (0, jnp.where(n[0] > SLOTS, unit, 0))

    own_slots = (units - 1) * SLOTS
    return pl.pallas_call(
        functools.partial(slots_body, units, len(added)),
        out_shape=jax.ShapeDtypeStruct((height, strip_width), BF16),
        grid_spec=pltpu.PrefetchScalarGridSpec(
            num_scalar_prefetch=3,
            grid=(per,),
            in_specs=[pl.BlockSpec((height, 2 * unit_width), lambda j, l, n, p: (0, 0))]
            + [pl.BlockSpec((height, unit_width), unit_block(u)) for u in range(2, units)]
            + [pl.BlockSpec((unit_width, tile), lambda j, l, n, p: (0, p[1] + j))]
            + [pl.BlockSpec((BLK, tile), own_block(slot)) for slot in range(own_slots)]
            + [pl.BlockSpec((height, tile), lambda j, l, n, p: (0, j))] * len(added)
            + [ANY] * len(first),
            out_specs=pl.BlockSpec((height, tile), lambda j, l, n, p: (0, j)),
        ),
        compiler_params=pltpu.CompilerParams(vmem_limit_bytes=40 * 2**20),
        cost_estimate=pl.CostEstimate(
            flops=4 * height * unit_width * strip_width,
            bytes_accessed=4 * unit_width * (height + strip_width)
            + 2 * (1 + len(added)) * height * strip_width,
            transcendentals=0,
        ),
        name="slots_product",
    )(
        local, jnp.reshape(count, (1,)), where_at, *([placed] * (units - 1)), arrived,
        *([ancestor] * own_slots), *added, *first,
    )


def small_sums_body(local, count, w_ref, x_ref, *refs):
    out_ref, total_ref = refs[-2:]
    at = pl.program_id(0)
    width = w_ref.shape[0] // 2
    half = x_ref.shape[1] // 2

    @pl.when(at == 0)
    def _():
        total_ref[...] = jnp.zeros_like(total_ref)

    @pl.when(at < count[0])
    def _():
        total_ref[:, : 2 * half] += mm(w_ref[:width, :], x_ref[...])
        total_ref[:, 2 * half :] += mm(w_ref[width:, :], x_ref[:, half:])

    @pl.when(at == pl.num_programs(0) - 1)
    def _():
        out_ref[...] = total_ref[...].astype(BF16)


def small_sums(placed, piece, local, count, first):
    width = placed.shape[0] // 2
    half = piece.shape[1] // 2
    slots = local.shape[0]
    return pl.pallas_call(
        small_sums_body,
        out_shape=jax.ShapeDtypeStruct((width, 3 * half), BF16),
        grid_spec=pltpu.PrefetchScalarGridSpec(
            num_scalar_prefetch=2,
            grid=(slots,),
            in_specs=[
                pl.BlockSpec((2 * width, BLK), lambda s, l, n: (0, SLOTS + s)),
                pl.BlockSpec((BLK, 2 * half), lambda s, l, n: (l[s], 0)),
            ]
            + [ANY] * len(first),
            out_specs=pl.BlockSpec((width, 3 * half), lambda s, l, n: (0, 0)),
            scratch_shapes=[pltpu.VMEM((width, 3 * half), F32)],
        ),
        compiler_params=pltpu.CompilerParams(vmem_limit_bytes=24 * 2**20),
        cost_estimate=pl.CostEstimate(
            flops=2 * SLOTS * BLK * width * 3 * half,
            bytes_accessed=4 * slots * BLK * width,
            transcendentals=0,
        ),
        name="small_sums",
    )(local, jnp.reshape(count, (1,)), placed, piece, *first)


def step_body(options, which, *refs):
    choices, arrived = refs[:options], refs[options : options + 2]
    outs = refs[-2:]
    for way in (0, 1):
        for option in range(options):

            @pl.when(which[way] == option)
            def _():
                total = choices[option][...].astype(F32) + arrived[way][...].astype(F32)
                outs[way][...] = total.astype(BF16)


def level_step(choices, which, arrived, first):
    height, wide = choices[0].shape
    tile = height // 4
    block = (tile, wide)

    def choice(option):
        def index(i, w):
            return jnp.where(jnp.logical_or(w[0] == option, w[1] == option), i, 0), 0

        return pl.BlockSpec(block, index)

    def whole(i, w):
        return i, 0

    shape = jax.ShapeDtypeStruct((height, wide), BF16)
    return pl.pallas_call(
        functools.partial(step_body, len(choices)),
        out_shape=(shape, shape),
        grid_spec=pltpu.PrefetchScalarGridSpec(
            num_scalar_prefetch=1,
            grid=(height // tile,),
            in_specs=[choice(option) for option in range(len(choices))]
            + [pl.BlockSpec(block, whole)] * 2
            + [ANY] * len(first),
            out_specs=(pl.BlockSpec(block, whole),) * 2,
        ),
        compiler_params=pltpu.CompilerParams(vmem_limit_bytes=40 * 2**20),
        cost_estimate=pl.CostEstimate(
            flops=2 * height * wide, bytes_accessed=12 * height * wide, transcendentals=0
        ),
        name="level_step",
    )(which, *choices, *arrived, *first)


def last_body(own_ref, up_ref, down_ref, *refs):
    first_ref, second_ref = refs[-2:]
    width = first_ref.shape[1]
    total = own_ref[...].astype(F32) + up_ref[...].astype(F32) + down_ref[...].astype(F32)
    first_ref[...] = total[:width].T.astype(BF16)
    second_ref[...] = total[width:].T.astype(BF16)


def last_sum(own, up, down, first):
    height, wide = own.shape
    tile = largest_tile(wide, 256)
    width = height // 2
    shape = jax.ShapeDtypeStruct((wide, width), BF16)
    return pl.pallas_call(
        last_body,
        out_shape=(shape, shape),
        grid=(wide // tile,),
        in_specs=[pl.BlockSpec((height, tile), lambda j: (0, j))] * 3 + [ANY] * len(first),
        out_specs=(pl.BlockSpec((tile, width), lambda j: (j, 0)),) * 2,
        compiler_params=pltpu.CompilerParams(vmem_limit_bytes=40 * 2**20),
        cost_estimate=pl.CostEstimate(
            flops=2 * height * wide, bytes_accessed=8 * height * wide, transcendentals=0
        ),
        name="last_sum",
    )(own, up, down, *first)


def split_body(parts, at, left_ref, right_ref, *refs):
    outs = refs[-parts:]
    size = outs[0].shape[0]
    for shift in range(parts):
        start = pl.multiple_of(lax.rem(at[0] + shift, parts) * size, 16)
        rows = pl.ds(start, size)
        total = left_ref[rows, :].astype(F32) + right_ref[rows, :].astype(F32)
        outs[shift][...] = total.astype(BF16)


def split_sum(left, right, at, parts, first):
    rows, wide = left.shape
    shape = jax.ShapeDtypeStruct((rows // parts, wide), BF16)
    vmem = pl.BlockSpec(memory_space=pltpu.VMEM)
    return pl.pallas_call(
        functools.partial(split_body, parts),
        out_shape=(shape,) * parts,
        in_specs=[SCALARS, vmem, vmem] + [ANY] * len(first),
        out_specs=(vmem,) * parts,
        compiler_params=pltpu.CompilerParams(vmem_limit_bytes=24 * 2**20),
        cost_estimate=pl.CostEstimate(
            flops=rows * wide, bytes_accessed=6 * rows * wide, transcendentals=0
        ),
        name="split_sum",
    )(jnp.reshape(at, (1,)).astype(jnp.int32), left, right, *first)


def total_of(base, pieces, first):
    vmem = pl.BlockSpec(memory_space=pltpu.VMEM)
    count = len(pieces)

    def kernel(base_ref, *refs):
        total = base_ref[...]
        for ref in refs[:count]:
            total = total + ref[...].astype(F32)
        refs[-1][...] = total.astype(BF16)

    return pl.pallas_call(
        kernel,
        out_shape=jax.ShapeDtypeStruct(base.shape, BF16),
        in_specs=[vmem] * (1 + count) + [ANY] * len(first),
        out_specs=vmem,
        name="total_of",
    )(base, *pieces, *first)


def left_over(seat, ancestor, gathered, link, lists, places, dropped):
    block_rows, columns = ancestor.shape
    first_row = seat.row * block_rows
    shaped = gathered.reshape(-1, BLK, gathered.shape[1])
    u1, u2 = (
        rows_onto(
            jnp.take(shaped, place, axis=0).reshape(-1, gathered.shape[1]),
            blocks, first_row, block_rows,
        )
        for blocks, place in zip(lists, places)
    )
    joined = jnp.concatenate([-u1.astype(F32), mm(u1, link) - u2.astype(F32)], axis=1)
    joined = jnp.where(jnp.repeat(dropped, BLK)[:, None], joined, 0.0).astype(BF16)
    strip_width = columns // (4 * seat.depth)
    side = (jnp.arange(columns, dtype=jnp.int32) // strip_width // 2) % 2
    partial = jnp.where((side != seat.side)[None, :], mm_first(joined, ancestor), 0.0)
    return lax.psum_scatter(partial, "rows", scatter_dimension=1, tiled=True)


def gather_small(seat, mine):
    levels = [mine] + [from_levels(mine, shift) for shift in range(1, seat.depth)]
    value = jnp.concatenate(
        [
            lax.select_n((seat.level - z) % seat.depth, *levels)
            if seat.depth > 2
            else jnp.where(seat.level == z, levels[0], levels[-1])
            for z in range(seat.depth)
        ]
    )
    for bit, at in ((2, seat.side), (1, seat.core)):
        other = swapped(value, "rows", bit)
        value = jnp.concatenate(
            [jnp.where(at == 0, value, other), jnp.where(at == 0, other, value)]
        )
    return value


def body_by_slots(
    ancestor,
    panel_below,
    panel_beside,
    inverse_lower,
    inverse_upper,
    list_below,
    list_beside,
    second_below,
    second_beside,
    linked_below,
    linked_beside,
    second_lower,
    second_upper,
    blocks_below,
    blocks_beside,
):
    seat = Seat()
    tile_rows, tile_cols = ancestor.shape
    block_count = tile_rows // BLK
    width = inverse_lower.shape[0]
    half = width // 2
    listed = list_below.shape[0]
    depth = seat.depth
    rows = 4 * depth
    pairs = 2 * depth
    at_first = seat.col == 0

    def either(first, second):
        return jnp.where(at_first, first, second)

    beside = mm_rows(either(panel_beside, second_beside), either(inverse_upper, second_upper))
    below = mm(either(panel_below, second_below), either(inverse_lower, second_lower))
    gathered = lax.all_gather(
        jnp.concatenate([beside, below]).astype(BF16), ("cols", "rows"), axis=0, tiled=True
    )
    link_below = mm(linked_below, second_lower).astype(BF16)
    link_beside = mm_rows(linked_beside, second_upper).astype(BF16)

    local, meta, *tables = plan_slots(
        seat.row, list_beside, blocks_beside, block_count, rows
    )
    count = meta[0]
    order = [sorted(range(depth), key=lambda d: (-abs(d - z), d)) for z in range(depth)]
    place = [[order[z].index(d) for d in range(depth)] for z in range(depth)]
    order_table = jnp.array(order, jnp.int32)
    targets = [order_table[seat.level, turn] for turn in range(depth)]

    def own(matrix):
        return lax.dynamic_slice_in_dim(matrix, seat.col * half, half, 1)

    base = mm(inverse_upper, inverse_lower).astype(BF16)
    base_link = mm(base, own(link_below))
    added = jnp.concatenate(
        [
            mm(inverse_upper, own(inverse_lower)),
            -base_link,
            mm(second_upper, own(second_lower)) + mm_first(link_beside, base_link.astype(BF16)),
        ],
        axis=1,
    )
    size = width // rows
    added = lax.dynamic_slice_in_dim(
        added, (seat.core * 2 + seat.side) * (width // 4) + seat.level * size, size, 0
    )

    def leaving_pair(turn):
        return targets[turn] * 2 + 1 - seat.side

    leaving, arrived, passed = [], [], []
    packed = pack(ancestor, local, leaving_pair(0), pairs, [])
    for turn in range(depth):
        passed.append(swapped(packed, "rows", 1))
        if turn + 1 < depth:
            packed = pack(ancestor, local, leaving_pair(turn + 1), pairs, leaving[-1:])
        leaving.append(
            merge(ancestor, passed[turn], local, meta, leaving_pair(turn), pairs, [packed])
        )
        arrived.append(swapped(leaving[-1], "rows", 2))

    placed = place_slots(gathered, link_beside, tables, leaving[-1:])

    def lower(shift, first):
        return lower_slots(
            ancestor, gathered, link_below, list_below, blocks_below,
            seat.col * (tile_cols // BLK), seat.col ^ shift, first,
        )

    def strip(turn, part, added, first):
        pair = targets[turn] * 2 + seat.side
        return slots_product(
            ancestor, placed, arrived[turn], local, count, pair * 2 + part, part, rows,
            added, first,
        )

    def far_strip(turn, first):
        return strip(turn, 1 - seat.core, [], first)

    def near_strip(turn, far, first):
        return strip(turn, seat.core, [swapped(far, "rows", 1)], first)

    def moved(values, step):
        gap = depth - 1 - step
        out = []
        for way, value in zip((1, -1), values):
            senders = [z for z in range(depth) if 0 <= z + way * gap < depth]
            out.append(
                lax.ppermute(
                    value, "rows",
                    [(z * 4 + i, (z + way) * 4 + i) for z in senders for i in range(4)],
                )
            )
        return out

    def next_step(step, layer, moving, first):
        gap = depth - 1 - step
        which = [
            [place[z][z + way * gap] if 0 <= z + way * gap < depth else 0 for z in range(depth)]
            for way in (1, -1)
        ]
        options = 1 + max(max(each) for each in which)
        which = jnp.array(which, jnp.int32)[:, seat.level]
        return level_step(layer[:options], which, moving, first)

    fars = [far_strip(0, [])]
    fars.append(far_strip(1, fars[-1:]))
    layer = [near_strip(0, fars[0], fars[-1:])]
    moving = moved([layer[0]] * 2, 0)
    given = lower(1, layer[-1:])
    layer.append(near_strip(1, fars[1], [given]))
    given_sums = small_sums(placed, given, local, count, layer[-1:])
    got_sums = swapped(given_sums, "cols", 1)
    last = [given_sums]
    for turn in range(2, depth):
        fars.append(far_strip(turn, last))
        if turn == 2:
            layer.append(near_strip(turn, fars[turn], []))
            stepped = next_step(1, layer, moving, layer[-1:])
            moving = moved(stepped, 1)
            kept = lower(0, stepped[:1])
            kept_sums = small_sums(placed, kept, local, count, [])
            sums = split_sum(kept_sums, got_sums, seat.core, 2, [])
            last = [sums[0]]
    sums = split_sum(
        sums[0], swapped(sums[1], "rows", 1), seat.side, 2, fars[-1:]
    )
    for turn in range(3, depth):
        layer.append(near_strip(turn, fars[turn], [sums[0]] + layer[3:]))
    sums = split_sum(sums[0], swapped(sums[1], "rows", 2), seat.level, depth, layer[-1:])
    for step in range(2, depth - 1):
        if step == 2:
            pieces = [sums[0]] + [
                from_levels(sums[shift], shift) for shift in range(1, depth)
            ]
            mine = total_of(added, pieces, moving)
        stepped = next_step(step, layer, moving, [mine])
        moving = moved(stepped, step)
    whole = gather_small(seat, mine)

    piece = kept.astype(F32) + swapped(given, "cols", 1).astype(F32)
    new_lower = piece[:, :half].astype(BF16)
    next_lower = piece[:, half:].astype(BF16)
    link_part = whole[:, half : 2 * half]
    link_other = swapped(link_part, "cols", 1)
    next_link = jnp.concatenate(
        [either(link_part, link_other), either(link_other, link_part)], axis=1
    )

    def with_rest(own, up, down):
        own_at = jnp.arange(block_count, dtype=jnp.int32)
        slot_dropped = jnp.logical_and(
            own_at < count, own_at >= 2 * SLOTS - jnp.minimum(meta[1], SLOTS)
        )
        dropped = jnp.any(
            jnp.logical_and(slot_dropped[:, None], local[:, None] == own_at[None, :]), axis=0
        )
        at = 2 * jnp.arange(listed, dtype=jnp.int32)
        total = own.astype(F32) + up.astype(F32) + down.astype(F32)
        total = total + left_over(
            seat, ancestor, gathered, link_beside, (list_beside, blocks_beside),
            (at, at + 2 * listed), dropped,
        )
        return total[:width].T.astype(BF16), total[width:].T.astype(BF16)

    def without_rest(own, up, down):
        return last_sum(own, up, down, [next_link, new_lower])

    new_upper, next_upper = lax.cond(
        meta[2] > 2 * SLOTS, with_rest, without_rest, layer[-1], *moving
    )
    return (
        new_lower, new_upper, whole[:, :half], next_lower, next_upper, next_link,
        whole[:, 2 * half :],
    )


def body(*arrays):
    ancestor, panel, list_beside = arrays[0], arrays[1], arrays[6]
    rows, cols = lax.axis_size("rows"), lax.axis_size("cols")
    by_slots = (
        cols == 2
        and rows % 4 == 0
        and rows >= 16
        and panel.shape[0] == BLK
        and list_beside.shape[0] == rows
        and ancestor.shape[0] % BLK == 0
        and ancestor.shape[0] // BLK >= 2 * SLOTS
        and ancestor.shape[0] // BLK % SLOTS == 0
        and ancestor.shape[1] % (rows * BLK) == 0
        and panel.shape[1] % (2 * rows) == 0
    )
    return (body_by_slots if by_slots else body_general)(*arrays)


def solution(mesh):
    return jax.shard_map(
        body,
        mesh=mesh,
        in_specs=(
            P("rows", "cols"),
            P("rows", None),
            P("rows", None),
            P(),
            P(),
            P(),
            P(),
            P("rows", None),
            P("rows", None),
            P(),
            P(),
            P(),
            P(),
            P(),
            P(),
        ),
        out_specs=(
            P("rows", "cols"),
            P(("cols", "rows"), None),
            P(None, "cols"),
            P("rows", "cols"),
            P(("cols", "rows"), None),
            P(),
            P(None, "cols"),
        ),
        check_vma=False,
    )
```

```python
import functools

import jax
import jax.numpy as jnp
from jax import lax
from jax.experimental import pallas as pl
from jax.experimental.pallas import tpu as pltpu
from jax.sharding import PartitionSpec as P

BLK = 128
F32 = jnp.float32
BF16 = jnp.bfloat16


def mm(left, right):
    return jnp.dot(left, right, preferred_element_type=F32)


def mm_rows(left, right):
    return lax.dot_general(left, right, (((1,), (1,)), ((), ())), preferred_element_type=F32)


def mm_first(left, right):
    return lax.dot_general(left, right, (((0,), (0,)), ((), ())), preferred_element_type=F32)


def largest_tile(size, limit):
    tile = min(limit, size)
    while size % tile:
        tile -= BLK
    return tile


def gather_pair(first, second, product):
    cols = lax.axis_size("cols")
    if cols == 2:
        at_first = lax.axis_index("cols") == 0
        mine = product(
            jnp.where(at_first, first[0], second[0]), jnp.where(at_first, first[1], second[1])
        ).astype(BF16)
        return lax.all_gather(mine, ("cols", "rows"), axis=0, tiled=True)
    return jnp.concatenate(
        [
            lax.all_gather(product(*each).astype(BF16), "rows", axis=0, tiled=True)
            for each in (first, second)
        ]
    )


def place_body(pos1, in1, pos2, in2, u1_ref, u2_ref, link_ref, out_ref):
    at = pl.program_id(0)
    width = u1_ref.shape[1]
    keep1 = in1[at].astype(F32)
    keep2 = in2[at].astype(F32)
    u1 = u1_ref[...]
    linked = mm(u1, link_ref[...])
    out_ref[:width, :] = (-u1.astype(F32) * keep1).T.astype(BF16)
    out_ref[width:, :] = (linked * keep1 - u2_ref[...].astype(F32) * keep2).T.astype(BF16)


def blocks_in_tile(blocks, first_block, block_count):
    ids = first_block + jnp.arange(block_count, dtype=jnp.int32)
    matches = ids[:, None] == blocks[None, :]
    places = jnp.sum(
        jnp.where(matches, jnp.arange(blocks.shape[0], dtype=jnp.int32)[None, :], 0), axis=1
    )
    return places.astype(jnp.int32), jnp.any(matches, axis=1).astype(jnp.int32)


def rows_onto(panel, blocks, first_row, row_count):
    global_rows = first_row + jnp.arange(row_count, dtype=jnp.int32)
    matches = (global_rows // BLK)[:, None] == blocks[None, :]
    places = jnp.sum(
        jnp.where(matches, jnp.arange(blocks.shape[0], dtype=jnp.int32)[None, :], 0), axis=1
    )
    picked = jnp.take(panel, places * BLK + global_rows % BLK, axis=0)
    return jnp.where(jnp.any(matches, axis=1)[:, None], picked, jnp.zeros_like(picked))


def place_panels(both, link, list1, list2, first_row, row_count):
    width = both.shape[1]
    listed = list1.shape[0]
    if row_count % BLK:
        u1 = rows_onto(both[: listed * BLK], list1, first_row, row_count)
        u2 = rows_onto(both[listed * BLK :], list2, first_row, row_count)
        joined = jnp.concatenate([-u1.astype(F32), mm(u1, link) - u2.astype(F32)], axis=1)
        return joined.T.astype(BF16)
    first_block = first_row // BLK
    block_count = row_count // BLK
    pos1, in1 = blocks_in_tile(list1, first_block, block_count)
    pos2, in2 = blocks_in_tile(list2, first_block, block_count)
    return pl.pallas_call(
        place_body,
        out_shape=jax.ShapeDtypeStruct((2 * width, block_count * BLK), BF16),
        grid_spec=pltpu.PrefetchScalarGridSpec(
            num_scalar_prefetch=4,
            grid=(block_count,),
            in_specs=[
                pl.BlockSpec((BLK, width), lambda b, p1, i1, p2, i2: (p1[b], 0)),
                pl.BlockSpec((BLK, width), lambda b, p1, i1, p2, i2: (listed + p2[b], 0)),
                pl.BlockSpec((width, width), lambda b, p1, i1, p2, i2: (0, 0)),
            ],
            out_specs=pl.BlockSpec((2 * width, BLK), lambda b, p1, i1, p2, i2: (0, b)),
        ),
        compiler_params=pltpu.CompilerParams(vmem_limit_bytes=24 * 2**20),
        cost_estimate=pl.CostEstimate(
            flops=2 * block_count * BLK * width * width,
            bytes_accessed=8 * block_count * BLK * width,
            transcendentals=0,
        ),
        name="place_panels",
    )(pos1, in1, pos2, in2, both, both, link)


def lower_body(listed, loc1, in1, loc2, in2, part, *refs):
    tiles1, tiles2 = refs[:listed], refs[listed : 2 * listed]
    l1_ref, v1_ref, l2_ref, out_ref = refs[2 * listed :]
    half = l1_ref.shape[1]
    picked1 = jnp.concatenate(
        [tiles1[k][...] * in1[k].astype(F32).astype(BF16) for k in range(listed)], axis=1
    )
    picked2 = jnp.concatenate(
        [tiles2[k][...] * in2[k].astype(F32).astype(BF16) for k in range(listed)], axis=1
    )
    out_ref[:, :half] = (-mm(picked1, l1_ref[...])).astype(BF16)
    out_ref[:, half:] = (mm(picked1, v1_ref[...]) - mm(picked2, l2_ref[...])).astype(BF16)


def lower_partial(ancestor, both, linked, list1, list2, first_block, part, parts):
    rows, columns = ancestor.shape
    width = both.shape[1]
    half = width // parts
    listed = list1.shape[0]
    depth = listed * BLK
    block_count = columns // BLK
    tile = largest_tile(rows, 512)

    def local(blocks):
        at = blocks - first_block
        inside = jnp.logical_and(at >= 0, at < block_count)
        return jnp.clip(at, 0, block_count - 1), inside.astype(jnp.int32)

    loc1, in1 = local(list1)
    loc2, in2 = local(list2)
    specs = [
        pl.BlockSpec((tile, BLK), functools.partial(lambda k, i, l1, i1, l2, i2, p: (i, l1[k]), k))
        for k in range(listed)
    ] + [
        pl.BlockSpec((tile, BLK), functools.partial(lambda k, i, l1, i1, l2, i2, p: (i, l2[k]), k))
        for k in range(listed)
    ]
    specs += [
        pl.BlockSpec((depth, half), lambda i, l1, i1, l2, i2, p: (0, p[0])),
        pl.BlockSpec((depth, half), lambda i, l1, i1, l2, i2, p: (0, p[0])),
        pl.BlockSpec((depth, half), lambda i, l1, i1, l2, i2, p: (1, p[0])),
    ]
    return pl.pallas_call(
        functools.partial(lower_body, listed),
        out_shape=jax.ShapeDtypeStruct((rows, 2 * half), BF16),
        grid_spec=pltpu.PrefetchScalarGridSpec(
            num_scalar_prefetch=5,
            grid=(rows // tile,),
            in_specs=specs,
            out_specs=pl.BlockSpec((tile, 2 * half), lambda i, l1, i1, l2, i2, p: (i, 0)),
        ),
        compiler_params=pltpu.CompilerParams(vmem_limit_bytes=40 * 2**20),
        cost_estimate=pl.CostEstimate(
            flops=6 * rows * depth * half,
            bytes_accessed=4 * rows * depth + 6 * depth * half,
            transcendentals=0,
        ),
        name="lower_partial",
    )(
        loc1, in1, loc2, in2, jnp.reshape(part, (1,)).astype(jnp.int32),
        *([ancestor] * (2 * listed)), both, linked, both,
    )


def strip_body(strip, w_ref, a_ref, *refs):
    total = mm(w_ref[...], a_ref[...])
    for ref in refs[:-1]:
        total = total + ref[...].astype(F32)
    refs[-1][...] = total.astype(BF16)


def strip_product(ancestor, placed, strip, strips, *added):
    rows, columns = ancestor.shape
    strip_width = columns // strips
    height = placed.shape[0]
    if strip_width % BLK:
        total = mm(
            placed, lax.dynamic_slice_in_dim(ancestor, strip * strip_width, strip_width, 1)
        )
        for each in added:
            total = total + each.astype(F32)
        return total.astype(BF16)
    tile = largest_tile(strip_width, 256)
    per = strip_width // tile
    return pl.pallas_call(
        strip_body,
        out_shape=jax.ShapeDtypeStruct((height, strip_width), BF16),
        grid_spec=pltpu.PrefetchScalarGridSpec(
            num_scalar_prefetch=1,
            grid=(per,),
            in_specs=[
                pl.BlockSpec((height, rows), lambda j, s: (0, 0)),
                pl.BlockSpec((rows, tile), lambda j, s: (0, s[0] * per + j)),
            ]
            + [pl.BlockSpec((height, tile), lambda j, s: (0, j))] * len(added),
            out_specs=pl.BlockSpec((height, tile), lambda j, s: (0, j)),
        ),
        compiler_params=pltpu.CompilerParams(vmem_limit_bytes=40 * 2**20),
        cost_estimate=pl.CostEstimate(
            flops=2 * height * rows * strip_width,
            bytes_accessed=2 * (rows * strip_width + height * rows)
            + 2 * (1 + len(added)) * height * strip_width,
            transcendentals=0,
        ),
        name="strip_product",
    )(jnp.reshape(strip, (1,)).astype(jnp.int32), placed, ancestor, *added)


def add_pair(left, right):
    return (left.astype(F32) + right.astype(F32)).astype(BF16)


def upper_sums(ancestor, placed):
    strips = lax.axis_size("rows")
    row_at = lax.axis_index("rows")
    inner = 4 if strips % 4 == 0 else 1
    if inner == 1:
        whole = strip_product(ancestor, placed, 0, 1)
        return lax.psum_scatter(whole.astype(F32), "rows", scatter_dimension=1, tiled=True)
    depth = strips // inner
    core, side, level = row_at % 2, (row_at // 2) % 2, row_at // 4
    to_core = [(i, i ^ 1) for i in range(strips)]
    to_side = [(i, i ^ 2) for i in range(strips)]
    order = [sorted(range(depth), key=lambda d: (-abs(d - z), d)) for z in range(depth)]
    place = [[order[z].index(d) for d in range(depth)] for z in range(depth)]
    order_table = jnp.array(order, jnp.int32)

    def strip_of(target, x, c):
        return (target * 2 + x) * 2 + c

    layer = []
    for turn in range(depth):
        target = order_table[level, turn]
        far = strip_product(ancestor, placed, strip_of(target, 1 - side, 1 - core), strips)
        far = lax.ppermute(far, "rows", to_core)
        near = strip_product(ancestor, placed, strip_of(target, side, 1 - core), strips)
        near = lax.ppermute(near, "rows", to_core)
        far = strip_product(ancestor, placed, strip_of(target, 1 - side, core), strips, far)
        far = lax.ppermute(far, "rows", to_side)
        layer.append(
            strip_product(ancestor, placed, strip_of(target, side, core), strips, near, far)
        )

    def own_part(step, way):
        gap = depth - 1 - step
        chosen = None
        for z in range(depth):
            target = z + way * gap
            if 0 <= target < depth:
                value = layer[place[z][target]]
                chosen = value if chosen is None else jnp.where(level == z, value, chosen)
        return chosen

    arrived = {1: None, -1: None}
    for step in range(depth - 1):
        gap = depth - 1 - step
        for way in (1, -1):
            senders = [z for z in range(depth) if 0 <= z + way * gap < depth]
            pairs = [
                (z * inner + i, (z + way) * inner + i) for z in senders for i in range(inner)
            ]
            value = own_part(step, way)
            if arrived[way] is not None:
                value = add_pair(value, arrived[way])
            arrived[way] = lax.ppermute(value, "rows", pairs)
    total = layer[-1].astype(F32)
    for way in (1, -1):
        if arrived[way] is not None:
            total = total + arrived[way].astype(F32)
    return total


def body_general(
    ancestor,
    panel_below,
    panel_beside,
    inverse_lower,
    inverse_upper,
    list_below,
    list_beside,
    second_below,
    second_beside,
    linked_below,
    linked_beside,
    second_lower,
    second_upper,
    blocks_below,
    blocks_beside,
):
    row_at = lax.axis_index("rows")
    col_at = lax.axis_index("cols")
    cols = lax.axis_size("cols")
    tile_rows, tile_cols = ancestor.shape
    width = inverse_lower.shape[0]
    half = width // cols

    beside = gather_pair((panel_beside, inverse_upper), (second_beside, second_upper), mm_rows)
    below = gather_pair((panel_below, inverse_lower), (second_below, second_lower), mm)
    link_below = mm(linked_below, second_lower).astype(BF16)
    link_beside = mm_rows(linked_beside, second_upper).astype(BF16)

    placed = place_panels(
        beside, link_beside, list_beside, blocks_beside,
        row_at * tile_rows, tile_rows,
    )
    upper = upper_sums(ancestor, placed)
    new_upper = upper[:width].T.astype(BF16)
    next_upper = upper[width:].T.astype(BF16)

    depth = below.shape[0] // 2
    linked = mm(below[:depth], link_below).astype(BF16)
    lower_total = None
    sums_total = None
    for shift in reversed(range(cols)):
        part = (col_at + shift) % cols
        piece = lower_partial(
            ancestor, below, linked, list_below, blocks_below,
            col_at * (tile_cols // BLK), part, cols,
        )
        sums = jnp.concatenate(
            [mm(placed[:width], piece), mm(placed[width:], piece[:, half:])], axis=1
        )
        if shift:
            pairs = [(i, (i + shift) % cols) for i in range(cols)]
            piece = lax.ppermute(piece, "cols", pairs)
            sums = lax.ppermute(sums, "cols", pairs)
        piece = piece.astype(F32)
        lower_total = piece if lower_total is None else lower_total + piece
        sums_total = sums if sums_total is None else sums_total + sums
    new_lower = lower_total[:, :half].astype(BF16)
    next_lower = lower_total[:, half:].astype(BF16)

    sums = lax.psum(sums_total, "rows")

    def own(matrix):
        return lax.dynamic_slice_in_dim(matrix, col_at * half, half, 1)

    base = mm(inverse_upper, inverse_lower).astype(BF16)
    base_link = mm(base, own(link_below))
    new_diagonal = (mm(inverse_upper, own(inverse_lower)) + sums[:, :half]).astype(BF16)
    link_part = (sums[:, half : 2 * half] - base_link).astype(BF16)
    next_link = lax.all_gather(link_part, "cols", axis=1, tiled=True)
    next_diagonal = (
        mm(second_upper, own(second_lower))
        + mm_first(link_beside, base_link.astype(BF16))
        + sums[:, 2 * half :]
    ).astype(BF16)
    return (new_lower, new_upper, new_diagonal, next_lower, next_upper, next_link, next_diagonal)


SLOTS = 4
FREE = pl.CostEstimate(flops=0, bytes_accessed=0, transcendentals=0)
ANY = pl.BlockSpec(memory_space=pl.ANY)
SCALARS = pl.BlockSpec(memory_space=pltpu.SMEM)


def swapped(value, axis, bit):
    size = lax.axis_size(axis)
    return lax.ppermute(value, axis, [(i, i ^ bit) for i in range(size)])


def from_levels(value, shift):
    size = lax.axis_size("rows")
    return lax.ppermute(value, "rows", [(i, (i + 4 * shift) % size) for i in range(size)])


class Seat:
    def __init__(self):
        row_at = lax.axis_index("rows")
        self.row = row_at
        self.core, self.side, self.level = row_at % 2, (row_at // 2) % 2, row_at // 4
        self.depth = lax.axis_size("rows") // 4
        self.col = lax.axis_index("cols")


def spread(item, depth):
    pair = jnp.concatenate([item, swapped(item, "rows", 2)])
    near = [pair] + [from_levels(pair, shift) for shift in range(1, depth)]
    beyond = [swapped(each, "cols", 1) for each in near]
    return (
        near + [swapped(each, "rows", 1) for each in near]
        + beyond + [swapped(each, "rows", 1) for each in beyond]
    )


def spread_place(seat, listed, which):
    at = jnp.arange(listed, dtype=jnp.int32)
    core, side, level = at % 2, (at // 2) % 2, at // 4
    apart = (seat.col ^ which) * 2 + (seat.core ^ core)
    return (apart * seat.depth + (seat.level - level) % seat.depth) * 2 + (seat.side ^ side)


def plan_body(block_count, row, l1, l2, local, meta, b1, m1, b2, m2, at1, at2):
    listed = l1.shape[0]
    tiles = at1.shape[0] // block_count
    depth = listed // 4
    own, column = row[0], row[1]

    def place_of(k, which):
        apart = (own >> 2) - (k >> 2)
        apart = jnp.where(apart < 0, apart + depth, apart)
        half = (column ^ which) * 2 + ((own ^ k) & 1)
        return (half * depth + apart) * 2 + (((own ^ k) >> 1) & 1)

    @pl.loop(0, at1.shape[0])
    def _(i):
        at1[i] = 0
        at2[i] = 0

    @pl.loop(0, listed)
    def _(k):
        at1[l1[k]] = k + 1
        at2[l2[k]] = k + 1

    @pl.loop(0, b1.shape[0])
    def _(s):
        b1[s] = 0
        m1[s] = 0
        b2[s] = 0
        m2[s] = 0

    def scan(tile, put):
        def step(b, rank):
            g = tile * block_count + b
            here = jnp.where(at1[g] + at2[g] > 0, 1, 0)
            put(rank, b, g, here)
            return rank + here

        return lax.fori_loop(0, block_count, step, jnp.int32(0))

    def place(slot, g):
        b1[slot] = place_of(jnp.maximum(at1[g] - 1, 0), 0)
        m1[slot] = jnp.where(at1[g] > 0, 1, 0)
        b2[slot] = place_of(jnp.maximum(at2[g] - 1, 0), 1)
        m2[slot] = jnp.where(at2[g] > 0, 1, 0)

    def put_own(rank, b, g, here):
        local[rank] = b
        place(SLOTS + rank, g)

    def put_facing(rank, b, g, here):
        @pl.when(jnp.logical_and(here > 0, rank < SLOTS))
        def _():
            place(rank, g)

    def nothing(rank, b, g, here):
        return None

    @pl.loop(0, block_count)
    def _(s):
        local[s] = 0

    meta[0] = scan(own, put_own)
    meta[1] = scan(own ^ 1, nothing)
    facing = scan(own ^ 2, put_facing)

    def put_beyond(rank, b, g, here):
        slot = facing + rank - SLOTS

        @pl.when(jnp.logical_and(here > 0, jnp.logical_and(rank >= SLOTS, slot < SLOTS)))
        def _():
            place(slot, g)

    scan(own ^ 3, put_beyond)

    def most(chip, found):
        count = scan(2 * chip, nothing) + scan(2 * chip + 1, nothing)
        return jnp.maximum(found, count)

    meta[2] = lax.fori_loop(0, tiles // 2, most, jnp.int32(0))


def plan_slots(row, column, list1, list2, block_count, tiles):
    def numbers(count):
        return jax.ShapeDtypeStruct((count,), jnp.int32)

    slots = SLOTS + block_count
    return pl.pallas_call(
        functools.partial(plan_body, block_count),
        out_shape=(numbers(block_count), numbers(3)) + (numbers(slots),) * 4,
        in_specs=[SCALARS] * 3,
        out_specs=(SCALARS,) * 6,
        scratch_shapes=[pltpu.SMEM((tiles * block_count,), jnp.int32)] * 2,
        name="plan_slots",
    )(jnp.stack([row, column]).astype(jnp.int32), list1, list2)


def place_slots_body(count, b1, m1, b2, m2, link_ref, *refs):
    pieces = refs[:count]
    out_ref, got, sems = refs[-3:]
    width = link_ref.shape[0]
    slots = b1.shape[0]

    def copies(s, act):
        for which, (block, used) in enumerate(((b1, m1), (b2, m2))):
            for at in range(count):

                @pl.when(jnp.logical_and(used[s] > 0, block[s] >> 1 == at))
                def _():
                    row = pl.multiple_of((block[s] & 1) * BLK, BLK)
                    copy = pltpu.make_async_copy(
                        pieces[at].at[pl.ds(row, BLK), :], got.at[which, s], sems.at[which, s]
                    )
                    getattr(copy, act)()

    @pl.loop(0, slots)
    def _(s):
        copies(s, "start")

    for s in range(slots):
        columns = pl.ds(s * BLK, BLK)
        used = m1[s] + m2[s] > 0

        @pl.when(used)
        def _():
            copies(s, "wait")
            u1 = jnp.where(m1[s] > 0, got[0, s].astype(F32), 0.0)
            u2 = jnp.where(m2[s] > 0, got[1, s].astype(F32), 0.0)
            linked = mm(u1.astype(BF16), link_ref[...])
            out_ref[:width, columns] = (-u1).T.astype(BF16)
            out_ref[width:, columns] = (linked - u2).T.astype(BF16)

        @pl.when(jnp.logical_not(used))
        def _():
            out_ref[:, columns] = jnp.zeros((2 * width, BLK), BF16)


def place_slots(pieces, link, tables):
    width = link.shape[0]
    slots = tables[0].shape[0]
    vmem = pl.BlockSpec(memory_space=pltpu.VMEM)
    return pl.pallas_call(
        functools.partial(place_slots_body, len(pieces)),
        out_shape=jax.ShapeDtypeStruct((2 * width, slots * BLK), BF16),
        in_specs=[SCALARS] * 4 + [vmem] + [ANY] * len(pieces),
        out_specs=vmem,
        scratch_shapes=[
            pltpu.VMEM((2, slots, BLK, width), BF16),
            pltpu.SemaphoreType.DMA((2, slots)),
        ],
        compiler_params=pltpu.CompilerParams(vmem_limit_bytes=56 * 2**20),
        cost_estimate=FREE,
        name="place_slots",
    )(*tables, link, *pieces)


def pack_body(local, pair, a_ref, *refs):
    refs[-1][...] = a_ref[...]


def pack(ancestor, local, pair, pairs, first):
    wide = ancestor.shape[1] // pairs
    return pl.pallas_call(
        pack_body,
        out_shape=jax.ShapeDtypeStruct((SLOTS * BLK, wide), BF16),
        grid_spec=pltpu.PrefetchScalarGridSpec(
            num_scalar_prefetch=2,
            grid=(SLOTS,),
            in_specs=[pl.BlockSpec((BLK, wide), lambda s, l, p: (l[SLOTS + s], p[0]))]
            + [ANY] * len(first),
            out_specs=pl.BlockSpec((BLK, wide), lambda s, l, p: (s, 0)),
        ),
        cost_estimate=FREE,
        name="pack_slots",
    )(local, jnp.reshape(pair, (1,)).astype(jnp.int32), ancestor, *first)


def merge_body(local, meta, pair, a_ref, got_ref, *refs):
    mine = pl.program_id(0) < meta[0]
    out_ref = refs[-1]

    @pl.when(mine)
    def _():
        out_ref[...] = a_ref[...]

    @pl.when(jnp.logical_not(mine))
    def _():
        out_ref[...] = got_ref[...]


def merge(ancestor, got, local, meta, pair, pairs, first):
    wide = ancestor.shape[1] // pairs
    return pl.pallas_call(
        merge_body,
        out_shape=jax.ShapeDtypeStruct((SLOTS * BLK, wide), BF16),
        grid_spec=pltpu.PrefetchScalarGridSpec(
            num_scalar_prefetch=3,
            grid=(SLOTS,),
            in_specs=[
                pl.BlockSpec((BLK, wide), lambda s, l, n, p: (l[s], p[0])),
                pl.BlockSpec(
                    (BLK, wide), lambda s, l, n, p: (jnp.clip(s - n[0], 0, SLOTS - 1), 0)
                ),
            ]
            + [ANY] * len(first),
            out_specs=pl.BlockSpec((BLK, wide), lambda s, l, n, p: (s, 0)),
        ),
        cost_estimate=FREE,
        name="merge_slots",
    )(local, meta, jnp.reshape(pair, (1,)).astype(jnp.int32), ancestor, got, *first)


def lower_slots_body(listed, block_count, l1, l2, at, *refs):
    tiles1, tiles2 = refs[:listed], refs[listed : 2 * listed]
    own1_ref, whole1_ref, own2_ref, link_ref = refs[2 * listed : 2 * listed + 4]
    out_ref, linked_ref = refs[-2:]
    half = link_ref.shape[1]
    depth = listed * BLK

    @pl.when(pl.program_id(0) == 0)
    def _():
        whole = whole1_ref[...].reshape(depth, whole1_ref.shape[2])
        linked_ref[...] = mm(whole, link_ref[...]).astype(BF16)

    def picked(tiles, blocks):
        kept = []
        for k in range(listed):
            place = blocks[k] - at[0]
            inside = jnp.logical_and(place >= 0, place < block_count)
            kept.append(tiles[k][...] * jnp.where(inside, 1.0, 0.0).astype(BF16))
        return jnp.concatenate(kept, axis=1)

    picked1 = picked(tiles1, l1)
    out_ref[:, :half] = (-mm(picked1, own1_ref[...].reshape(depth, half))).astype(BF16)
    second = mm(picked1, linked_ref[...])
    second = second - mm(picked(tiles2, l2), own2_ref[...].reshape(depth, half))
    out_ref[:, half:] = second.astype(BF16)


def lower_slots(ancestor, gathered, link, list1, list2, first_block, part, first):
    rows, columns = ancestor.shape
    listed, width = list1.shape[0], link.shape[0]
    half = width // 2
    block_count = columns // BLK
    tile = largest_tile(rows, 512)
    shaped = gathered.reshape(2 * listed, BLK, width)
    at = jnp.stack([first_block, part]).astype(jnp.int32)

    def column(which, k):
        def index(i, l1, l2, at):
            return i, jnp.clip((l1, l2)[which][k] - at[0], 0, block_count - 1)

        return pl.BlockSpec((tile, BLK), index)

    specs = [column(which, k) for which in (0, 1) for k in range(listed)]
    specs += [
        pl.BlockSpec((listed, BLK, half), lambda i, l1, l2, at: (0, 0, at[1])),
        pl.BlockSpec((listed, BLK, width), lambda i, l1, l2, at: (0, 0, 0)),
        pl.BlockSpec((listed, BLK, half), lambda i, l1, l2, at: (1, 0, at[1])),
        pl.BlockSpec((width, half), lambda i, l1, l2, at: (0, at[1])),
    ]
    return pl.pallas_call(
        functools.partial(lower_slots_body, listed, block_count),
        out_shape=jax.ShapeDtypeStruct((rows, 2 * half), BF16),
        grid_spec=pltpu.PrefetchScalarGridSpec(
            num_scalar_prefetch=3,
            grid=(rows // tile,),
            in_specs=specs + [ANY] * len(first),
            out_specs=pl.BlockSpec((tile, 2 * half), lambda i, l1, l2, at: (i, 0)),
            scratch_shapes=[pltpu.VMEM((listed * BLK, half), BF16)],
        ),
        compiler_params=pltpu.CompilerParams(vmem_limit_bytes=56 * 2**20),
        cost_estimate=FREE,
        name="lower_slots",
    )(
        list1, list2, at, *([ancestor] * (2 * listed)), shaped, shaped, shaped, link, *first
    )


def slots_body(adds, local, count, at, w_ref, arrived_ref, *refs):
    tiles = refs[:SLOTS]
    added = refs[SLOTS : SLOTS + adds]
    placed_ref, ancestor_ref = refs[SLOTS + adds : SLOTS + adds + 2]
    out_ref, rest_w, rest_a, sems = refs[-4:]
    first = [arrived_ref[...]] + [ref[...] for ref in tiles]
    total = mm(w_ref[...], jnp.concatenate(first, axis=0))
    for ref in added:
        total = total + ref[...].astype(F32)
    out_ref[...] = total.astype(BF16)

    @pl.when(count[0] > SLOTS)
    def _():
        tile = out_ref.shape[1]
        more = rest_a.shape[0] // BLK
        column = pl.multiple_of((at[0] + pl.program_id(0)) * tile, BLK)
        copies = [
            pltpu.make_async_copy(
                placed_ref.at[:, pl.ds(2 * SLOTS * BLK, more * BLK)], rest_w, sems.at[more]
            )
        ]
        for s in range(more):
            row = pl.multiple_of(local[SLOTS + s] * BLK, BLK)
            copies.append(
                pltpu.make_async_copy(
                    ancestor_ref.at[pl.ds(row, BLK), pl.ds(column, tile)],
                    rest_a.at[pl.ds(s * BLK, BLK), :],
                    sems.at[s],
                )
            )
        for copy in copies:
            copy.start()
        for copy in copies:
            copy.wait()
        again = mm(w_ref[...], jnp.concatenate(first, axis=0))
        again = again + mm(rest_w[...], rest_a[...])
        for ref in added:
            again = again + ref[...].astype(F32)
        out_ref[...] = again.astype(BF16)


def slots_product(
    ancestor, placed, arrived, local, count, strip, within, strips, added, first
):
    columns = ancestor.shape[1]
    strip_width = columns // strips
    height = placed.shape[0]
    tile = largest_tile(strip_width, 384)
    per = strip_width // tile
    more = placed.shape[1] // BLK - 2 * SLOTS
    where_at = jnp.stack([strip * per, within * per]).astype(jnp.int32)

    def own_block(slot):
        return lambda j, l, n, p: (l[slot], p[0] + j)

    return pl.pallas_call(
        functools.partial(slots_body, len(added)),
        out_shape=jax.ShapeDtypeStruct((height, strip_width), BF16),
        grid_spec=pltpu.PrefetchScalarGridSpec(
            num_scalar_prefetch=3,
            grid=(per,),
            in_specs=[pl.BlockSpec((height, 2 * SLOTS * BLK), lambda j, l, n, p: (0, 0))]
            + [pl.BlockSpec((SLOTS * BLK, tile), lambda j, l, n, p: (0, p[1] + j))]
            + [pl.BlockSpec((BLK, tile), own_block(slot)) for slot in range(SLOTS)]
            + [pl.BlockSpec((height, tile), lambda j, l, n, p: (0, j))] * len(added)
            + [ANY] * (2 + len(first)),
            out_specs=pl.BlockSpec((height, tile), lambda j, l, n, p: (0, j)),
            scratch_shapes=[
                pltpu.VMEM((height, more * BLK), BF16),
                pltpu.VMEM((more * BLK, tile), BF16),
                pltpu.SemaphoreType.DMA((more + 1,)),
            ],
        ),
        compiler_params=pltpu.CompilerParams(vmem_limit_bytes=56 * 2**20),
        cost_estimate=FREE,
        name="slots_product",
    )(
        local, jnp.reshape(count, (1,)), where_at, placed, arrived, *([ancestor] * SLOTS),
        *added, placed, ancestor, *first,
    )


def small_sums_body(local, count, w_ref, x_ref, *refs):
    out_ref, total_ref = refs[-2:]
    at = pl.program_id(0)
    width = w_ref.shape[0] // 2
    half = x_ref.shape[1] // 2

    @pl.when(at == 0)
    def _():
        total_ref[...] = jnp.zeros_like(total_ref)

    @pl.when(at < count[0])
    def _():
        total_ref[:, : 2 * half] += mm(w_ref[:width, :], x_ref[...])
        total_ref[:, 2 * half :] += mm(w_ref[width:, :], x_ref[:, half:])

    @pl.when(at == pl.num_programs(0) - 1)
    def _():
        out_ref[...] = total_ref[...].astype(BF16)


def small_sums(placed, piece, local, count, first):
    width = placed.shape[0] // 2
    half = piece.shape[1] // 2
    slots = local.shape[0]
    return pl.pallas_call(
        small_sums_body,
        out_shape=jax.ShapeDtypeStruct((width, 3 * half), BF16),
        grid_spec=pltpu.PrefetchScalarGridSpec(
            num_scalar_prefetch=2,
            grid=(slots,),
            in_specs=[
                pl.BlockSpec((2 * width, BLK), lambda s, l, n: (0, SLOTS + s)),
                pl.BlockSpec((BLK, 2 * half), lambda s, l, n: (l[s], 0)),
            ]
            + [ANY] * len(first),
            out_specs=pl.BlockSpec((width, 3 * half), lambda s, l, n: (0, 0)),
            scratch_shapes=[pltpu.VMEM((width, 3 * half), F32)],
        ),
        compiler_params=pltpu.CompilerParams(vmem_limit_bytes=56 * 2**20),
        cost_estimate=FREE,
        name="small_sums",
    )(local, jnp.reshape(count, (1,)), placed, piece, *first)


def step_body(options, which, *refs):
    choices, arrived = refs[:options], refs[options : options + 2]
    outs = refs[-2:]
    for way in (0, 1):
        for option in range(options):

            @pl.when(which[way] == option)
            def _():
                total = choices[option][...].astype(F32) + arrived[way][...].astype(F32)
                outs[way][...] = total.astype(BF16)


def level_step(choices, which, arrived, first):
    height, wide = choices[0].shape
    tile = height // 4
    block = (tile, wide)

    def choice(option):
        def index(i, w):
            return jnp.where(jnp.logical_or(w[0] == option, w[1] == option), i, 0), 0

        return pl.BlockSpec(block, index)

    def whole(i, w):
        return i, 0

    shape = jax.ShapeDtypeStruct((height, wide), BF16)
    return pl.pallas_call(
        functools.partial(step_body, len(choices)),
        out_shape=(shape, shape),
        grid_spec=pltpu.PrefetchScalarGridSpec(
            num_scalar_prefetch=1,
            grid=(height // tile,),
            in_specs=[choice(option) for option in range(len(choices))]
            + [pl.BlockSpec(block, whole)] * 2
            + [ANY] * len(first),
            out_specs=(pl.BlockSpec(block, whole),) * 2,
        ),
        compiler_params=pltpu.CompilerParams(vmem_limit_bytes=56 * 2**20),
        cost_estimate=FREE,
        name="level_step",
    )(which, *choices, *arrived, *first)


def last_body(own_ref, up_ref, down_ref, *refs):
    first_ref, second_ref = refs[-2:]
    width = first_ref.shape[1]
    total = own_ref[...].astype(F32) + up_ref[...].astype(F32) + down_ref[...].astype(F32)
    first_ref[...] = total[:width].T.astype(BF16)
    second_ref[...] = total[width:].T.astype(BF16)


def last_sum(own, up, down, first):
    height, wide = own.shape
    tile = largest_tile(wide, 256)
    width = height // 2
    shape = jax.ShapeDtypeStruct((wide, width), BF16)
    return pl.pallas_call(
        last_body,
        out_shape=(shape, shape),
        grid=(wide // tile,),
        in_specs=[pl.BlockSpec((height, tile), lambda j: (0, j))] * 3 + [ANY] * len(first),
        out_specs=(pl.BlockSpec((tile, width), lambda j: (j, 0)),) * 2,
        compiler_params=pltpu.CompilerParams(vmem_limit_bytes=56 * 2**20),
        cost_estimate=FREE,
        name="last_sum",
    )(own, up, down, *first)


def split_body(parts, at, left_ref, right_ref, *refs):
    outs = refs[-parts:]
    size = outs[0].shape[0]
    for shift in range(parts):
        start = pl.multiple_of(lax.rem(at[0] + shift, parts) * size, 16)
        rows = pl.ds(start, size)
        total = left_ref[rows, :].astype(F32) + right_ref[rows, :].astype(F32)
        outs[shift][...] = total.astype(BF16)


def split_sum(left, right, at, parts, first):
    rows, wide = left.shape
    shape = jax.ShapeDtypeStruct((rows // parts, wide), BF16)
    vmem = pl.BlockSpec(memory_space=pltpu.VMEM)
    return pl.pallas_call(
        functools.partial(split_body, parts),
        out_shape=(shape,) * parts,
        in_specs=[SCALARS, vmem, vmem] + [ANY] * len(first),
        out_specs=(vmem,) * parts,
        compiler_params=pltpu.CompilerParams(vmem_limit_bytes=56 * 2**20),
        cost_estimate=FREE,
        name="split_sum",
    )(jnp.reshape(at, (1,)).astype(jnp.int32), left, right, *first)


def total_of(base, pieces, first):
    vmem = pl.BlockSpec(memory_space=pltpu.VMEM)
    count = len(pieces)

    def kernel(base_ref, *refs):
        total = base_ref[...]
        for ref in refs[:count]:
            total = total + ref[...].astype(F32)
        refs[-1][...] = total.astype(BF16)

    return pl.pallas_call(
        kernel,
        out_shape=jax.ShapeDtypeStruct(base.shape, BF16),
        in_specs=[vmem] * (1 + count) + [ANY] * len(first),
        out_specs=vmem,
        name="total_of",
    )(base, *pieces, *first)


def left_over(seat, ancestor, pieces, link, lists, places, dropped):
    block_rows, columns = ancestor.shape
    width = link.shape[0]
    first_row = seat.row * block_rows
    shaped = jnp.concatenate(pieces).reshape(-1, BLK, width)
    u1, u2 = (
        rows_onto(
            jnp.take(shaped, place, axis=0).reshape(-1, width), blocks, first_row, block_rows
        )
        for blocks, place in zip(lists, places)
    )
    joined = jnp.concatenate([-u1.astype(F32), mm(u1, link) - u2.astype(F32)], axis=1)
    joined = jnp.where(jnp.repeat(dropped, BLK)[:, None], joined, 0.0).astype(BF16)
    wide = columns // (2 * seat.depth)
    partial = jnp.concatenate(
        [
            mm_first(
                joined,
                lax.dynamic_slice_in_dim(
                    ancestor, (2 * level + 1 - seat.side) * wide, wide, 1
                ),
            ).astype(BF16)
            for level in range(seat.depth)
        ],
        axis=1,
    )
    groups = [
        [4 * level + 2 * side + core for level in range(seat.depth) for core in range(2)]
        for side in range(2)
    ]
    own = lax.psum_scatter(
        partial, "rows", scatter_dimension=1, axis_index_groups=groups, tiled=True
    )
    return swapped(own, "rows", 2).astype(F32)


def gather_small(seat, mine):
    levels = [mine] + [from_levels(mine, shift) for shift in range(1, seat.depth)]
    value = jnp.concatenate(
        [
            lax.select_n((seat.level - z) % seat.depth, *levels)
            if seat.depth > 2
            else jnp.where(seat.level == z, levels[0], levels[-1])
            for z in range(seat.depth)
        ]
    )
    for bit, at in ((2, seat.side), (1, seat.core)):
        other = swapped(value, "rows", bit)
        value = jnp.concatenate(
            [jnp.where(at == 0, value, other), jnp.where(at == 0, other, value)]
        )
    return value


def body_by_slots(
    ancestor,
    panel_below,
    panel_beside,
    inverse_lower,
    inverse_upper,
    list_below,
    list_beside,
    second_below,
    second_beside,
    linked_below,
    linked_beside,
    second_lower,
    second_upper,
    blocks_below,
    blocks_beside,
):
    seat = Seat()
    tile_rows, tile_cols = ancestor.shape
    block_count = tile_rows // BLK
    width = inverse_lower.shape[0]
    half = width // 2
    listed = list_below.shape[0]
    depth = seat.depth
    rows = 4 * depth
    pairs = 2 * depth
    at_first = seat.col == 0

    def either(first, second):
        return jnp.where(at_first, first, second)

    beside = mm_rows(either(panel_beside, second_beside), either(inverse_upper, second_upper))
    item = beside.astype(BF16)
    pieces = spread(item, depth)
    below = mm(either(panel_below, second_below), either(inverse_lower, second_lower))
    gathered = lax.all_gather(below.astype(BF16), ("cols", "rows"), axis=0, tiled=True)
    link_below = mm(linked_below, second_lower).astype(BF16)
    link_beside = mm_rows(linked_beside, second_upper).astype(BF16)

    local, meta, *tables = plan_slots(
        seat.row, seat.col, list_beside, blocks_beside, block_count, rows
    )
    count = meta[0]
    order = [sorted(range(depth), key=lambda d: (-abs(d - z), d)) for z in range(depth)]
    place = [[order[z].index(d) for d in range(depth)] for z in range(depth)]
    order_table = jnp.array(order, jnp.int32)
    targets = [order_table[seat.level, turn] for turn in range(depth)]

    def own(matrix):
        return lax.dynamic_slice_in_dim(matrix, seat.col * half, half, 1)

    base = mm(inverse_upper, inverse_lower).astype(BF16)
    base_link = mm(base, own(link_below))
    added = jnp.concatenate(
        [
            mm(inverse_upper, own(inverse_lower)),
            -base_link,
            mm(second_upper, own(second_lower)) + mm_first(link_beside, base_link.astype(BF16)),
        ],
        axis=1,
    )
    size = width // rows
    added = lax.dynamic_slice_in_dim(
        added, (seat.core * 2 + seat.side) * (width // 4) + seat.level * size, size, 0
    )

    def leaving_pair(turn):
        return targets[turn] * 2 + 1 - seat.side

    passed, arrived = [], []

    def send(turn, first):
        pair = leaving_pair(turn)
        merged = merge(ancestor, passed[turn], local, meta, pair, pairs, first)
        arrived.append(swapped(merged, "rows", 2))
        return merged

    last = []
    for turn in range(depth):
        packed = pack(ancestor, local, leaving_pair(turn), pairs, last)
        passed.append(swapped(packed, "rows", 1))
        last = [pieces[0], packed]
        if turn in (1, 2):
            last = [send(turn - 1, [packed])]

    placed = place_slots(pieces, link_beside, tables)

    def lower(shift, first):
        return lower_slots(
            ancestor, gathered, link_below, list_below, blocks_below,
            seat.col * (tile_cols // BLK), seat.col ^ shift, first,
        )

    def strip(turn, part, added, first):
        pair = targets[turn] * 2 + seat.side
        return slots_product(
            ancestor, placed, arrived[turn], local, count, pair * 2 + part, part, rows,
            added, first,
        )

    def far_strip(turn, first):
        return strip(turn, 1 - seat.core, [], first)

    def near_strip(turn, far, first):
        return strip(turn, seat.core, [swapped(far, "rows", 1)], first)

    def moved(values, step):
        gap = depth - 1 - step
        out = []
        for way, value in zip((1, -1), values):
            senders = [z for z in range(depth) if 0 <= z + way * gap < depth]
            out.append(
                lax.ppermute(
                    value, "rows",
                    [(z * 4 + i, (z + way) * 4 + i) for z in senders for i in range(4)],
                )
            )
        return out

    def next_step(step, layer, moving, first):
        gap = depth - 1 - step
        which = [
            [place[z][z + way * gap] if 0 <= z + way * gap < depth else 0 for z in range(depth)]
            for way in (1, -1)
        ]
        options = 1 + max(max(each) for each in which)
        which = jnp.array(which, jnp.int32)[:, seat.level]
        return level_step(layer[:options], which, moving, first)

    far = far_strip(0, [])
    merged = send(2, [far])
    layer = [near_strip(0, far, [merged])]
    moving = moved([layer[0]] * 2, 0)
    given = lower(1, layer[-1:])
    given_sums = small_sums(placed, given, local, count, [])
    got_sums = swapped(given_sums, "cols", 1)
    far = far_strip(1, [given_sums])
    layer.append(near_strip(1, far, []))
    stepped = next_step(1, layer, moving, [])
    moving = moved(stepped, 1)
    kept = lower(0, stepped[:1])
    kept_sums = small_sums(placed, kept, local, count, [])
    sums = split_sum(kept_sums, got_sums, seat.core, 2, [])
    far = far_strip(2, sums[:1])
    sums = split_sum(sums[0], swapped(sums[1], "rows", 1), seat.side, 2, [far])
    merged = sums[0]
    for turn in range(3, depth):
        merged = send(turn, [merged])
    layer.append(near_strip(2, far, [merged]))
    sums = split_sum(sums[0], swapped(sums[1], "rows", 2), seat.level, depth, layer[-1:])
    pieces_of_sum = [sums[0]] + [
        from_levels(sums[shift], shift) for shift in range(1, depth)
    ]
    mine = total_of(added, pieces_of_sum, moving)
    for step in range(2, depth - 1):
        stepped = next_step(step, layer, moving, [mine])
        moving = moved(stepped, step)
        far = far_strip(step + 1, stepped[:1])
        layer.append(near_strip(step + 1, far, []))
    whole = gather_small(seat, mine)

    piece = kept.astype(F32) + swapped(given, "cols", 1).astype(F32)
    new_lower = piece[:, :half].astype(BF16)
    next_lower = piece[:, half:].astype(BF16)
    link_part = whole[:, half : 2 * half]
    link_other = swapped(link_part, "cols", 1)
    next_link = jnp.concatenate(
        [either(link_part, link_other), either(link_other, link_part)], axis=1
    )

    def with_rest(own, up, down):
        own_at = jnp.arange(block_count, dtype=jnp.int32)
        slot_dropped = jnp.logical_and(
            own_at < count, own_at >= 2 * SLOTS - jnp.minimum(meta[1], SLOTS)
        )
        dropped = jnp.any(
            jnp.logical_and(slot_dropped[:, None], local[:, None] == own_at[None, :]), axis=0
        )
        places = spread_place(seat, listed, 0), spread_place(seat, listed, 1)
        total = own.astype(F32) + up.astype(F32) + down.astype(F32)
        total = total + left_over(
            seat, ancestor, pieces, link_beside, (list_beside, blocks_beside), places, dropped,
        )
        return total[:width].T.astype(BF16), total[width:].T.astype(BF16)

    def without_rest(own, up, down):
        return last_sum(own, up, down, [next_link, new_lower])

    new_upper, next_upper = lax.cond(
        meta[2] > 2 * SLOTS, with_rest, without_rest, layer[-1], *moving
    )
    return (
        new_lower, new_upper, whole[:, :half], next_lower, next_upper, next_link,
        whole[:, 2 * half :],
    )


def body(*arrays):
    ancestor, panel, list_beside = arrays[0], arrays[1], arrays[6]
    rows, cols = lax.axis_size("rows"), lax.axis_size("cols")
    by_slots = (
        cols == 2
        and rows % 4 == 0
        and rows >= 16
        and panel.shape[0] == BLK
        and list_beside.shape[0] == rows
        and ancestor.shape[0] % BLK == 0
        and ancestor.shape[0] // BLK >= 2 * SLOTS
        and ancestor.shape[0] // BLK % SLOTS == 0
        and ancestor.shape[1] % (rows * BLK) == 0
        and panel.shape[1] % (2 * rows) == 0
    )
    return (body_by_slots if by_slots else body_general)(*arrays)


def solution(mesh):
    return jax.shard_map(
        body,
        mesh=mesh,
        in_specs=(
            P("rows", "cols"),
            P("rows", None),
            P("rows", None),
            P(),
            P(),
            P(),
            P(),
            P("rows", None),
            P("rows", None),
            P(),
            P(),
            P(),
            P(),
            P(),
            P(),
        ),
        out_specs=(
            P("rows", "cols"),
            P(("cols", "rows"), None),
            P(None, "cols"),
            P("rows", "cols"),
            P(("cols", "rows"), None),
            P(),
            P(None, "cols"),
        ),
        check_vma=False,
    )
```

```python
import functools

import jax
import jax.numpy as jnp
from jax import lax
from jax.experimental import pallas as pl
from jax.experimental.pallas import tpu as pltpu
from jax.sharding import PartitionSpec as P

BLK = 128
F32 = jnp.float32
BF16 = jnp.bfloat16


def mm(left, right):
    return jnp.dot(left, right, preferred_element_type=F32)


def mm_rows(left, right):
    return lax.dot_general(left, right, (((1,), (1,)), ((), ())), preferred_element_type=F32)


def mm_first(left, right):
    return lax.dot_general(left, right, (((0,), (0,)), ((), ())), preferred_element_type=F32)


def largest_tile(size, limit):
    tile = min(limit, size)
    while size % tile:
        tile -= BLK
    return tile


def gather_pair(first, second, product):
    cols = lax.axis_size("cols")
    if cols == 2:
        at_first = lax.axis_index("cols") == 0
        mine = product(
            jnp.where(at_first, first[0], second[0]), jnp.where(at_first, first[1], second[1])
        ).astype(BF16)
        return lax.all_gather(mine, ("cols", "rows"), axis=0, tiled=True)
    return jnp.concatenate(
        [
            lax.all_gather(product(*each).astype(BF16), "rows", axis=0, tiled=True)
            for each in (first, second)
        ]
    )


def place_body(pos1, in1, pos2, in2, u1_ref, u2_ref, link_ref, out_ref):
    at = pl.program_id(0)
    width = u1_ref.shape[1]
    keep1 = in1[at].astype(F32)
    keep2 = in2[at].astype(F32)
    u1 = u1_ref[...]
    linked = mm(u1, link_ref[...])
    out_ref[:width, :] = (-u1.astype(F32) * keep1).T.astype(BF16)
    out_ref[width:, :] = (linked * keep1 - u2_ref[...].astype(F32) * keep2).T.astype(BF16)


def blocks_in_tile(blocks, first_block, block_count):
    ids = first_block + jnp.arange(block_count, dtype=jnp.int32)
    matches = ids[:, None] == blocks[None, :]
    places = jnp.sum(
        jnp.where(matches, jnp.arange(blocks.shape[0], dtype=jnp.int32)[None, :], 0), axis=1
    )
    return places.astype(jnp.int32), jnp.any(matches, axis=1).astype(jnp.int32)


def rows_onto(panel, blocks, first_row, row_count):
    global_rows = first_row + jnp.arange(row_count, dtype=jnp.int32)
    matches = (global_rows // BLK)[:, None] == blocks[None, :]
    places = jnp.sum(
        jnp.where(matches, jnp.arange(blocks.shape[0], dtype=jnp.int32)[None, :], 0), axis=1
    )
    picked = jnp.take(panel, places * BLK + global_rows % BLK, axis=0)
    return jnp.where(jnp.any(matches, axis=1)[:, None], picked, jnp.zeros_like(picked))


def place_panels(both, link, list1, list2, first_row, row_count):
    width = both.shape[1]
    listed = list1.shape[0]
    if row_count % BLK:
        u1 = rows_onto(both[: listed * BLK], list1, first_row, row_count)
        u2 = rows_onto(both[listed * BLK :], list2, first_row, row_count)
        joined = jnp.concatenate([-u1.astype(F32), mm(u1, link) - u2.astype(F32)], axis=1)
        return joined.T.astype(BF16)
    first_block = first_row // BLK
    block_count = row_count // BLK
    pos1, in1 = blocks_in_tile(list1, first_block, block_count)
    pos2, in2 = blocks_in_tile(list2, first_block, block_count)
    return pl.pallas_call(
        place_body,
        out_shape=jax.ShapeDtypeStruct((2 * width, block_count * BLK), BF16),
        grid_spec=pltpu.PrefetchScalarGridSpec(
            num_scalar_prefetch=4,
            grid=(block_count,),
            in_specs=[
                pl.BlockSpec((BLK, width), lambda b, p1, i1, p2, i2: (p1[b], 0)),
                pl.BlockSpec((BLK, width), lambda b, p1, i1, p2, i2: (listed + p2[b], 0)),
                pl.BlockSpec((width, width), lambda b, p1, i1, p2, i2: (0, 0)),
            ],
            out_specs=pl.BlockSpec((2 * width, BLK), lambda b, p1, i1, p2, i2: (0, b)),
        ),
        compiler_params=pltpu.CompilerParams(vmem_limit_bytes=24 * 2**20),
        cost_estimate=pl.CostEstimate(
            flops=2 * block_count * BLK * width * width,
            bytes_accessed=8 * block_count * BLK * width,
            transcendentals=0,
        ),
        name="place_panels",
    )(pos1, in1, pos2, in2, both, both, link)


def lower_body(listed, loc1, in1, loc2, in2, part, *refs):
    tiles1, tiles2 = refs[:listed], refs[listed : 2 * listed]
    l1_ref, v1_ref, l2_ref, out_ref = refs[2 * listed :]
    half = l1_ref.shape[1]
    picked1 = jnp.concatenate(
        [tiles1[k][...] * in1[k].astype(F32).astype(BF16) for k in range(listed)], axis=1
    )
    picked2 = jnp.concatenate(
        [tiles2[k][...] * in2[k].astype(F32).astype(BF16) for k in range(listed)], axis=1
    )
    out_ref[:, :half] = (-mm(picked1, l1_ref[...])).astype(BF16)
    out_ref[:, half:] = (mm(picked1, v1_ref[...]) - mm(picked2, l2_ref[...])).astype(BF16)


def lower_partial(ancestor, both, linked, list1, list2, first_block, part, parts):
    rows, columns = ancestor.shape
    width = both.shape[1]
    half = width // parts
    listed = list1.shape[0]
    depth = listed * BLK
    block_count = columns // BLK
    tile = largest_tile(rows, 512)

    def local(blocks):
        at = blocks - first_block
        inside = jnp.logical_and(at >= 0, at < block_count)
        return jnp.clip(at, 0, block_count - 1), inside.astype(jnp.int32)

    loc1, in1 = local(list1)
    loc2, in2 = local(list2)
    specs = [
        pl.BlockSpec((tile, BLK), functools.partial(lambda k, i, l1, i1, l2, i2, p: (i, l1[k]), k))
        for k in range(listed)
    ] + [
        pl.BlockSpec((tile, BLK), functools.partial(lambda k, i, l1, i1, l2, i2, p: (i, l2[k]), k))
        for k in range(listed)
    ]
    specs += [
        pl.BlockSpec((depth, half), lambda i, l1, i1, l2, i2, p: (0, p[0])),
        pl.BlockSpec((depth, half), lambda i, l1, i1, l2, i2, p: (0, p[0])),
        pl.BlockSpec((depth, half), lambda i, l1, i1, l2, i2, p: (1, p[0])),
    ]
    return pl.pallas_call(
        functools.partial(lower_body, listed),
        out_shape=jax.ShapeDtypeStruct((rows, 2 * half), BF16),
        grid_spec=pltpu.PrefetchScalarGridSpec(
            num_scalar_prefetch=5,
            grid=(rows // tile,),
            in_specs=specs,
            out_specs=pl.BlockSpec((tile, 2 * half), lambda i, l1, i1, l2, i2, p: (i, 0)),
        ),
        compiler_params=pltpu.CompilerParams(vmem_limit_bytes=40 * 2**20),
        cost_estimate=pl.CostEstimate(
            flops=6 * rows * depth * half,
            bytes_accessed=4 * rows * depth + 6 * depth * half,
            transcendentals=0,
        ),
        name="lower_partial",
    )(
        loc1, in1, loc2, in2, jnp.reshape(part, (1,)).astype(jnp.int32),
        *([ancestor] * (2 * listed)), both, linked, both,
    )


def strip_body(strip, w_ref, a_ref, *refs):
    total = mm(w_ref[...], a_ref[...])
    for ref in refs[:-1]:
        total = total + ref[...].astype(F32)
    refs[-1][...] = total.astype(BF16)


def strip_product(ancestor, placed, strip, strips, *added):
    rows, columns = ancestor.shape
    strip_width = columns // strips
    height = placed.shape[0]
    if strip_width % BLK:
        total = mm(
            placed, lax.dynamic_slice_in_dim(ancestor, strip * strip_width, strip_width, 1)
        )
        for each in added:
            total = total + each.astype(F32)
        return total.astype(BF16)
    tile = largest_tile(strip_width, 256)
    per = strip_width // tile
    return pl.pallas_call(
        strip_body,
        out_shape=jax.ShapeDtypeStruct((height, strip_width), BF16),
        grid_spec=pltpu.PrefetchScalarGridSpec(
            num_scalar_prefetch=1,
            grid=(per,),
            in_specs=[
                pl.BlockSpec((height, rows), lambda j, s: (0, 0)),
                pl.BlockSpec((rows, tile), lambda j, s: (0, s[0] * per + j)),
            ]
            + [pl.BlockSpec((height, tile), lambda j, s: (0, j))] * len(added),
            out_specs=pl.BlockSpec((height, tile), lambda j, s: (0, j)),
        ),
        compiler_params=pltpu.CompilerParams(vmem_limit_bytes=40 * 2**20),
        cost_estimate=pl.CostEstimate(
            flops=2 * height * rows * strip_width,
            bytes_accessed=2 * (rows * strip_width + height * rows)
            + 2 * (1 + len(added)) * height * strip_width,
            transcendentals=0,
        ),
        name="strip_product",
    )(jnp.reshape(strip, (1,)).astype(jnp.int32), placed, ancestor, *added)


def add_pair(left, right):
    return (left.astype(F32) + right.astype(F32)).astype(BF16)


def upper_sums(ancestor, placed):
    strips = lax.axis_size("rows")
    row_at = lax.axis_index("rows")
    inner = 4 if strips % 4 == 0 else 1
    if inner == 1:
        whole = strip_product(ancestor, placed, 0, 1)
        return lax.psum_scatter(whole.astype(F32), "rows", scatter_dimension=1, tiled=True)
    depth = strips // inner
    core, side, level = row_at % 2, (row_at // 2) % 2, row_at // 4
    to_core = [(i, i ^ 1) for i in range(strips)]
    to_side = [(i, i ^ 2) for i in range(strips)]
    order = [sorted(range(depth), key=lambda d: (-abs(d - z), d)) for z in range(depth)]
    place = [[order[z].index(d) for d in range(depth)] for z in range(depth)]
    order_table = jnp.array(order, jnp.int32)

    def strip_of(target, x, c):
        return (target * 2 + x) * 2 + c

    layer = []
    for turn in range(depth):
        target = order_table[level, turn]
        far = strip_product(ancestor, placed, strip_of(target, 1 - side, 1 - core), strips)
        far = lax.ppermute(far, "rows", to_core)
        near = strip_product(ancestor, placed, strip_of(target, side, 1 - core), strips)
        near = lax.ppermute(near, "rows", to_core)
        far = strip_product(ancestor, placed, strip_of(target, 1 - side, core), strips, far)
        far = lax.ppermute(far, "rows", to_side)
        layer.append(
            strip_product(ancestor, placed, strip_of(target, side, core), strips, near, far)
        )

    def own_part(step, way):
        gap = depth - 1 - step
        chosen = None
        for z in range(depth):
            target = z + way * gap
            if 0 <= target < depth:
                value = layer[place[z][target]]
                chosen = value if chosen is None else jnp.where(level == z, value, chosen)
        return chosen

    arrived = {1: None, -1: None}
    for step in range(depth - 1):
        gap = depth - 1 - step
        for way in (1, -1):
            senders = [z for z in range(depth) if 0 <= z + way * gap < depth]
            pairs = [
                (z * inner + i, (z + way) * inner + i) for z in senders for i in range(inner)
            ]
            value = own_part(step, way)
            if arrived[way] is not None:
                value = add_pair(value, arrived[way])
            arrived[way] = lax.ppermute(value, "rows", pairs)
    total = layer[-1].astype(F32)
    for way in (1, -1):
        if arrived[way] is not None:
            total = total + arrived[way].astype(F32)
    return total


def body_general(
    ancestor,
    panel_below,
    panel_beside,
    inverse_lower,
    inverse_upper,
    list_below,
    list_beside,
    second_below,
    second_beside,
    linked_below,
    linked_beside,
    second_lower,
    second_upper,
    blocks_below,
    blocks_beside,
):
    row_at = lax.axis_index("rows")
    col_at = lax.axis_index("cols")
    cols = lax.axis_size("cols")
    tile_rows, tile_cols = ancestor.shape
    width = inverse_lower.shape[0]
    half = width // cols

    beside = gather_pair((panel_beside, inverse_upper), (second_beside, second_upper), mm_rows)
    below = gather_pair((panel_below, inverse_lower), (second_below, second_lower), mm)
    link_below = mm(linked_below, second_lower).astype(BF16)
    link_beside = mm_rows(linked_beside, second_upper).astype(BF16)

    placed = place_panels(
        beside, link_beside, list_beside, blocks_beside,
        row_at * tile_rows, tile_rows,
    )
    upper = upper_sums(ancestor, placed)
    new_upper = upper[:width].T.astype(BF16)
    next_upper = upper[width:].T.astype(BF16)

    depth = below.shape[0] // 2
    linked = mm(below[:depth], link_below).astype(BF16)
    lower_total = None
    sums_total = None
    for shift in reversed(range(cols)):
        part = (col_at + shift) % cols
        piece = lower_partial(
            ancestor, below, linked, list_below, blocks_below,
            col_at * (tile_cols // BLK), part, cols,
        )
        sums = jnp.concatenate(
            [mm(placed[:width], piece), mm(placed[width:], piece[:, half:])], axis=1
        )
        if shift:
            pairs = [(i, (i + shift) % cols) for i in range(cols)]
            piece = lax.ppermute(piece, "cols", pairs)
            sums = lax.ppermute(sums, "cols", pairs)
        piece = piece.astype(F32)
        lower_total = piece if lower_total is None else lower_total + piece
        sums_total = sums if sums_total is None else sums_total + sums
    new_lower = lower_total[:, :half].astype(BF16)
    next_lower = lower_total[:, half:].astype(BF16)

    sums = lax.psum(sums_total, "rows")

    def own(matrix):
        return lax.dynamic_slice_in_dim(matrix, col_at * half, half, 1)

    base = mm(inverse_upper, inverse_lower).astype(BF16)
    base_link = mm(base, own(link_below))
    new_diagonal = (mm(inverse_upper, own(inverse_lower)) + sums[:, :half]).astype(BF16)
    link_part = (sums[:, half : 2 * half] - base_link).astype(BF16)
    next_link = lax.all_gather(link_part, "cols", axis=1, tiled=True)
    next_diagonal = (
        mm(second_upper, own(second_lower))
        + mm_first(link_beside, base_link.astype(BF16))
        + sums[:, 2 * half :]
    ).astype(BF16)
    return (new_lower, new_upper, new_diagonal, next_lower, next_upper, next_link, next_diagonal)


SLOTS = 4
FREE = pl.CostEstimate(flops=0, bytes_accessed=0, transcendentals=0)
ANY = pl.BlockSpec(memory_space=pl.ANY)
SCALARS = pl.BlockSpec(memory_space=pltpu.SMEM)


def swapped(value, axis, bit):
    size = lax.axis_size(axis)
    return lax.ppermute(value, axis, [(i, i ^ bit) for i in range(size)])


def from_levels(value, shift):
    size = lax.axis_size("rows")
    return lax.ppermute(value, "rows", [(i, (i + 4 * shift) % size) for i in range(size)])


class Seat:
    def __init__(self):
        row_at = lax.axis_index("rows")
        self.row = row_at
        self.core, self.side, self.level = row_at % 2, (row_at // 2) % 2, row_at // 4
        self.depth = lax.axis_size("rows") // 4
        self.col = lax.axis_index("cols")


def spread(item, depth):
    pair = jnp.concatenate([item, swapped(item, "rows", 2)])
    near = [pair] + [from_levels(pair, shift) for shift in range(1, depth)]
    beyond = [swapped(each, "cols", 1) for each in near]
    return (
        near + [swapped(each, "rows", 1) for each in near]
        + beyond + [swapped(each, "rows", 1) for each in beyond]
    )


def spread_order(seat):
    at = jnp.arange(4 * seat.depth, dtype=jnp.int32)
    apart_core, rest = at // (2 * seat.depth), at % (2 * seat.depth)
    level = (seat.level - rest // 2) % seat.depth
    return (level * 2 + (seat.side ^ (rest % 2))) * 2 + (seat.core ^ apart_core)


def plan_body(block_count, row, l1, l2, local, meta, b1, m1, b2, m2, at1, at2):
    listed = l1.shape[0]
    tiles = at1.shape[0] // block_count
    own = row[0]

    @pl.loop(0, at1.shape[0])
    def _(i):
        at1[i] = 0
        at2[i] = 0

    @pl.loop(0, listed)
    def _(k):
        at1[l1[k]] = k + 1
        at2[l2[k]] = k + 1

    @pl.loop(0, b1.shape[0])
    def _(s):
        b1[s] = 0
        m1[s] = 0
        b2[s] = 0
        m2[s] = 0

    def scan(tile, put):
        def step(b, rank):
            g = tile * block_count + b
            here = jnp.where(at1[g] + at2[g] > 0, 1, 0)
            put(rank, b, g, here)
            return rank + here

        return lax.fori_loop(0, block_count, step, jnp.int32(0))

    def place(slot, g):
        b1[slot] = 2 * jnp.maximum(at1[g] - 1, 0)
        m1[slot] = jnp.where(at1[g] > 0, 1, 0)
        b2[slot] = 2 * jnp.maximum(at2[g] - 1, 0) + 1
        m2[slot] = jnp.where(at2[g] > 0, 1, 0)

    def put_own(rank, b, g, here):
        local[rank] = b
        place(SLOTS + rank, g)

    def put_facing(rank, b, g, here):
        @pl.when(jnp.logical_and(here > 0, rank < SLOTS))
        def _():
            place(rank, g)

    def nothing(rank, b, g, here):
        return None

    @pl.loop(0, block_count)
    def _(s):
        local[s] = 0

    meta[0] = scan(own, put_own)
    meta[1] = scan(own ^ 1, nothing)
    facing = scan(own ^ 2, put_facing)

    def put_beyond(rank, b, g, here):
        slot = facing + rank - SLOTS

        @pl.when(jnp.logical_and(here > 0, jnp.logical_and(rank >= SLOTS, slot < SLOTS)))
        def _():
            place(slot, g)

    scan(own ^ 3, put_beyond)

    def most(chip, found):
        count = scan(2 * chip, nothing) + scan(2 * chip + 1, nothing)
        return jnp.maximum(found, count)

    meta[2] = lax.fori_loop(0, tiles // 2, most, jnp.int32(0))


def plan_slots(row, list1, list2, block_count, tiles):
    def numbers(count):
        return jax.ShapeDtypeStruct((count,), jnp.int32)

    slots = SLOTS + block_count
    return pl.pallas_call(
        functools.partial(plan_body, block_count),
        out_shape=(numbers(block_count), numbers(3)) + (numbers(slots),) * 4,
        in_specs=[SCALARS] * 3,
        out_specs=(SCALARS,) * 6,
        scratch_shapes=[pltpu.SMEM((tiles * block_count,), jnp.int32)] * 2,
        name="plan_slots",
    )(jnp.reshape(row, (1,)).astype(jnp.int32), list1, list2)


def place_slots_body(b1, m1, b2, m2, u1_ref, u2_ref, link_ref, *refs):
    out_ref = refs[-1]
    at = pl.program_id(0)
    width = u1_ref.shape[1]
    used = m1[at] + m2[at] > 0

    @pl.when(used)
    def _():
        u1 = u1_ref[...].astype(F32) * m1[at].astype(F32)
        u2 = u2_ref[...].astype(F32) * m2[at].astype(F32)
        linked = mm(u1.astype(BF16), link_ref[...])
        out_ref[:width, :] = (-u1).T.astype(BF16)
        out_ref[width:, :] = (linked - u2).T.astype(BF16)

    @pl.when(jnp.logical_not(used))
    def _():
        out_ref[...] = jnp.zeros_like(out_ref)


def place_slots(gathered, link, tables, first):
    width = gathered.shape[1]
    count = tables[0].shape[0]
    return pl.pallas_call(
        place_slots_body,
        out_shape=jax.ShapeDtypeStruct((2 * width, count * BLK), BF16),
        grid_spec=pltpu.PrefetchScalarGridSpec(
            num_scalar_prefetch=4,
            grid=(count,),
            in_specs=[
                pl.BlockSpec((BLK, width), lambda s, p1, i1, p2, i2: (p1[s], 0)),
                pl.BlockSpec((BLK, width), lambda s, p1, i1, p2, i2: (p2[s], 0)),
                pl.BlockSpec((width, width), lambda s, p1, i1, p2, i2: (0, 0)),
            ]
            + [ANY] * len(first),
            out_specs=pl.BlockSpec((2 * width, BLK), lambda s, p1, i1, p2, i2: (0, s)),
        ),
        compiler_params=pltpu.CompilerParams(vmem_limit_bytes=56 * 2**20),
        cost_estimate=FREE,
        name="place_slots",
    )(*tables, gathered, gathered, link, *first)


def pack_body(local, pair, a_ref, *refs):
    refs[-1][...] = a_ref[...]


def pack(ancestor, local, columns, pairs):
    wide = ancestor.shape[1] // pairs
    turns = columns.shape[0]
    return pl.pallas_call(
        pack_body,
        out_shape=jax.ShapeDtypeStruct((SLOTS * BLK, turns * wide), BF16),
        grid_spec=pltpu.PrefetchScalarGridSpec(
            num_scalar_prefetch=2,
            grid=(turns, SLOTS),
            in_specs=[pl.BlockSpec((BLK, wide), lambda t, s, l, p: (l[SLOTS + s], p[t]))],
            out_specs=pl.BlockSpec((BLK, wide), lambda t, s, l, p: (s, t)),
        ),
        cost_estimate=FREE,
        name="pack_slots",
    )(local, columns, ancestor)


def merge_body(local, meta, pair, a_ref, got_ref, *refs):
    mine = pl.program_id(0) < meta[0]
    out_ref = refs[-1]

    @pl.when(mine)
    def _():
        out_ref[...] = a_ref[...]

    @pl.when(jnp.logical_not(mine))
    def _():
        out_ref[...] = got_ref[...]


def merge(ancestor, got, local, meta, pair, turn, pairs, first):
    wide = ancestor.shape[1] // pairs
    return pl.pallas_call(
        merge_body,
        out_shape=jax.ShapeDtypeStruct((SLOTS * BLK, wide), BF16),
        grid_spec=pltpu.PrefetchScalarGridSpec(
            num_scalar_prefetch=3,
            grid=(SLOTS,),
            in_specs=[
                pl.BlockSpec((BLK, wide), lambda s, l, n, p: (l[s], p[0])),
                pl.BlockSpec(
                    (BLK, wide), lambda s, l, n, p: (jnp.clip(s - n[0], 0, SLOTS - 1), turn)
                ),
            ]
            + [ANY] * len(first),
            out_specs=pl.BlockSpec((BLK, wide), lambda s, l, n, p: (s, 0)),
        ),
        cost_estimate=FREE,
        name="merge_slots",
    )(local, meta, jnp.reshape(pair, (1,)).astype(jnp.int32), ancestor, got, *first)


def lower_slots_body(groups, block_count, l1, l2, at, *refs):
    listed = groups * SLOTS
    tiles = (refs[:listed], refs[listed : 2 * listed])
    panel_refs, link_ref = refs[2 * listed : 2 * listed + 2], refs[2 * listed + 2]
    given_ref, kept_ref, linked_ref, total_ref = refs[-4:]
    width = link_ref.shape[0]
    half = width // 2
    rows = SLOTS * BLK

    @pl.when(pl.program_id(0) == 0)
    def _():
        linked_ref[...] = mm(panel_refs[0][...], link_ref[...]).astype(BF16)

    total_ref[...] = jnp.zeros_like(total_ref)
    for which, blocks in ((0, l1), (1, l2)):
        for group in range(groups):
            inside = []
            for k in range(group * SLOTS, (group + 1) * SLOTS):
                place = blocks[k] - at[0]
                inside.append(
                    jnp.where(jnp.logical_and(place >= 0, place < block_count), 1, 0)
                )

            @pl.when(sum(inside) > 0)
            def _():
                kept = [
                    tiles[which][group * SLOTS + k][...] * inside[k].astype(F32).astype(BF16)
                    for k in range(SLOTS)
                ]
                picked = jnp.concatenate(kept, axis=1)
                part = pl.ds(group * rows, rows)
                panel = panel_refs[which][part, :]
                if which == 0:
                    total_ref[:, :width] -= mm(picked, panel)
                    total_ref[:, width:] += mm(picked, linked_ref[part, :])
                else:
                    total_ref[:, width:] -= mm(picked, panel)

    for column, (own, other) in ((0, (kept_ref, given_ref)), (1, (given_ref, kept_ref))):

        @pl.when(at[1] == column)
        def _():
            for out, start in ((own, 0), (other, half)):
                out[:, :half] = total_ref[:, start : start + half].astype(BF16)
                second = total_ref[:, width + start : width + start + half]
                out[:, half:] = second.astype(BF16)


def lower_slots(ancestor, panels, link, list1, list2, first_block, column, first):
    rows, columns = ancestor.shape
    listed, width = list1.shape[0], link.shape[0]
    block_count = columns // BLK
    tile = largest_tile(rows, 512)
    at = jnp.stack([first_block, column]).astype(jnp.int32)

    def picked(which, k):
        def index(i, l1, l2, at):
            place = (l1, l2)[which][k] - at[0]
            inside = jnp.logical_and(place >= 0, place < block_count)
            return jnp.where(inside, i, 0), jnp.clip(place, 0, block_count - 1)

        return pl.BlockSpec((tile, BLK), index)

    specs = [picked(which, k) for which in (0, 1) for k in range(listed)]
    specs += [
        pl.BlockSpec((listed * BLK, width), lambda i, l1, l2, at: (at[1], 0)),
        pl.BlockSpec((listed * BLK, width), lambda i, l1, l2, at: (1 - at[1], 0)),
        pl.BlockSpec((width, width), lambda i, l1, l2, at: (0, 0)),
    ]
    shape = jax.ShapeDtypeStruct((rows, width), BF16)
    return pl.pallas_call(
        functools.partial(lower_slots_body, listed // SLOTS, block_count),
        out_shape=(shape, shape),
        grid_spec=pltpu.PrefetchScalarGridSpec(
            num_scalar_prefetch=3,
            grid=(rows // tile,),
            in_specs=specs + [ANY] * len(first),
            out_specs=(pl.BlockSpec((tile, width), lambda i, l1, l2, at: (i, 0)),) * 2,
            scratch_shapes=[
                pltpu.VMEM((listed * BLK, width), BF16),
                pltpu.VMEM((tile, 2 * width), F32),
            ],
        ),
        compiler_params=pltpu.CompilerParams(vmem_limit_bytes=56 * 2**20),
        cost_estimate=FREE,
        name="lower_slots",
    )(list1, list2, at, *([ancestor] * (2 * listed)), panels, panels, link, *first)


def slots_body(adds, local, count, at, w_ref, arrived_ref, *refs):
    tiles = refs[:SLOTS]
    added = refs[SLOTS : SLOTS + adds]
    placed_ref, ancestor_ref = refs[SLOTS + adds : SLOTS + adds + 2]
    out_ref, rest_w, rest_a, sems = refs[-4:]
    first = [arrived_ref[...]] + [ref[...] for ref in tiles]
    total = mm(w_ref[...], jnp.concatenate(first, axis=0))
    for ref in added:
        total = total + ref[...].astype(F32)
    out_ref[...] = total.astype(BF16)

    @pl.when(count[0] > SLOTS)
    def _():
        tile = out_ref.shape[1]
        more = rest_a.shape[0] // BLK
        column = pl.multiple_of((at[0] + pl.program_id(0)) * tile, BLK)
        copies = [
            pltpu.make_async_copy(
                placed_ref.at[:, pl.ds(2 * SLOTS * BLK, more * BLK)], rest_w, sems.at[more]
            )
        ]
        for s in range(more):
            row = pl.multiple_of(local[SLOTS + s] * BLK, BLK)
            copies.append(
                pltpu.make_async_copy(
                    ancestor_ref.at[pl.ds(row, BLK), pl.ds(column, tile)],
                    rest_a.at[pl.ds(s * BLK, BLK), :],
                    sems.at[s],
                )
            )
        for copy in copies:
            copy.start()
        for copy in copies:
            copy.wait()
        again = mm(w_ref[...], jnp.concatenate(first, axis=0))
        again = again + mm(rest_w[...], rest_a[...])
        for ref in added:
            again = again + ref[...].astype(F32)
        out_ref[...] = again.astype(BF16)


def slots_product(
    ancestor, placed, arrived, local, count, strip, within, strips, added, first
):
    columns = ancestor.shape[1]
    strip_width = columns // strips
    height = placed.shape[0]
    tile = largest_tile(strip_width, 384)
    per = strip_width // tile
    more = placed.shape[1] // BLK - 2 * SLOTS
    where_at = jnp.stack([strip * per, within * per]).astype(jnp.int32)

    def own_block(slot):
        return lambda j, l, n, p: (l[slot], p[0] + j)

    return pl.pallas_call(
        functools.partial(slots_body, len(added)),
        out_shape=jax.ShapeDtypeStruct((height, strip_width), BF16),
        grid_spec=pltpu.PrefetchScalarGridSpec(
            num_scalar_prefetch=3,
            grid=(per,),
            in_specs=[pl.BlockSpec((height, 2 * SLOTS * BLK), lambda j, l, n, p: (0, 0))]
            + [pl.BlockSpec((SLOTS * BLK, tile), lambda j, l, n, p: (0, p[1] + j))]
            + [pl.BlockSpec((BLK, tile), own_block(slot)) for slot in range(SLOTS)]
            + [pl.BlockSpec((height, tile), lambda j, l, n, p: (0, j))] * len(added)
            + [ANY] * (2 + len(first)),
            out_specs=pl.BlockSpec((height, tile), lambda j, l, n, p: (0, j)),
            scratch_shapes=[
                pltpu.VMEM((height, more * BLK), BF16),
                pltpu.VMEM((more * BLK, tile), BF16),
                pltpu.SemaphoreType.DMA((more + 1,)),
            ],
        ),
        compiler_params=pltpu.CompilerParams(vmem_limit_bytes=56 * 2**20),
        cost_estimate=FREE,
        name="slots_product",
    )(
        local, jnp.reshape(count, (1,)), where_at, placed, arrived, *([ancestor] * SLOTS),
        *added, placed, ancestor, *first,
    )


def small_sums_body(local, count, w_ref, *refs):
    tiles, outs, totals = refs[: 2 * SLOTS], refs[-4:-2], refs[-2:]
    at = pl.program_id(0)
    width = w_ref.shape[0] // 2
    half = width // 2

    @pl.when(at == 0)
    def _():
        for total in totals:
            total[...] = jnp.zeros_like(total)

    @pl.when(at * SLOTS < count[0])
    def _():
        for which, total in enumerate(totals):
            group = tiles[which * SLOTS : (which + 1) * SLOTS]
            rows = jnp.concatenate([ref[...] for ref in group], axis=0)
            total[:, : 2 * half] += mm(w_ref[:width, :], rows)
            total[:, 2 * half :] += mm(w_ref[width:, :], rows[:, half:])

    @pl.when(at == pl.num_programs(0) - 1)
    def _():
        for out, total in zip(outs, totals):
            out[...] = total[...].astype(BF16)


def small_sums(placed, pieces, local, count, first):
    width = placed.shape[0] // 2
    wide = 3 * width // 2
    slots = local.shape[0]

    def row(k):
        def index(s, l, n):
            return l[jnp.where(s * SLOTS < n[0], s, 0) * SLOTS + k], 0

        return pl.BlockSpec((BLK, width), index)

    shape = jax.ShapeDtypeStruct((width, wide), BF16)
    return pl.pallas_call(
        small_sums_body,
        out_shape=(shape, shape),
        grid_spec=pltpu.PrefetchScalarGridSpec(
            num_scalar_prefetch=2,
            grid=(slots // SLOTS,),
            in_specs=[
                pl.BlockSpec(
                    (2 * width, SLOTS * BLK),
                    lambda s, l, n: (0, 1 + jnp.where(s * SLOTS < n[0], s, 0)),
                )
            ]
            + [row(k) for k in range(SLOTS)] * 2
            + [ANY] * len(first),
            out_specs=(pl.BlockSpec((width, wide), lambda s, l, n: (0, 0)),) * 2,
            scratch_shapes=[pltpu.VMEM((width, wide), F32)] * 2,
        ),
        compiler_params=pltpu.CompilerParams(vmem_limit_bytes=56 * 2**20),
        cost_estimate=FREE,
        name="small_sums",
    )(
        local, jnp.reshape(count, (1,)), placed, *([pieces[0]] * SLOTS),
        *([pieces[1]] * SLOTS), *first,
    )


def step_body(options, which, *refs):
    choices, arrived = refs[:options], refs[options : options + 2]
    outs = refs[-2:]
    for way in (0, 1):
        for option in range(options):

            @pl.when(which[way] == option)
            def _():
                came = arrived[way][...].astype(F32) * which[2 + way].astype(F32)
                outs[way][...] = (choices[option][...].astype(F32) + came).astype(BF16)


def level_step(choices, which, arrived, first):
    height, wide = choices[0].shape
    tile = height // 4
    block = (tile, wide)

    def choice(option):
        def index(i, w):
            return jnp.where(jnp.logical_or(w[0] == option, w[1] == option), i, 0), 0

        return pl.BlockSpec(block, index)

    def whole(i, w):
        return i, 0

    shape = jax.ShapeDtypeStruct((height, wide), BF16)
    return pl.pallas_call(
        functools.partial(step_body, len(choices)),
        out_shape=(shape, shape),
        grid_spec=pltpu.PrefetchScalarGridSpec(
            num_scalar_prefetch=1,
            grid=(height // tile,),
            in_specs=[choice(option) for option in range(len(choices))]
            + [pl.BlockSpec(block, whole)] * 2
            + [ANY] * len(first),
            out_specs=(pl.BlockSpec(block, whole),) * 2,
        ),
        compiler_params=pltpu.CompilerParams(vmem_limit_bytes=56 * 2**20),
        cost_estimate=FREE,
        name="level_step",
    )(which, *choices, *arrived, *first)


def last_body(own_ref, up_ref, down_ref, *refs):
    first_ref, second_ref = refs[-2:]
    width = first_ref.shape[1]
    total = own_ref[...].astype(F32) + up_ref[...].astype(F32) + down_ref[...].astype(F32)
    first_ref[...] = total[:width].T.astype(BF16)
    second_ref[...] = total[width:].T.astype(BF16)


def last_sum(own, up, down, first):
    height, wide = own.shape
    tile = largest_tile(wide, 256)
    width = height // 2
    shape = jax.ShapeDtypeStruct((wide, width), BF16)
    return pl.pallas_call(
        last_body,
        out_shape=(shape, shape),
        grid=(wide // tile,),
        in_specs=[pl.BlockSpec((height, tile), lambda j: (0, j))] * 3 + [ANY] * len(first),
        out_specs=(pl.BlockSpec((tile, width), lambda j: (j, 0)),) * 2,
        compiler_params=pltpu.CompilerParams(vmem_limit_bytes=56 * 2**20),
        cost_estimate=FREE,
        name="last_sum",
    )(own, up, down, *first)


def split_body(parts, at, left_ref, right_ref, *refs):
    outs = refs[-parts:]
    size = outs[0].shape[0]
    for shift in range(parts):
        start = pl.multiple_of(lax.rem(at[0] + shift, parts) * size, 16)
        rows = pl.ds(start, size)
        total = left_ref[rows, :].astype(F32) + right_ref[rows, :].astype(F32)
        outs[shift][...] = total.astype(BF16)


def split_sum(left, right, at, parts, first):
    rows, wide = left.shape
    shape = jax.ShapeDtypeStruct((rows // parts, wide), BF16)
    vmem = pl.BlockSpec(memory_space=pltpu.VMEM)
    return pl.pallas_call(
        functools.partial(split_body, parts),
        out_shape=(shape,) * parts,
        in_specs=[SCALARS, vmem, vmem] + [ANY] * len(first),
        out_specs=(vmem,) * parts,
        compiler_params=pltpu.CompilerParams(vmem_limit_bytes=56 * 2**20),
        cost_estimate=FREE,
        name="split_sum",
    )(jnp.reshape(at, (1,)).astype(jnp.int32), left, right, *first)


def pair_sum(pieces, first):
    vmem = pl.BlockSpec(memory_space=pltpu.VMEM)
    count = len(pieces)

    def kernel(*refs):
        total = refs[0][...].astype(F32)
        for ref in refs[1:count]:
            total = total + ref[...].astype(F32)
        refs[-1][...] = total.astype(BF16)

    return pl.pallas_call(
        kernel,
        out_shape=jax.ShapeDtypeStruct(pieces[0].shape, BF16),
        in_specs=[vmem] * count + [ANY] * len(first),
        out_specs=vmem,
        cost_estimate=FREE,
        name="pair_sum",
    )(*pieces, *first)


def left_over(seat, ancestor, gathered, link, lists, places, dropped):
    block_rows, columns = ancestor.shape
    width = link.shape[0]
    first_row = seat.row * block_rows
    shaped = gathered.reshape(-1, BLK, width)
    u1, u2 = (
        rows_onto(
            jnp.take(shaped, place, axis=0).reshape(-1, width), blocks, first_row, block_rows
        )
        for blocks, place in zip(lists, places)
    )
    joined = jnp.concatenate([-u1.astype(F32), mm(u1, link) - u2.astype(F32)], axis=1)
    joined = jnp.where(jnp.repeat(dropped, BLK)[:, None], joined, 0.0).astype(BF16)
    wide = columns // (2 * seat.depth)
    partial = jnp.concatenate(
        [
            mm_first(
                joined,
                lax.dynamic_slice_in_dim(
                    ancestor, (2 * level + 1 - seat.side) * wide, wide, 1
                ),
            ).astype(BF16)
            for level in range(seat.depth)
        ],
        axis=1,
    )
    groups = [
        [4 * level + 2 * side + core for level in range(seat.depth) for core in range(2)]
        for side in range(2)
    ]
    own = lax.psum_scatter(
        partial, "rows", scatter_dimension=1, axis_index_groups=groups, tiled=True
    )
    return swapped(own, "rows", 2).astype(F32)


def gather_small(seat, value):
    for bit, at in ((2, seat.side), (1, seat.core)):
        other = swapped(value, "rows", bit)
        value = jnp.concatenate(
            [jnp.where(at == 0, value, other), jnp.where(at == 0, other, value)]
        )
    return value


def body_by_slots(
    ancestor,
    panel_below,
    panel_beside,
    inverse_lower,
    inverse_upper,
    list_below,
    list_beside,
    second_below,
    second_beside,
    linked_below,
    linked_beside,
    second_lower,
    second_upper,
    blocks_below,
    blocks_beside,
):
    seat = Seat()
    tile_rows, tile_cols = ancestor.shape
    block_count = tile_rows // BLK
    width = inverse_lower.shape[0]
    half = width // 2
    listed = list_below.shape[0]
    depth = seat.depth
    rows = 4 * depth
    pairs = 2 * depth
    at_first = seat.col == 0

    def either(first, second):
        return jnp.where(at_first, first, second)

    beside = jnp.concatenate(
        [mm_rows(panel_beside, inverse_upper), mm_rows(second_beside, second_upper)]
    )
    gathered = lax.all_gather(beside.astype(BF16), "rows", axis=0, tiled=True)
    below = mm(either(panel_below, second_below), either(inverse_lower, second_lower))
    panels = jnp.concatenate(spread(below.astype(BF16), depth))
    spread_at = spread_order(seat)
    link_below = mm(linked_below, second_lower).astype(BF16)
    link_beside = mm_rows(linked_beside, second_upper).astype(BF16)

    local, meta, *tables = plan_slots(
        seat.row, list_beside, blocks_beside, block_count, rows
    )
    count = meta[0]
    order = [sorted(range(depth), key=lambda d: (-abs(d - z), d)) for z in range(depth)]
    place = [[order[z].index(d) for d in range(depth)] for z in range(depth)]
    order_table = jnp.array(order, jnp.int32)
    targets = [order_table[seat.level, turn] for turn in range(depth)]

    def own(matrix):
        return lax.dynamic_slice_in_dim(matrix, seat.col * half, half, 1)

    base = mm(inverse_upper, inverse_lower).astype(BF16)
    base_link = mm(base, own(link_below))
    added = jnp.concatenate(
        [
            mm(inverse_upper, own(inverse_lower)),
            -base_link,
            mm(second_upper, own(second_lower)) + mm_first(link_beside, base_link.astype(BF16)),
        ],
        axis=1,
    )
    added = lax.dynamic_slice_in_dim(
        added, (seat.core * 2 + seat.side) * (width // 4), width // 4, 0
    )

    columns = jnp.stack([target * 2 + 1 - seat.side for target in targets])
    passed = swapped(pack(ancestor, local, columns, pairs), "rows", 1)
    arrived = []

    def send(turn, first):
        merged = merge(ancestor, passed, local, meta, columns[turn], turn, pairs, first)
        arrived.append(swapped(merged, "rows", 2))
        return merged

    merged = send(0, [])
    merged = send(1, [merged])
    merged = send(2, [merged])
    placed = place_slots(gathered, link_beside, tables, [merged])

    def strip(turn, part, added, first):
        pair = targets[turn] * 2 + seat.side
        return slots_product(
            ancestor, placed, arrived[turn], local, count, pair * 2 + part, part, rows,
            added, first,
        )

    def far_strip(turn, first):
        return strip(turn, 1 - seat.core, [], first)

    def near_strip(turn, far, first):
        return strip(turn, seat.core, [swapped(far, "rows", 1)], first)

    def moved(values, step):
        gap = depth - 1 - step
        ways = []
        for way in (1, -1):
            senders = [z for z in range(depth) if 0 <= z + way * gap < depth]
            ways.append([(z * 4 + i, (z + way) * 4 + i) for z in senders for i in range(4)])
        if step == 0:
            return [lax.ppermute(values[0], "rows", ways[0] + ways[1])]
        return [lax.ppermute(value, "rows", way) for value, way in zip(values, ways)]

    def next_step(step, layer, moving, first):
        gap = depth - 1 - step
        which = [
            [place[z][z + way * gap] if 0 <= z + way * gap < depth else 0 for z in range(depth)]
            for way in (1, -1)
        ]
        options = 1 + max(max(each) for each in which)
        which = jnp.array(which, jnp.int32)[:, seat.level]
        takes = jnp.ones((2,), jnp.int32)
        if len(moving) == 1:
            takes = jnp.stack([seat.level == 1, seat.level == depth - 2]).astype(jnp.int32)
        which = jnp.concatenate([which, takes])
        return level_step(layer[:options], which, [moving[0], moving[-1]], first)

    far = far_strip(0, [])
    layer = [near_strip(0, far, [])]
    moving = moved([layer[0]] * 2, 0)
    given, kept = lower_slots(
        ancestor, panels, link_below, list_below[spread_at], blocks_below[spread_at],
        seat.col * (tile_cols // BLK), seat.col, layer[-1:],
    )
    given_sums, kept_sums = small_sums(placed, (given, kept), local, count, [])
    got_sums = swapped(given_sums, "cols", 1)
    far = far_strip(1, [given_sums])
    layer.append(near_strip(1, far, []))
    stepped = next_step(1, layer, moving, [])
    moving = moved(stepped, 1)
    sums = split_sum(kept_sums, got_sums, seat.core, 2, stepped[:1])
    far = far_strip(2, sums[:1])
    sums = split_sum(sums[0], swapped(sums[1], "rows", 1), seat.side, 2, [far])
    merged = sums[0]
    for turn in range(3, depth):
        merged = send(turn, [merged])
    layer.append(near_strip(2, far, [merged]))
    mine = pair_sum([sums[0], swapped(sums[1], "rows", 2)], layer[-1:])
    bits = (depth - 1).bit_length()
    for bit in range(bits):
        base_now = [added] if bit == bits - 1 else []
        mine = pair_sum([mine, swapped(mine, "rows", 4 << bit)] + base_now, [])
    for step in range(2, depth - 1):
        stepped = next_step(step, layer, moving, [mine])
        moving = moved(stepped, step)
        far = far_strip(step + 1, stepped[:1])
        layer.append(near_strip(step + 1, far, []))
    whole = gather_small(seat, mine)

    given = jnp.where(got_sums[0, 0] == got_sums[0, 0], given, jnp.zeros_like(given))
    piece = kept.astype(F32) + swapped(given, "cols", 1).astype(F32)
    new_lower = piece[:, :half].astype(BF16)
    next_lower = piece[:, half:].astype(BF16)
    link_part = whole[:, half : 2 * half]
    link_other = swapped(link_part, "cols", 1)
    next_link = jnp.concatenate(
        [either(link_part, link_other), either(link_other, link_part)], axis=1
    )

    def with_rest(own, up, down):
        own_at = jnp.arange(block_count, dtype=jnp.int32)
        slot_dropped = jnp.logical_and(
            own_at < count, own_at >= 2 * SLOTS - jnp.minimum(meta[1], SLOTS)
        )
        dropped = jnp.any(
            jnp.logical_and(slot_dropped[:, None], local[:, None] == own_at[None, :]), axis=0
        )
        at = 2 * jnp.arange(listed, dtype=jnp.int32)
        total = own.astype(F32) + up.astype(F32) + down.astype(F32)
        total = total + left_over(
            seat, ancestor, gathered, link_beside, (list_beside, blocks_beside), (at, at + 1),
            dropped,
        )
        return total[:width].T.astype(BF16), total[width:].T.astype(BF16)

    def without_rest(own, up, down):
        return last_sum(own, up, down, [next_link, new_lower])

    new_upper, next_upper = lax.cond(
        meta[2] > 2 * SLOTS, with_rest, without_rest, layer[-1], *moving
    )
    return (
        new_lower, new_upper, whole[:, :half], next_lower, next_upper, next_link,
        whole[:, 2 * half :],
    )


def body(*arrays):
    ancestor, panel, list_beside = arrays[0], arrays[1], arrays[6]
    rows, cols = lax.axis_size("rows"), lax.axis_size("cols")
    by_slots = (
        cols == 2
        and rows % 4 == 0
        and rows >= 16
        and rows & (rows - 1) == 0
        and panel.shape[0] == BLK
        and list_beside.shape[0] == rows
        and ancestor.shape[0] % BLK == 0
        and ancestor.shape[0] // BLK >= 2 * SLOTS
        and ancestor.shape[0] // BLK % SLOTS == 0
        and ancestor.shape[1] % (rows * BLK) == 0
        and panel.shape[1] % (2 * rows) == 0
    )
    return (body_by_slots if by_slots else body_general)(*arrays)


def solution(mesh):
    return jax.shard_map(
        body,
        mesh=mesh,
        in_specs=(
            P("rows", "cols"),
            P("rows", None),
            P("rows", None),
            P(),
            P(),
            P(),
            P(),
            P("rows", None),
            P("rows", None),
            P(),
            P(),
            P(),
            P(),
            P(),
            P(),
        ),
        out_specs=(
            P("rows", "cols"),
            P(("cols", "rows"), None),
            P(None, "cols"),
            P("rows", "cols"),
            P(("cols", "rows"), None),
            P(),
            P(None, "cols"),
        ),
        check_vma=False,
    )
```

```python
import functools

import jax
import jax.numpy as jnp
from jax import lax
from jax.experimental import pallas as pl
from jax.experimental.pallas import tpu as pltpu
from jax.sharding import PartitionSpec as P

BLK = 128
F32 = jnp.float32
BF16 = jnp.bfloat16


def mm(left, right):
    return jnp.dot(left, right, preferred_element_type=F32)


def mm_rows(left, right):
    return lax.dot_general(left, right, (((1,), (1,)), ((), ())), preferred_element_type=F32)


def mm_first(left, right):
    return lax.dot_general(left, right, (((0,), (0,)), ((), ())), preferred_element_type=F32)


def largest_tile(size, limit):
    tile = min(limit, size)
    while size % tile:
        tile -= BLK
    return tile


def gather_pair(first, second, product):
    cols = lax.axis_size("cols")
    if cols == 2:
        at_first = lax.axis_index("cols") == 0
        mine = product(
            jnp.where(at_first, first[0], second[0]), jnp.where(at_first, first[1], second[1])
        ).astype(BF16)
        return lax.all_gather(mine, ("cols", "rows"), axis=0, tiled=True)
    return jnp.concatenate(
        [
            lax.all_gather(product(*each).astype(BF16), "rows", axis=0, tiled=True)
            for each in (first, second)
        ]
    )


def place_body(pos1, in1, pos2, in2, u1_ref, u2_ref, link_ref, out_ref):
    at = pl.program_id(0)
    width = u1_ref.shape[1]
    keep1 = in1[at].astype(F32)
    keep2 = in2[at].astype(F32)
    u1 = u1_ref[...]
    linked = mm(u1, link_ref[...])
    out_ref[:width, :] = (-u1.astype(F32) * keep1).T.astype(BF16)
    out_ref[width:, :] = (linked * keep1 - u2_ref[...].astype(F32) * keep2).T.astype(BF16)


def blocks_in_tile(blocks, first_block, block_count):
    ids = first_block + jnp.arange(block_count, dtype=jnp.int32)
    matches = ids[:, None] == blocks[None, :]
    places = jnp.sum(
        jnp.where(matches, jnp.arange(blocks.shape[0], dtype=jnp.int32)[None, :], 0), axis=1
    )
    return places.astype(jnp.int32), jnp.any(matches, axis=1).astype(jnp.int32)


def rows_onto(panel, blocks, first_row, row_count):
    global_rows = first_row + jnp.arange(row_count, dtype=jnp.int32)
    matches = (global_rows // BLK)[:, None] == blocks[None, :]
    places = jnp.sum(
        jnp.where(matches, jnp.arange(blocks.shape[0], dtype=jnp.int32)[None, :], 0), axis=1
    )
    picked = jnp.take(panel, places * BLK + global_rows % BLK, axis=0)
    return jnp.where(jnp.any(matches, axis=1)[:, None], picked, jnp.zeros_like(picked))


def place_panels(both, link, list1, list2, first_row, row_count):
    width = both.shape[1]
    listed = list1.shape[0]
    if row_count % BLK:
        u1 = rows_onto(both[: listed * BLK], list1, first_row, row_count)
        u2 = rows_onto(both[listed * BLK :], list2, first_row, row_count)
        joined = jnp.concatenate([-u1.astype(F32), mm(u1, link) - u2.astype(F32)], axis=1)
        return joined.T.astype(BF16)
    first_block = first_row // BLK
    block_count = row_count // BLK
    pos1, in1 = blocks_in_tile(list1, first_block, block_count)
    pos2, in2 = blocks_in_tile(list2, first_block, block_count)
    return pl.pallas_call(
        place_body,
        out_shape=jax.ShapeDtypeStruct((2 * width, block_count * BLK), BF16),
        grid_spec=pltpu.PrefetchScalarGridSpec(
            num_scalar_prefetch=4,
            grid=(block_count,),
            in_specs=[
                pl.BlockSpec((BLK, width), lambda b, p1, i1, p2, i2: (p1[b], 0)),
                pl.BlockSpec((BLK, width), lambda b, p1, i1, p2, i2: (listed + p2[b], 0)),
                pl.BlockSpec((width, width), lambda b, p1, i1, p2, i2: (0, 0)),
            ],
            out_specs=pl.BlockSpec((2 * width, BLK), lambda b, p1, i1, p2, i2: (0, b)),
        ),
        compiler_params=pltpu.CompilerParams(vmem_limit_bytes=24 * 2**20),
        cost_estimate=pl.CostEstimate(
            flops=2 * block_count * BLK * width * width,
            bytes_accessed=8 * block_count * BLK * width,
            transcendentals=0,
        ),
        name="place_panels",
    )(pos1, in1, pos2, in2, both, both, link)


def lower_body(listed, loc1, in1, loc2, in2, part, *refs):
    tiles1, tiles2 = refs[:listed], refs[listed : 2 * listed]
    l1_ref, v1_ref, l2_ref, out_ref = refs[2 * listed :]
    half = l1_ref.shape[1]
    picked1 = jnp.concatenate(
        [tiles1[k][...] * in1[k].astype(F32).astype(BF16) for k in range(listed)], axis=1
    )
    picked2 = jnp.concatenate(
        [tiles2[k][...] * in2[k].astype(F32).astype(BF16) for k in range(listed)], axis=1
    )
    out_ref[:, :half] = (-mm(picked1, l1_ref[...])).astype(BF16)
    out_ref[:, half:] = (mm(picked1, v1_ref[...]) - mm(picked2, l2_ref[...])).astype(BF16)


def lower_partial(ancestor, both, linked, list1, list2, first_block, part, parts):
    rows, columns = ancestor.shape
    width = both.shape[1]
    half = width // parts
    listed = list1.shape[0]
    depth = listed * BLK
    block_count = columns // BLK
    tile = largest_tile(rows, 512)

    def local(blocks):
        at = blocks - first_block
        inside = jnp.logical_and(at >= 0, at < block_count)
        return jnp.clip(at, 0, block_count - 1), inside.astype(jnp.int32)

    loc1, in1 = local(list1)
    loc2, in2 = local(list2)
    specs = [
        pl.BlockSpec((tile, BLK), functools.partial(lambda k, i, l1, i1, l2, i2, p: (i, l1[k]), k))
        for k in range(listed)
    ] + [
        pl.BlockSpec((tile, BLK), functools.partial(lambda k, i, l1, i1, l2, i2, p: (i, l2[k]), k))
        for k in range(listed)
    ]
    specs += [
        pl.BlockSpec((depth, half), lambda i, l1, i1, l2, i2, p: (0, p[0])),
        pl.BlockSpec((depth, half), lambda i, l1, i1, l2, i2, p: (0, p[0])),
        pl.BlockSpec((depth, half), lambda i, l1, i1, l2, i2, p: (1, p[0])),
    ]
    return pl.pallas_call(
        functools.partial(lower_body, listed),
        out_shape=jax.ShapeDtypeStruct((rows, 2 * half), BF16),
        grid_spec=pltpu.PrefetchScalarGridSpec(
            num_scalar_prefetch=5,
            grid=(rows // tile,),
            in_specs=specs,
            out_specs=pl.BlockSpec((tile, 2 * half), lambda i, l1, i1, l2, i2, p: (i, 0)),
        ),
        compiler_params=pltpu.CompilerParams(vmem_limit_bytes=40 * 2**20),
        cost_estimate=pl.CostEstimate(
            flops=6 * rows * depth * half,
            bytes_accessed=4 * rows * depth + 6 * depth * half,
            transcendentals=0,
        ),
        name="lower_partial",
    )(
        loc1, in1, loc2, in2, jnp.reshape(part, (1,)).astype(jnp.int32),
        *([ancestor] * (2 * listed)), both, linked, both,
    )


def strip_body(strip, w_ref, a_ref, *refs):
    total = mm(w_ref[...], a_ref[...])
    for ref in refs[:-1]:
        total = total + ref[...].astype(F32)
    refs[-1][...] = total.astype(BF16)


def strip_product(ancestor, placed, strip, strips, *added):
    rows, columns = ancestor.shape
    strip_width = columns // strips
    height = placed.shape[0]
    if strip_width % BLK:
        total = mm(
            placed, lax.dynamic_slice_in_dim(ancestor, strip * strip_width, strip_width, 1)
        )
        for each in added:
            total = total + each.astype(F32)
        return total.astype(BF16)
    tile = largest_tile(strip_width, 256)
    per = strip_width // tile
    return pl.pallas_call(
        strip_body,
        out_shape=jax.ShapeDtypeStruct((height, strip_width), BF16),
        grid_spec=pltpu.PrefetchScalarGridSpec(
            num_scalar_prefetch=1,
            grid=(per,),
            in_specs=[
                pl.BlockSpec((height, rows), lambda j, s: (0, 0)),
                pl.BlockSpec((rows, tile), lambda j, s: (0, s[0] * per + j)),
            ]
            + [pl.BlockSpec((height, tile), lambda j, s: (0, j))] * len(added),
            out_specs=pl.BlockSpec((height, tile), lambda j, s: (0, j)),
        ),
        compiler_params=pltpu.CompilerParams(vmem_limit_bytes=40 * 2**20),
        cost_estimate=pl.CostEstimate(
            flops=2 * height * rows * strip_width,
            bytes_accessed=2 * (rows * strip_width + height * rows)
            + 2 * (1 + len(added)) * height * strip_width,
            transcendentals=0,
        ),
        name="strip_product",
    )(jnp.reshape(strip, (1,)).astype(jnp.int32), placed, ancestor, *added)


def add_pair(left, right):
    return (left.astype(F32) + right.astype(F32)).astype(BF16)


def upper_sums(ancestor, placed):
    strips = lax.axis_size("rows")
    row_at = lax.axis_index("rows")
    inner = 4 if strips % 4 == 0 else 1
    if inner == 1:
        whole = strip_product(ancestor, placed, 0, 1)
        return lax.psum_scatter(whole.astype(F32), "rows", scatter_dimension=1, tiled=True)
    depth = strips // inner
    core, side, level = row_at % 2, (row_at // 2) % 2, row_at // 4
    to_core = [(i, i ^ 1) for i in range(strips)]
    to_side = [(i, i ^ 2) for i in range(strips)]
    order = [sorted(range(depth), key=lambda d: (-abs(d - z), d)) for z in range(depth)]
    place = [[order[z].index(d) for d in range(depth)] for z in range(depth)]
    order_table = jnp.array(order, jnp.int32)

    def strip_of(target, x, c):
        return (target * 2 + x) * 2 + c

    layer = []
    for turn in range(depth):
        target = order_table[level, turn]
        far = strip_product(ancestor, placed, strip_of(target, 1 - side, 1 - core), strips)
        far = lax.ppermute(far, "rows", to_core)
        near = strip_product(ancestor, placed, strip_of(target, side, 1 - core), strips)
        near = lax.ppermute(near, "rows", to_core)
        far = strip_product(ancestor, placed, strip_of(target, 1 - side, core), strips, far)
        far = lax.ppermute(far, "rows", to_side)
        layer.append(
            strip_product(ancestor, placed, strip_of(target, side, core), strips, near, far)
        )

    def own_part(step, way):
        gap = depth - 1 - step
        chosen = None
        for z in range(depth):
            target = z + way * gap
            if 0 <= target < depth:
                value = layer[place[z][target]]
                chosen = value if chosen is None else jnp.where(level == z, value, chosen)
        return chosen

    arrived = {1: None, -1: None}
    for step in range(depth - 1):
        gap = depth - 1 - step
        for way in (1, -1):
            senders = [z for z in range(depth) if 0 <= z + way * gap < depth]
            pairs = [
                (z * inner + i, (z + way) * inner + i) for z in senders for i in range(inner)
            ]
            value = own_part(step, way)
            if arrived[way] is not None:
                value = add_pair(value, arrived[way])
            arrived[way] = lax.ppermute(value, "rows", pairs)
    total = layer[-1].astype(F32)
    for way in (1, -1):
        if arrived[way] is not None:
            total = total + arrived[way].astype(F32)
    return total


def body_general(
    ancestor,
    panel_below,
    panel_beside,
    inverse_lower,
    inverse_upper,
    list_below,
    list_beside,
    second_below,
    second_beside,
    linked_below,
    linked_beside,
    second_lower,
    second_upper,
    blocks_below,
    blocks_beside,
):
    row_at = lax.axis_index("rows")
    col_at = lax.axis_index("cols")
    cols = lax.axis_size("cols")
    tile_rows, tile_cols = ancestor.shape
    width = inverse_lower.shape[0]
    half = width // cols

    beside = gather_pair((panel_beside, inverse_upper), (second_beside, second_upper), mm_rows)
    below = gather_pair((panel_below, inverse_lower), (second_below, second_lower), mm)
    link_below = mm(linked_below, second_lower).astype(BF16)
    link_beside = mm_rows(linked_beside, second_upper).astype(BF16)

    placed = place_panels(
        beside, link_beside, list_beside, blocks_beside,
        row_at * tile_rows, tile_rows,
    )
    upper = upper_sums(ancestor, placed)
    new_upper = upper[:width].T.astype(BF16)
    next_upper = upper[width:].T.astype(BF16)

    depth = below.shape[0] // 2
    linked = mm(below[:depth], link_below).astype(BF16)
    lower_total = None
    sums_total = None
    for shift in reversed(range(cols)):
        part = (col_at + shift) % cols
        piece = lower_partial(
            ancestor, below, linked, list_below, blocks_below,
            col_at * (tile_cols // BLK), part, cols,
        )
        sums = jnp.concatenate(
            [mm(placed[:width], piece), mm(placed[width:], piece[:, half:])], axis=1
        )
        if shift:
            pairs = [(i, (i + shift) % cols) for i in range(cols)]
            piece = lax.ppermute(piece, "cols", pairs)
            sums = lax.ppermute(sums, "cols", pairs)
        piece = piece.astype(F32)
        lower_total = piece if lower_total is None else lower_total + piece
        sums_total = sums if sums_total is None else sums_total + sums
    new_lower = lower_total[:, :half].astype(BF16)
    next_lower = lower_total[:, half:].astype(BF16)

    sums = lax.psum(sums_total, "rows")

    def own(matrix):
        return lax.dynamic_slice_in_dim(matrix, col_at * half, half, 1)

    base = mm(inverse_upper, inverse_lower).astype(BF16)
    base_link = mm(base, own(link_below))
    new_diagonal = (mm(inverse_upper, own(inverse_lower)) + sums[:, :half]).astype(BF16)
    link_part = (sums[:, half : 2 * half] - base_link).astype(BF16)
    next_link = lax.all_gather(link_part, "cols", axis=1, tiled=True)
    next_diagonal = (
        mm(second_upper, own(second_lower))
        + mm_first(link_beside, base_link.astype(BF16))
        + sums[:, 2 * half :]
    ).astype(BF16)
    return (new_lower, new_upper, new_diagonal, next_lower, next_upper, next_link, next_diagonal)


SLOTS = 4
FREE = pl.CostEstimate(flops=0, bytes_accessed=0, transcendentals=0)
ANY = pl.BlockSpec(memory_space=pl.ANY)
SCALARS = pl.BlockSpec(memory_space=pltpu.SMEM)


def swapped(value, axis, bit):
    size = lax.axis_size(axis)
    return lax.ppermute(value, axis, [(i, i ^ bit) for i in range(size)])


def from_levels(value, shift):
    size = lax.axis_size("rows")
    return lax.ppermute(value, "rows", [(i, (i + 4 * shift) % size) for i in range(size)])


class Seat:
    def __init__(self):
        row_at = lax.axis_index("rows")
        self.row = row_at
        self.core, self.side, self.level = row_at % 2, (row_at // 2) % 2, row_at // 4
        self.depth = lax.axis_size("rows") // 4
        self.col = lax.axis_index("cols")


def spread(item, depth):
    pair = jnp.concatenate([item, swapped(item, "rows", 2)])
    near = [pair] + [from_levels(pair, shift) for shift in range(1, depth)]
    beyond = [swapped(each, "cols", 1) for each in near]
    return (
        near + [swapped(each, "rows", 1) for each in near]
        + beyond + [swapped(each, "rows", 1) for each in beyond]
    )


def spread_place(seat, listed, which):
    at = jnp.arange(listed, dtype=jnp.int32)
    core, side, level = at % 2, (at // 2) % 2, at // 4
    apart = (seat.col ^ which) * 2 + (seat.core ^ core)
    return (apart * seat.depth + (seat.level - level) % seat.depth) * 2 + (seat.side ^ side)


def plan_body(block_count, row, l1, l2, local, meta, b1, m1, b2, m2, at1, at2):
    listed = l1.shape[0]
    tiles = at1.shape[0] // block_count
    depth = listed // 4
    own, column = row[0], row[1]

    def place_of(k, which):
        apart = (own >> 2) - (k >> 2)
        apart = jnp.where(apart < 0, apart + depth, apart)
        half = (column ^ which) * 2 + ((own ^ k) & 1)
        return (half * depth + apart) * 2 + (((own ^ k) >> 1) & 1)

    @pl.loop(0, at1.shape[0])
    def _(i):
        at1[i] = 0
        at2[i] = 0

    @pl.loop(0, listed)
    def _(k):
        at1[l1[k]] = k + 1
        at2[l2[k]] = k + 1

    @pl.loop(0, b1.shape[0])
    def _(s):
        b1[s] = 0
        m1[s] = 0
        b2[s] = 0
        m2[s] = 0

    def scan(tile, put):
        def step(b, rank):
            g = tile * block_count + b
            here = jnp.where(at1[g] + at2[g] > 0, 1, 0)
            put(rank, b, g, here)
            return rank + here

        return lax.fori_loop(0, block_count, step, jnp.int32(0))

    def place(slot, g):
        b1[slot] = place_of(jnp.maximum(at1[g] - 1, 0), 0)
        m1[slot] = jnp.where(at1[g] > 0, 1, 0)
        b2[slot] = place_of(jnp.maximum(at2[g] - 1, 0), 1)
        m2[slot] = jnp.where(at2[g] > 0, 1, 0)

    def put_own(rank, b, g, here):
        local[rank] = b
        place(SLOTS + rank, g)

    def put_facing(rank, b, g, here):
        @pl.when(jnp.logical_and(here > 0, rank < SLOTS))
        def _():
            place(rank, g)

    def nothing(rank, b, g, here):
        return None

    @pl.loop(0, block_count)
    def _(s):
        local[s] = 0

    meta[0] = scan(own, put_own)
    meta[1] = scan(own ^ 1, nothing)
    facing = scan(own ^ 2, put_facing)

    def put_beyond(rank, b, g, here):
        slot = facing + rank - SLOTS

        @pl.when(jnp.logical_and(here > 0, jnp.logical_and(rank >= SLOTS, slot < SLOTS)))
        def _():
            place(slot, g)

    scan(own ^ 3, put_beyond)

    def most(chip, found):
        count = scan(2 * chip, nothing) + scan(2 * chip + 1, nothing)
        return jnp.maximum(found, count)

    meta[2] = lax.fori_loop(0, tiles // 2, most, jnp.int32(0))


def plan_slots(row, column, list1, list2, block_count, tiles):
    def numbers(count):
        return jax.ShapeDtypeStruct((count,), jnp.int32)

    slots = SLOTS + block_count
    return pl.pallas_call(
        functools.partial(plan_body, block_count),
        out_shape=(numbers(block_count), numbers(3)) + (numbers(slots),) * 4,
        in_specs=[SCALARS] * 3,
        out_specs=(SCALARS,) * 6,
        scratch_shapes=[pltpu.SMEM((tiles * block_count,), jnp.int32)] * 2,
        name="plan_slots",
    )(jnp.stack([row, column]).astype(jnp.int32), list1, list2)


def place_slots_body(count, b1, m1, b2, m2, link_ref, *refs):
    pieces = refs[:count]
    out_ref, got, sems = refs[-3:]
    width = link_ref.shape[0]
    slots = b1.shape[0]

    def copies(s, act):
        for which, (block, used) in enumerate(((b1, m1), (b2, m2))):
            for at in range(count):

                @pl.when(jnp.logical_and(used[s] > 0, block[s] >> 1 == at))
                def _():
                    row = pl.multiple_of((block[s] & 1) * BLK, BLK)
                    copy = pltpu.make_async_copy(
                        pieces[at].at[pl.ds(row, BLK), :], got.at[which, s], sems.at[which, s]
                    )
                    getattr(copy, act)()

    @pl.loop(0, slots)
    def _(s):
        copies(s, "start")

    for s in range(slots):
        columns = pl.ds(s * BLK, BLK)
        used = m1[s] + m2[s] > 0

        @pl.when(used)
        def _():
            copies(s, "wait")
            u1 = jnp.where(m1[s] > 0, got[0, s].astype(F32), 0.0)
            u2 = jnp.where(m2[s] > 0, got[1, s].astype(F32), 0.0)
            linked = mm(u1.astype(BF16), link_ref[...])
            out_ref[:width, columns] = (-u1).T.astype(BF16)
            out_ref[width:, columns] = (linked - u2).T.astype(BF16)

        @pl.when(jnp.logical_not(used))
        def _():
            out_ref[:, columns] = jnp.zeros((2 * width, BLK), BF16)


def place_slots(pieces, link, tables, first):
    width = link.shape[0]
    slots = tables[0].shape[0]
    vmem = pl.BlockSpec(memory_space=pltpu.VMEM)
    return pl.pallas_call(
        functools.partial(place_slots_body, len(pieces)),
        out_shape=jax.ShapeDtypeStruct((2 * width, slots * BLK), BF16),
        in_specs=[SCALARS] * 4 + [vmem] + [ANY] * (len(pieces) + len(first)),
        out_specs=vmem,
        scratch_shapes=[
            pltpu.VMEM((2, slots, BLK, width), BF16),
            pltpu.SemaphoreType.DMA((2, slots)),
        ],
        compiler_params=pltpu.CompilerParams(vmem_limit_bytes=56 * 2**20),
        cost_estimate=FREE,
        name="place_slots",
    )(*tables, link, *pieces, *first)


def pack_body(local, pair, a_ref, *refs):
    refs[-1][...] = a_ref[...]


def pack(ancestor, local, columns, pairs, first):
    wide = ancestor.shape[1] // pairs
    turns = columns.shape[0]
    return pl.pallas_call(
        pack_body,
        out_shape=jax.ShapeDtypeStruct((SLOTS * BLK, turns * wide), BF16),
        grid_spec=pltpu.PrefetchScalarGridSpec(
            num_scalar_prefetch=2,
            grid=(turns, SLOTS),
            in_specs=[pl.BlockSpec((BLK, wide), lambda t, s, l, p: (l[SLOTS + s], p[t]))]
            + [ANY] * len(first),
            out_specs=pl.BlockSpec((BLK, wide), lambda t, s, l, p: (s, t)),
        ),
        cost_estimate=FREE,
        name="pack_slots",
    )(local, columns, ancestor, *first)


def merge_body(local, meta, pair, a_ref, got_ref, *refs):
    mine = pl.program_id(0) < meta[0]
    out_ref = refs[-1]

    @pl.when(mine)
    def _():
        out_ref[...] = a_ref[...]

    @pl.when(jnp.logical_not(mine))
    def _():
        out_ref[...] = got_ref[...]


def merge(ancestor, got, local, meta, pair, turn, pairs, first):
    wide = ancestor.shape[1] // pairs
    return pl.pallas_call(
        merge_body,
        out_shape=jax.ShapeDtypeStruct((SLOTS * BLK, wide), BF16),
        grid_spec=pltpu.PrefetchScalarGridSpec(
            num_scalar_prefetch=3,
            grid=(SLOTS,),
            in_specs=[
                pl.BlockSpec((BLK, wide), lambda s, l, n, p: (l[s], p[0])),
                pl.BlockSpec(
                    (BLK, wide), lambda s, l, n, p: (jnp.clip(s - n[0], 0, SLOTS - 1), turn)
                ),
            ]
            + [ANY] * len(first),
            out_specs=pl.BlockSpec((BLK, wide), lambda s, l, n, p: (s, 0)),
        ),
        cost_estimate=FREE,
        name="merge_slots",
    )(local, meta, jnp.reshape(pair, (1,)).astype(jnp.int32), ancestor, got, *first)


def lower_slots_body(groups, block_count, l1, l2, at, *refs):
    listed = groups * SLOTS
    tiles = (refs[:listed], refs[listed : 2 * listed])
    panel_refs, link_ref = refs[2 * listed : 2 * listed + 2], refs[2 * listed + 2]
    given_ref, kept_ref, linked_ref, total_ref = refs[-4:]
    width = link_ref.shape[0]
    half = width // 2

    @pl.when(pl.program_id(0) == 0)
    def _():
        linked_ref[...] = mm(panel_refs[0][...], link_ref[...]).astype(BF16)

    def picked(which, blocks):
        kept = []
        for k in range(listed):
            place = blocks[k] - at[0]
            inside = jnp.logical_and(place >= 0, place < block_count)
            kept.append(tiles[which][k][...] * jnp.where(inside, 1.0, 0.0).astype(BF16))
        return jnp.concatenate(kept, axis=1)

    picked1 = picked(0, l1)
    total_ref[:, :width] = -mm(picked1, panel_refs[0][...])
    second = mm(picked1, linked_ref[...]) - mm(picked(1, l2), panel_refs[1][...])
    total_ref[:, width:] = second

    for column, (own, other) in ((0, (kept_ref, given_ref)), (1, (given_ref, kept_ref))):

        @pl.when(at[1] == column)
        def _():
            for out, start in ((own, 0), (other, half)):
                out[:, :half] = total_ref[:, start : start + half].astype(BF16)
                second = total_ref[:, width + start : width + start + half]
                out[:, half:] = second.astype(BF16)


def lower_slots(ancestor, panels, link, list1, list2, first_block, column, first):
    rows, columns = ancestor.shape
    listed, width = list1.shape[0], link.shape[0]
    block_count = columns // BLK
    tile = largest_tile(rows, 512)
    at = jnp.stack([first_block, column]).astype(jnp.int32)

    def picked(which, k):
        def index(i, l1, l2, at):
            place = (l1, l2)[which][k] - at[0]
            inside = jnp.logical_and(place >= 0, place < block_count)
            return jnp.where(inside, i, 0), jnp.clip(place, 0, block_count - 1)

        return pl.BlockSpec((tile, BLK), index)

    specs = [picked(which, k) for which in (0, 1) for k in range(listed)]
    specs += [
        pl.BlockSpec((listed * BLK, width), lambda i, l1, l2, at: (0, 0)),
        pl.BlockSpec((listed * BLK, width), lambda i, l1, l2, at: (1, 0)),
        pl.BlockSpec((width, width), lambda i, l1, l2, at: (0, 0)),
    ]
    shape = jax.ShapeDtypeStruct((rows, width), BF16)
    return pl.pallas_call(
        functools.partial(lower_slots_body, listed // SLOTS, block_count),
        out_shape=(shape, shape),
        grid_spec=pltpu.PrefetchScalarGridSpec(
            num_scalar_prefetch=3,
            grid=(rows // tile,),
            in_specs=specs + [ANY] * len(first),
            out_specs=(pl.BlockSpec((tile, width), lambda i, l1, l2, at: (i, 0)),) * 2,
            scratch_shapes=[
                pltpu.VMEM((listed * BLK, width), BF16),
                pltpu.VMEM((tile, 2 * width), F32),
            ],
        ),
        compiler_params=pltpu.CompilerParams(vmem_limit_bytes=56 * 2**20),
        cost_estimate=FREE,
        name="lower_slots",
    )(list1, list2, at, *([ancestor] * (2 * listed)), panels, panels, link, *first)


def slots_body(adds, local, count, at, w_ref, arrived_ref, *refs):
    tiles = refs[:SLOTS]
    added = refs[SLOTS : SLOTS + adds]
    placed_ref, ancestor_ref = refs[SLOTS + adds : SLOTS + adds + 2]
    out_ref, rest_w, rest_a, sems = refs[-4:]
    first = [arrived_ref[...]] + [ref[...] for ref in tiles]
    total = mm(w_ref[...], jnp.concatenate(first, axis=0))
    for ref in added:
        total = total + ref[...].astype(F32)
    out_ref[...] = total.astype(BF16)

    @pl.when(count[0] > SLOTS)
    def _():
        tile = out_ref.shape[1]
        more = rest_a.shape[0] // BLK
        column = pl.multiple_of((at[0] + pl.program_id(0)) * tile, BLK)
        copies = [
            pltpu.make_async_copy(
                placed_ref.at[:, pl.ds(2 * SLOTS * BLK, more * BLK)], rest_w, sems.at[more]
            )
        ]
        for s in range(more):
            row = pl.multiple_of(local[SLOTS + s] * BLK, BLK)
            copies.append(
                pltpu.make_async_copy(
                    ancestor_ref.at[pl.ds(row, BLK), pl.ds(column, tile)],
                    rest_a.at[pl.ds(s * BLK, BLK), :],
                    sems.at[s],
                )
            )
        for copy in copies:
            copy.start()
        for copy in copies:
            copy.wait()
        again = mm(w_ref[...], jnp.concatenate(first, axis=0))
        again = again + mm(rest_w[...], rest_a[...])
        for ref in added:
            again = again + ref[...].astype(F32)
        out_ref[...] = again.astype(BF16)


def slots_product(
    ancestor, placed, arrived, local, count, strip, within, strips, added, first
):
    columns = ancestor.shape[1]
    strip_width = columns // strips
    height = placed.shape[0]
    tile = largest_tile(strip_width, 384)
    per = strip_width // tile
    more = placed.shape[1] // BLK - 2 * SLOTS
    where_at = jnp.stack([strip * per, within * per]).astype(jnp.int32)

    def own_block(slot):
        return lambda j, l, n, p: (l[slot], p[0] + j)

    return pl.pallas_call(
        functools.partial(slots_body, len(added)),
        out_shape=jax.ShapeDtypeStruct((height, strip_width), BF16),
        grid_spec=pltpu.PrefetchScalarGridSpec(
            num_scalar_prefetch=3,
            grid=(per,),
            in_specs=[pl.BlockSpec((height, 2 * SLOTS * BLK), lambda j, l, n, p: (0, 0))]
            + [pl.BlockSpec((SLOTS * BLK, tile), lambda j, l, n, p: (0, p[1] + j))]
            + [pl.BlockSpec((BLK, tile), own_block(slot)) for slot in range(SLOTS)]
            + [pl.BlockSpec((height, tile), lambda j, l, n, p: (0, j))] * len(added)
            + [ANY] * (2 + len(first)),
            out_specs=pl.BlockSpec((height, tile), lambda j, l, n, p: (0, j)),
            scratch_shapes=[
                pltpu.VMEM((height, more * BLK), BF16),
                pltpu.VMEM((more * BLK, tile), BF16),
                pltpu.SemaphoreType.DMA((more + 1,)),
            ],
        ),
        compiler_params=pltpu.CompilerParams(vmem_limit_bytes=56 * 2**20),
        cost_estimate=FREE,
        name="slots_product",
    )(
        local, jnp.reshape(count, (1,)), where_at, placed, arrived, *([ancestor] * SLOTS),
        *added, placed, ancestor, *first,
    )


def small_sums_body(local, count, w_ref, *refs):
    tiles, outs, totals = refs[: 2 * SLOTS], refs[-4:-2], refs[-2:]
    at = pl.program_id(0)
    width = w_ref.shape[0] // 2
    half = width // 2

    @pl.when(at == 0)
    def _():
        for total in totals:
            total[...] = jnp.zeros_like(total)

    @pl.when(at * SLOTS < count[0])
    def _():
        for which, total in enumerate(totals):
            group = tiles[which * SLOTS : (which + 1) * SLOTS]
            rows = jnp.concatenate([ref[...] for ref in group], axis=0)
            total[:, : 2 * half] += mm(w_ref[:width, :], rows)
            total[:, 2 * half :] += mm(w_ref[width:, :], rows[:, half:])

    @pl.when(at == pl.num_programs(0) - 1)
    def _():
        for out, total in zip(outs, totals):
            out[...] = total[...].astype(BF16)


def small_sums(placed, pieces, local, count, first):
    width = placed.shape[0] // 2
    wide = 3 * width // 2
    slots = local.shape[0]

    def row(k):
        def index(s, l, n):
            return l[jnp.where(s * SLOTS < n[0], s, 0) * SLOTS + k], 0

        return pl.BlockSpec((BLK, width), index)

    shape = jax.ShapeDtypeStruct((width, wide), BF16)
    return pl.pallas_call(
        small_sums_body,
        out_shape=(shape, shape),
        grid_spec=pltpu.PrefetchScalarGridSpec(
            num_scalar_prefetch=2,
            grid=(slots // SLOTS,),
            in_specs=[
                pl.BlockSpec(
                    (2 * width, SLOTS * BLK),
                    lambda s, l, n: (0, 1 + jnp.where(s * SLOTS < n[0], s, 0)),
                )
            ]
            + [row(k) for k in range(SLOTS)] * 2
            + [ANY] * len(first),
            out_specs=(pl.BlockSpec((width, wide), lambda s, l, n: (0, 0)),) * 2,
            scratch_shapes=[pltpu.VMEM((width, wide), F32)] * 2,
        ),
        compiler_params=pltpu.CompilerParams(vmem_limit_bytes=56 * 2**20),
        cost_estimate=FREE,
        name="small_sums",
    )(
        local, jnp.reshape(count, (1,)), placed, *([pieces[0]] * SLOTS),
        *([pieces[1]] * SLOTS), *first,
    )


def step_body(options, which, *refs):
    choices, arrived = refs[:options], refs[options : options + 2]
    outs = refs[-2:]
    for way in (0, 1):
        for option in range(options):

            @pl.when(which[way] == option)
            def _():
                came = arrived[way][...].astype(F32) * which[2 + way].astype(F32)
                outs[way][...] = (choices[option][...].astype(F32) + came).astype(BF16)


def level_step(choices, which, arrived, first):
    height, wide = choices[0].shape
    tile = height // 4
    block = (tile, wide)

    def choice(option):
        def index(i, w):
            return jnp.where(jnp.logical_or(w[0] == option, w[1] == option), i, 0), 0

        return pl.BlockSpec(block, index)

    def whole(i, w):
        return i, 0

    shape = jax.ShapeDtypeStruct((height, wide), BF16)
    return pl.pallas_call(
        functools.partial(step_body, len(choices)),
        out_shape=(shape, shape),
        grid_spec=pltpu.PrefetchScalarGridSpec(
            num_scalar_prefetch=1,
            grid=(height // tile,),
            in_specs=[choice(option) for option in range(len(choices))]
            + [pl.BlockSpec(block, whole)] * 2
            + [ANY] * len(first),
            out_specs=(pl.BlockSpec(block, whole),) * 2,
        ),
        compiler_params=pltpu.CompilerParams(vmem_limit_bytes=56 * 2**20),
        cost_estimate=FREE,
        name="level_step",
    )(which, *choices, *arrived, *first)


def last_body(own_ref, up_ref, down_ref, *refs):
    first_ref, second_ref = refs[-2:]
    width = first_ref.shape[1]
    total = own_ref[...].astype(F32) + up_ref[...].astype(F32) + down_ref[...].astype(F32)
    first_ref[...] = total[:width].T.astype(BF16)
    second_ref[...] = total[width:].T.astype(BF16)


def last_sum(own, up, down, first):
    height, wide = own.shape
    tile = largest_tile(wide, 256)
    width = height // 2
    shape = jax.ShapeDtypeStruct((wide, width), BF16)
    return pl.pallas_call(
        last_body,
        out_shape=(shape, shape),
        grid=(wide // tile,),
        in_specs=[pl.BlockSpec((height, tile), lambda j: (0, j))] * 3 + [ANY] * len(first),
        out_specs=(pl.BlockSpec((tile, width), lambda j: (j, 0)),) * 2,
        compiler_params=pltpu.CompilerParams(vmem_limit_bytes=56 * 2**20),
        cost_estimate=FREE,
        name="last_sum",
    )(own, up, down, *first)


def split_body(parts, at, left_ref, right_ref, *refs):
    outs = refs[-parts:]
    size = outs[0].shape[0]
    for shift in range(parts):
        start = pl.multiple_of(lax.rem(at[0] + shift, parts) * size, 16)
        rows = pl.ds(start, size)
        total = left_ref[rows, :].astype(F32) + right_ref[rows, :].astype(F32)
        outs[shift][...] = total.astype(BF16)


def split_sum(left, right, at, parts, first):
    rows, wide = left.shape
    shape = jax.ShapeDtypeStruct((rows // parts, wide), BF16)
    vmem = pl.BlockSpec(memory_space=pltpu.VMEM)
    return pl.pallas_call(
        functools.partial(split_body, parts),
        out_shape=(shape,) * parts,
        in_specs=[SCALARS, vmem, vmem] + [ANY] * len(first),
        out_specs=(vmem,) * parts,
        compiler_params=pltpu.CompilerParams(vmem_limit_bytes=56 * 2**20),
        cost_estimate=FREE,
        name="split_sum",
    )(jnp.reshape(at, (1,)).astype(jnp.int32), left, right, *first)


def pair_sum(pieces, first):
    vmem = pl.BlockSpec(memory_space=pltpu.VMEM)
    count = len(pieces)

    def kernel(*refs):
        total = refs[0][...].astype(F32)
        for ref in refs[1:count]:
            total = total + ref[...].astype(F32)
        refs[-1][...] = total.astype(BF16)

    return pl.pallas_call(
        kernel,
        out_shape=jax.ShapeDtypeStruct(pieces[0].shape, BF16),
        in_specs=[vmem] * count + [ANY] * len(first),
        out_specs=vmem,
        cost_estimate=FREE,
        name="pair_sum",
    )(*pieces, *first)


def left_over(seat, ancestor, pieces, link, lists, places, dropped):
    block_rows, columns = ancestor.shape
    width = link.shape[0]
    first_row = seat.row * block_rows
    shaped = jnp.concatenate(pieces).reshape(-1, BLK, width)
    u1, u2 = (
        rows_onto(
            jnp.take(shaped, place, axis=0).reshape(-1, width), blocks, first_row, block_rows
        )
        for blocks, place in zip(lists, places)
    )
    joined = jnp.concatenate([-u1.astype(F32), mm(u1, link) - u2.astype(F32)], axis=1)
    joined = jnp.where(jnp.repeat(dropped, BLK)[:, None], joined, 0.0).astype(BF16)
    wide = columns // (2 * seat.depth)
    partial = jnp.concatenate(
        [
            mm_first(
                joined,
                lax.dynamic_slice_in_dim(
                    ancestor, (2 * level + 1 - seat.side) * wide, wide, 1
                ),
            ).astype(BF16)
            for level in range(seat.depth)
        ],
        axis=1,
    )
    groups = [
        [4 * level + 2 * side + core for level in range(seat.depth) for core in range(2)]
        for side in range(2)
    ]
    own = lax.psum_scatter(
        partial, "rows", scatter_dimension=1, axis_index_groups=groups, tiled=True
    )
    return swapped(own, "rows", 2).astype(F32)


def gather_small(seat, value):
    for bit, at in ((2, seat.side), (1, seat.core)):
        other = swapped(value, "rows", bit)
        value = jnp.concatenate(
            [jnp.where(at == 0, value, other), jnp.where(at == 0, other, value)]
        )
    return value


def body_by_slots(
    ancestor,
    panel_below,
    panel_beside,
    inverse_lower,
    inverse_upper,
    list_below,
    list_beside,
    second_below,
    second_beside,
    linked_below,
    linked_beside,
    second_lower,
    second_upper,
    blocks_below,
    blocks_beside,
):
    seat = Seat()
    tile_rows, tile_cols = ancestor.shape
    block_count = tile_rows // BLK
    width = inverse_lower.shape[0]
    half = width // 2
    listed = list_below.shape[0]
    depth = seat.depth
    rows = 4 * depth
    pairs = 2 * depth
    at_first = seat.col == 0

    def either(first, second):
        return jnp.where(at_first, first, second)

    beside = mm_rows(either(panel_beside, second_beside), either(inverse_upper, second_upper))
    pieces = spread(beside.astype(BF16), depth)
    below = mm(either(panel_below, second_below), either(inverse_lower, second_lower))
    panels = lax.all_gather(below.astype(BF16), ("cols", "rows"), axis=0, tiled=True)
    link_below = mm(linked_below, second_lower).astype(BF16)
    link_beside = mm_rows(linked_beside, second_upper).astype(BF16)

    local, meta, *tables = plan_slots(
        seat.row, seat.col, list_beside, blocks_beside, block_count, rows
    )
    count = meta[0]
    order = [sorted(range(depth), key=lambda d: (-abs(d - z), d)) for z in range(depth)]
    place = [[order[z].index(d) for d in range(depth)] for z in range(depth)]
    order_table = jnp.array(order, jnp.int32)
    targets = [order_table[seat.level, turn] for turn in range(depth)]

    def own(matrix):
        return lax.dynamic_slice_in_dim(matrix, seat.col * half, half, 1)

    base = mm(inverse_upper, inverse_lower).astype(BF16)
    base_link = mm(base, own(link_below))
    added = jnp.concatenate(
        [
            mm(inverse_upper, own(inverse_lower)),
            -base_link,
            mm(second_upper, own(second_lower)) + mm_first(link_beside, base_link.astype(BF16)),
        ],
        axis=1,
    )
    added = lax.dynamic_slice_in_dim(
        added, (seat.core * 2 + seat.side) * (width // 4), width // 4, 0
    )

    columns = jnp.stack([target * 2 + 1 - seat.side for target in targets])
    passed = swapped(pack(ancestor, local, columns, pairs, pieces[:1]), "rows", 1)
    arrived = []

    def send(turn, first):
        merged = merge(ancestor, passed, local, meta, columns[turn], turn, pairs, first)
        arrived.append(swapped(merged, "rows", 2))
        return merged

    merged = []
    for turn in range(depth):
        merged = [send(turn, merged)]
    placed = place_slots(pieces, link_beside, tables, merged)

    def strip(turn, part, added, first):
        pair = targets[turn] * 2 + seat.side
        return slots_product(
            ancestor, placed, arrived[turn], local, count, pair * 2 + part, part, rows,
            added, first,
        )

    def far_strip(turn, first):
        return strip(turn, 1 - seat.core, [], first)

    def near_strip(turn, far, first):
        return strip(turn, seat.core, [swapped(far, "rows", 1)], first)

    def moved(values, step):
        gap = depth - 1 - step
        ways = []
        for way in (1, -1):
            senders = [z for z in range(depth) if 0 <= z + way * gap < depth]
            ways.append([(z * 4 + i, (z + way) * 4 + i) for z in senders for i in range(4)])
        if step == 0:
            return [lax.ppermute(values[0], "rows", ways[0] + ways[1])]
        return [lax.ppermute(value, "rows", way) for value, way in zip(values, ways)]

    def next_step(step, layer, moving, first):
        gap = depth - 1 - step
        which = [
            [place[z][z + way * gap] if 0 <= z + way * gap < depth else 0 for z in range(depth)]
            for way in (1, -1)
        ]
        options = 1 + max(max(each) for each in which)
        which = jnp.array(which, jnp.int32)[:, seat.level]
        takes = jnp.ones((2,), jnp.int32)
        if len(moving) == 1:
            takes = jnp.stack([seat.level == 1, seat.level == depth - 2]).astype(jnp.int32)
        which = jnp.concatenate([which, takes])
        return level_step(layer[:options], which, [moving[0], moving[-1]], first)

    far = far_strip(0, [])
    layer = [near_strip(0, far, [])]
    moving = moved([layer[0]] * 2, 0)
    far = far_strip(1, layer[:1])
    layer.append(near_strip(1, far, []))
    given, kept = lower_slots(
        ancestor, panels, link_below, list_below, blocks_below,
        seat.col * (tile_cols // BLK), seat.col, layer[-1:],
    )
    given_sums, kept_sums = small_sums(placed, (given, kept), local, count, [])
    got_sums = swapped(given_sums, "cols", 1)
    stepped = next_step(1, layer, moving, [given_sums])
    moving = moved(stepped, 1)
    far = far_strip(2, stepped[:1])
    layer.append(near_strip(2, far, []))
    sums = split_sum(kept_sums, got_sums, seat.core, 2, layer[-1:])
    sums = split_sum(sums[0], swapped(sums[1], "rows", 1), seat.side, 2, [])
    mine = pair_sum([sums[0], swapped(sums[1], "rows", 2)], [])
    for step in range(2, depth - 1):
        stepped = next_step(step, layer, moving, [mine])
        moving = moved(stepped, step)
        far = far_strip(step + 1, stepped[:1])
        layer.append(near_strip(step + 1, far, []))
    bits = (depth - 1).bit_length()
    for bit in range(bits):
        base_now = [added] if bit == bits - 1 else []
        mine = pair_sum(
            [mine, swapped(mine, "rows", 4 << bit)] + base_now, [] if bit else stepped[:1]
        )
    whole = gather_small(seat, mine)

    given = jnp.where(got_sums[0, 0] == got_sums[0, 0], given, jnp.zeros_like(given))
    piece = kept.astype(F32) + swapped(given, "cols", 1).astype(F32)
    new_lower = piece[:, :half].astype(BF16)
    next_lower = piece[:, half:].astype(BF16)
    link_part = whole[:, half : 2 * half]
    link_other = swapped(link_part, "cols", 1)
    next_link = jnp.concatenate(
        [either(link_part, link_other), either(link_other, link_part)], axis=1
    )

    def with_rest(own, up, down):
        own_at = jnp.arange(block_count, dtype=jnp.int32)
        slot_dropped = jnp.logical_and(
            own_at < count, own_at >= 2 * SLOTS - jnp.minimum(meta[1], SLOTS)
        )
        dropped = jnp.any(
            jnp.logical_and(slot_dropped[:, None], local[:, None] == own_at[None, :]), axis=0
        )
        places = spread_place(seat, listed, 0), spread_place(seat, listed, 1)
        total = own.astype(F32) + up.astype(F32) + down.astype(F32)
        total = total + left_over(
            seat, ancestor, pieces, link_beside, (list_beside, blocks_beside), places, dropped,
        )
        return total[:width].T.astype(BF16), total[width:].T.astype(BF16)

    def without_rest(own, up, down):
        return last_sum(own, up, down, [next_link, new_lower])

    new_upper, next_upper = lax.cond(
        meta[2] > 2 * SLOTS, with_rest, without_rest, layer[-1], *moving
    )
    return (
        new_lower, new_upper, whole[:, :half], next_lower, next_upper, next_link,
        whole[:, 2 * half :],
    )


def body(*arrays):
    ancestor, panel, list_beside = arrays[0], arrays[1], arrays[6]
    rows, cols = lax.axis_size("rows"), lax.axis_size("cols")
    by_slots = (
        cols == 2
        and rows % 4 == 0
        and rows >= 16
        and rows & (rows - 1) == 0
        and panel.shape[0] == BLK
        and list_beside.shape[0] == rows
        and ancestor.shape[0] % BLK == 0
        and ancestor.shape[0] // BLK >= 2 * SLOTS
        and ancestor.shape[0] // BLK % SLOTS == 0
        and ancestor.shape[1] % (rows * BLK) == 0
        and panel.shape[1] % (2 * rows) == 0
    )
    return (body_by_slots if by_slots else body_general)(*arrays)


def solution(mesh):
    return jax.shard_map(
        body,
        mesh=mesh,
        in_specs=(
            P("rows", "cols"),
            P("rows", None),
            P("rows", None),
            P(),
            P(),
            P(),
            P(),
            P("rows", None),
            P("rows", None),
            P(),
            P(),
            P(),
            P(),
            P(),
            P(),
        ),
        out_specs=(
            P("rows", "cols"),
            P(("cols", "rows"), None),
            P(None, "cols"),
            P("rows", "cols"),
            P(("cols", "rows"), None),
            P(),
            P(None, "cols"),
        ),
        check_vma=False,
    )
```

```python
import functools

import jax
import jax.numpy as jnp
from jax import lax
from jax.experimental import pallas as pl
from jax.experimental.pallas import tpu as pltpu
from jax.sharding import PartitionSpec as P

BLK = 128
F32 = jnp.float32
BF16 = jnp.bfloat16


def mm(left, right):
    return jnp.dot(left, right, preferred_element_type=F32)


def mm_rows(left, right):
    return lax.dot_general(left, right, (((1,), (1,)), ((), ())), preferred_element_type=F32)


def mm_first(left, right):
    return lax.dot_general(left, right, (((0,), (0,)), ((), ())), preferred_element_type=F32)


def largest_tile(size, limit):
    tile = min(limit, size)
    while size % tile:
        tile -= BLK
    return tile


def gather_pair(first, second, product):
    cols = lax.axis_size("cols")
    if cols == 2:
        at_first = lax.axis_index("cols") == 0
        mine = product(
            jnp.where(at_first, first[0], second[0]), jnp.where(at_first, first[1], second[1])
        ).astype(BF16)
        return lax.all_gather(mine, ("cols", "rows"), axis=0, tiled=True)
    return jnp.concatenate(
        [
            lax.all_gather(product(*each).astype(BF16), "rows", axis=0, tiled=True)
            for each in (first, second)
        ]
    )


def place_body(pos1, in1, pos2, in2, u1_ref, u2_ref, link_ref, out_ref):
    at = pl.program_id(0)
    width = u1_ref.shape[1]
    keep1 = in1[at].astype(F32)
    keep2 = in2[at].astype(F32)
    u1 = u1_ref[...]
    linked = mm(u1, link_ref[...])
    out_ref[:width, :] = (-u1.astype(F32) * keep1).T.astype(BF16)
    out_ref[width:, :] = (linked * keep1 - u2_ref[...].astype(F32) * keep2).T.astype(BF16)


def blocks_in_tile(blocks, first_block, block_count):
    ids = first_block + jnp.arange(block_count, dtype=jnp.int32)
    matches = ids[:, None] == blocks[None, :]
    places = jnp.sum(
        jnp.where(matches, jnp.arange(blocks.shape[0], dtype=jnp.int32)[None, :], 0), axis=1
    )
    return places.astype(jnp.int32), jnp.any(matches, axis=1).astype(jnp.int32)


def rows_onto(panel, blocks, first_row, row_count):
    global_rows = first_row + jnp.arange(row_count, dtype=jnp.int32)
    matches = (global_rows // BLK)[:, None] == blocks[None, :]
    places = jnp.sum(
        jnp.where(matches, jnp.arange(blocks.shape[0], dtype=jnp.int32)[None, :], 0), axis=1
    )
    picked = jnp.take(panel, places * BLK + global_rows % BLK, axis=0)
    return jnp.where(jnp.any(matches, axis=1)[:, None], picked, jnp.zeros_like(picked))


def place_panels(both, link, list1, list2, first_row, row_count):
    width = both.shape[1]
    listed = list1.shape[0]
    if row_count % BLK:
        u1 = rows_onto(both[: listed * BLK], list1, first_row, row_count)
        u2 = rows_onto(both[listed * BLK :], list2, first_row, row_count)
        joined = jnp.concatenate([-u1.astype(F32), mm(u1, link) - u2.astype(F32)], axis=1)
        return joined.T.astype(BF16)
    first_block = first_row // BLK
    block_count = row_count // BLK
    pos1, in1 = blocks_in_tile(list1, first_block, block_count)
    pos2, in2 = blocks_in_tile(list2, first_block, block_count)
    return pl.pallas_call(
        place_body,
        out_shape=jax.ShapeDtypeStruct((2 * width, block_count * BLK), BF16),
        grid_spec=pltpu.PrefetchScalarGridSpec(
            num_scalar_prefetch=4,
            grid=(block_count,),
            in_specs=[
                pl.BlockSpec((BLK, width), lambda b, p1, i1, p2, i2: (p1[b], 0)),
                pl.BlockSpec((BLK, width), lambda b, p1, i1, p2, i2: (listed + p2[b], 0)),
                pl.BlockSpec((width, width), lambda b, p1, i1, p2, i2: (0, 0)),
            ],
            out_specs=pl.BlockSpec((2 * width, BLK), lambda b, p1, i1, p2, i2: (0, b)),
        ),
        compiler_params=pltpu.CompilerParams(vmem_limit_bytes=24 * 2**20),
        cost_estimate=pl.CostEstimate(
            flops=2 * block_count * BLK * width * width,
            bytes_accessed=8 * block_count * BLK * width,
            transcendentals=0,
        ),
        name="place_panels",
    )(pos1, in1, pos2, in2, both, both, link)


def lower_body(listed, loc1, in1, loc2, in2, part, *refs):
    tiles1, tiles2 = refs[:listed], refs[listed : 2 * listed]
    l1_ref, v1_ref, l2_ref, out_ref = refs[2 * listed :]
    half = l1_ref.shape[1]
    picked1 = jnp.concatenate(
        [tiles1[k][...] * in1[k].astype(F32).astype(BF16) for k in range(listed)], axis=1
    )
    picked2 = jnp.concatenate(
        [tiles2[k][...] * in2[k].astype(F32).astype(BF16) for k in range(listed)], axis=1
    )
    out_ref[:, :half] = (-mm(picked1, l1_ref[...])).astype(BF16)
    out_ref[:, half:] = (mm(picked1, v1_ref[...]) - mm(picked2, l2_ref[...])).astype(BF16)


def lower_partial(ancestor, both, linked, list1, list2, first_block, part, parts):
    rows, columns = ancestor.shape
    width = both.shape[1]
    half = width // parts
    listed = list1.shape[0]
    depth = listed * BLK
    block_count = columns // BLK
    tile = largest_tile(rows, 512)

    def local(blocks):
        at = blocks - first_block
        inside = jnp.logical_and(at >= 0, at < block_count)
        return jnp.clip(at, 0, block_count - 1), inside.astype(jnp.int32)

    loc1, in1 = local(list1)
    loc2, in2 = local(list2)
    specs = [
        pl.BlockSpec((tile, BLK), functools.partial(lambda k, i, l1, i1, l2, i2, p: (i, l1[k]), k))
        for k in range(listed)
    ] + [
        pl.BlockSpec((tile, BLK), functools.partial(lambda k, i, l1, i1, l2, i2, p: (i, l2[k]), k))
        for k in range(listed)
    ]
    specs += [
        pl.BlockSpec((depth, half), lambda i, l1, i1, l2, i2, p: (0, p[0])),
        pl.BlockSpec((depth, half), lambda i, l1, i1, l2, i2, p: (0, p[0])),
        pl.BlockSpec((depth, half), lambda i, l1, i1, l2, i2, p: (1, p[0])),
    ]
    return pl.pallas_call(
        functools.partial(lower_body, listed),
        out_shape=jax.ShapeDtypeStruct((rows, 2 * half), BF16),
        grid_spec=pltpu.PrefetchScalarGridSpec(
            num_scalar_prefetch=5,
            grid=(rows // tile,),
            in_specs=specs,
            out_specs=pl.BlockSpec((tile, 2 * half), lambda i, l1, i1, l2, i2, p: (i, 0)),
        ),
        compiler_params=pltpu.CompilerParams(vmem_limit_bytes=40 * 2**20),
        cost_estimate=pl.CostEstimate(
            flops=6 * rows * depth * half,
            bytes_accessed=4 * rows * depth + 6 * depth * half,
            transcendentals=0,
        ),
        name="lower_partial",
    )(
        loc1, in1, loc2, in2, jnp.reshape(part, (1,)).astype(jnp.int32),
        *([ancestor] * (2 * listed)), both, linked, both,
    )


def strip_body(strip, w_ref, a_ref, *refs):
    total = mm(w_ref[...], a_ref[...])
    for ref in refs[:-1]:
        total = total + ref[...].astype(F32)
    refs[-1][...] = total.astype(BF16)


def strip_product(ancestor, placed, strip, strips, *added):
    rows, columns = ancestor.shape
    strip_width = columns // strips
    height = placed.shape[0]
    if strip_width % BLK:
        total = mm(
            placed, lax.dynamic_slice_in_dim(ancestor, strip * strip_width, strip_width, 1)
        )
        for each in added:
            total = total + each.astype(F32)
        return total.astype(BF16)
    tile = largest_tile(strip_width, 256)
    per = strip_width // tile
    return pl.pallas_call(
        strip_body,
        out_shape=jax.ShapeDtypeStruct((height, strip_width), BF16),
        grid_spec=pltpu.PrefetchScalarGridSpec(
            num_scalar_prefetch=1,
            grid=(per,),
            in_specs=[
                pl.BlockSpec((height, rows), lambda j, s: (0, 0)),
                pl.BlockSpec((rows, tile), lambda j, s: (0, s[0] * per + j)),
            ]
            + [pl.BlockSpec((height, tile), lambda j, s: (0, j))] * len(added),
            out_specs=pl.BlockSpec((height, tile), lambda j, s: (0, j)),
        ),
        compiler_params=pltpu.CompilerParams(vmem_limit_bytes=40 * 2**20),
        cost_estimate=pl.CostEstimate(
            flops=2 * height * rows * strip_width,
            bytes_accessed=2 * (rows * strip_width + height * rows)
            + 2 * (1 + len(added)) * height * strip_width,
            transcendentals=0,
        ),
        name="strip_product",
    )(jnp.reshape(strip, (1,)).astype(jnp.int32), placed, ancestor, *added)


def add_pair(left, right):
    return (left.astype(F32) + right.astype(F32)).astype(BF16)


def upper_sums(ancestor, placed):
    strips = lax.axis_size("rows")
    row_at = lax.axis_index("rows")
    inner = 4 if strips % 4 == 0 else 1
    if inner == 1:
        whole = strip_product(ancestor, placed, 0, 1)
        return lax.psum_scatter(whole.astype(F32), "rows", scatter_dimension=1, tiled=True)
    depth = strips // inner
    core, side, level = row_at % 2, (row_at // 2) % 2, row_at // 4
    to_core = [(i, i ^ 1) for i in range(strips)]
    to_side = [(i, i ^ 2) for i in range(strips)]
    order = [sorted(range(depth), key=lambda d: (-abs(d - z), d)) for z in range(depth)]
    place = [[order[z].index(d) for d in range(depth)] for z in range(depth)]
    order_table = jnp.array(order, jnp.int32)

    def strip_of(target, x, c):
        return (target * 2 + x) * 2 + c

    layer = []
    for turn in range(depth):
        target = order_table[level, turn]
        far = strip_product(ancestor, placed, strip_of(target, 1 - side, 1 - core), strips)
        far = lax.ppermute(far, "rows", to_core)
        near = strip_product(ancestor, placed, strip_of(target, side, 1 - core), strips)
        near = lax.ppermute(near, "rows", to_core)
        far = strip_product(ancestor, placed, strip_of(target, 1 - side, core), strips, far)
        far = lax.ppermute(far, "rows", to_side)
        layer.append(
            strip_product(ancestor, placed, strip_of(target, side, core), strips, near, far)
        )

    def own_part(step, way):
        gap = depth - 1 - step
        chosen = None
        for z in range(depth):
            target = z + way * gap
            if 0 <= target < depth:
                value = layer[place[z][target]]
                chosen = value if chosen is None else jnp.where(level == z, value, chosen)
        return chosen

    arrived = {1: None, -1: None}
    for step in range(depth - 1):
        gap = depth - 1 - step
        for way in (1, -1):
            senders = [z for z in range(depth) if 0 <= z + way * gap < depth]
            pairs = [
                (z * inner + i, (z + way) * inner + i) for z in senders for i in range(inner)
            ]
            value = own_part(step, way)
            if arrived[way] is not None:
                value = add_pair(value, arrived[way])
            arrived[way] = lax.ppermute(value, "rows", pairs)
    total = layer[-1].astype(F32)
    for way in (1, -1):
        if arrived[way] is not None:
            total = total + arrived[way].astype(F32)
    return total


def body_general(
    ancestor,
    panel_below,
    panel_beside,
    inverse_lower,
    inverse_upper,
    list_below,
    list_beside,
    second_below,
    second_beside,
    linked_below,
    linked_beside,
    second_lower,
    second_upper,
    blocks_below,
    blocks_beside,
):
    row_at = lax.axis_index("rows")
    col_at = lax.axis_index("cols")
    cols = lax.axis_size("cols")
    tile_rows, tile_cols = ancestor.shape
    width = inverse_lower.shape[0]
    half = width // cols

    beside = gather_pair((panel_beside, inverse_upper), (second_beside, second_upper), mm_rows)
    below = gather_pair((panel_below, inverse_lower), (second_below, second_lower), mm)
    link_below = mm(linked_below, second_lower).astype(BF16)
    link_beside = mm_rows(linked_beside, second_upper).astype(BF16)

    placed = place_panels(
        beside, link_beside, list_beside, blocks_beside,
        row_at * tile_rows, tile_rows,
    )
    upper = upper_sums(ancestor, placed)
    new_upper = upper[:width].T.astype(BF16)
    next_upper = upper[width:].T.astype(BF16)

    depth = below.shape[0] // 2
    linked = mm(below[:depth], link_below).astype(BF16)
    lower_total = None
    sums_total = None
    for shift in reversed(range(cols)):
        part = (col_at + shift) % cols
        piece = lower_partial(
            ancestor, below, linked, list_below, blocks_below,
            col_at * (tile_cols // BLK), part, cols,
        )
        sums = jnp.concatenate(
            [mm(placed[:width], piece), mm(placed[width:], piece[:, half:])], axis=1
        )
        if shift:
            pairs = [(i, (i + shift) % cols) for i in range(cols)]
            piece = lax.ppermute(piece, "cols", pairs)
            sums = lax.ppermute(sums, "cols", pairs)
        piece = piece.astype(F32)
        lower_total = piece if lower_total is None else lower_total + piece
        sums_total = sums if sums_total is None else sums_total + sums
    new_lower = lower_total[:, :half].astype(BF16)
    next_lower = lower_total[:, half:].astype(BF16)

    sums = lax.psum(sums_total, "rows")

    def own(matrix):
        return lax.dynamic_slice_in_dim(matrix, col_at * half, half, 1)

    base = mm(inverse_upper, inverse_lower).astype(BF16)
    base_link = mm(base, own(link_below))
    new_diagonal = (mm(inverse_upper, own(inverse_lower)) + sums[:, :half]).astype(BF16)
    link_part = (sums[:, half : 2 * half] - base_link).astype(BF16)
    next_link = lax.all_gather(link_part, "cols", axis=1, tiled=True)
    next_diagonal = (
        mm(second_upper, own(second_lower))
        + mm_first(link_beside, base_link.astype(BF16))
        + sums[:, 2 * half :]
    ).astype(BF16)
    return (new_lower, new_upper, new_diagonal, next_lower, next_upper, next_link, next_diagonal)


SLOTS = 4
FREE = pl.CostEstimate(flops=0, bytes_accessed=0, transcendentals=0)
ANY = pl.BlockSpec(memory_space=pl.ANY)
SCALARS = pl.BlockSpec(memory_space=pltpu.SMEM)


def swapped(value, axis, bit):
    size = lax.axis_size(axis)
    return lax.ppermute(value, axis, [(i, i ^ bit) for i in range(size)])


def from_levels(value, shift):
    size = lax.axis_size("rows")
    return lax.ppermute(value, "rows", [(i, (i + 4 * shift) % size) for i in range(size)])


class Seat:
    def __init__(self):
        row_at = lax.axis_index("rows")
        self.row = row_at
        self.core, self.side, self.level = row_at % 2, (row_at // 2) % 2, row_at // 4
        self.depth = lax.axis_size("rows") // 4
        self.col = lax.axis_index("cols")


def spread(item, depth):
    pair = jnp.concatenate([item, swapped(item, "rows", 2)])
    near = [pair] + [from_levels(pair, shift) for shift in range(1, depth)]
    beyond = [swapped(each, "cols", 1) for each in near]
    return (
        near + [swapped(each, "rows", 1) for each in near]
        + beyond + [swapped(each, "rows", 1) for each in beyond]
    )


def spread_place(seat, listed, which):
    at = jnp.arange(listed, dtype=jnp.int32)
    core, side, level = at % 2, (at // 2) % 2, at // 4
    apart = (seat.col ^ which) * 2 + (seat.core ^ core)
    return (apart * seat.depth + (seat.level - level) % seat.depth) * 2 + (seat.side ^ side)


def plan_body(block_count, row, l1, l2, local, meta, b1, m1, b2, m2, at1, at2):
    listed = l1.shape[0]
    tiles = at1.shape[0] // block_count
    depth = listed // 4
    own, column = row[0], row[1]

    def place_of(k, which):
        apart = (own >> 2) - (k >> 2)
        apart = jnp.where(apart < 0, apart + depth, apart)
        half = (column ^ which) * 2 + ((own ^ k) & 1)
        return (half * depth + apart) * 2 + (((own ^ k) >> 1) & 1)

    @pl.loop(0, at1.shape[0])
    def _(i):
        at1[i] = 0
        at2[i] = 0

    @pl.loop(0, listed)
    def _(k):
        at1[l1[k]] = k + 1
        at2[l2[k]] = k + 1

    @pl.loop(0, b1.shape[0])
    def _(s):
        b1[s] = 0
        m1[s] = 0
        b2[s] = 0
        m2[s] = 0

    def scan(tile, put):
        def step(b, rank):
            g = tile * block_count + b
            here = jnp.where(at1[g] + at2[g] > 0, 1, 0)
            put(rank, b, g, here)
            return rank + here

        return lax.fori_loop(0, block_count, step, jnp.int32(0))

    def place(slot, g):
        b1[slot] = place_of(jnp.maximum(at1[g] - 1, 0), 0)
        m1[slot] = jnp.where(at1[g] > 0, 1, 0)
        b2[slot] = place_of(jnp.maximum(at2[g] - 1, 0), 1)
        m2[slot] = jnp.where(at2[g] > 0, 1, 0)

    def put_own(rank, b, g, here):
        local[rank] = b
        place(SLOTS + rank, g)

    def put_facing(rank, b, g, here):
        @pl.when(jnp.logical_and(here > 0, rank < SLOTS))
        def _():
            place(rank, g)

    def nothing(rank, b, g, here):
        return None

    @pl.loop(0, block_count)
    def _(s):
        local[s] = 0

    meta[0] = scan(own, put_own)
    meta[1] = scan(own ^ 1, nothing)
    facing = scan(own ^ 2, put_facing)

    def put_beyond(rank, b, g, here):
        slot = facing + rank - SLOTS

        @pl.when(jnp.logical_and(here > 0, jnp.logical_and(rank >= SLOTS, slot < SLOTS)))
        def _():
            place(slot, g)

    scan(own ^ 3, put_beyond)

    def most(chip, found):
        count = scan(2 * chip, nothing) + scan(2 * chip + 1, nothing)
        return jnp.maximum(found, count)

    meta[2] = lax.fori_loop(0, tiles // 2, most, jnp.int32(0))


def plan_slots(row, column, list1, list2, block_count, tiles):
    def numbers(count):
        return jax.ShapeDtypeStruct((count,), jnp.int32)

    slots = SLOTS + block_count
    return pl.pallas_call(
        functools.partial(plan_body, block_count),
        out_shape=(numbers(block_count), numbers(3)) + (numbers(slots),) * 4,
        in_specs=[SCALARS] * 3,
        out_specs=(SCALARS,) * 6,
        scratch_shapes=[pltpu.SMEM((tiles * block_count,), jnp.int32)] * 2,
        name="plan_slots",
    )(jnp.stack([row, column]).astype(jnp.int32), list1, list2)


def place_slots_body(count, b1, m1, b2, m2, link_ref, *refs):
    pieces = refs[:count]
    out_ref, got, sems = refs[-3:]
    width = link_ref.shape[0]
    slots = b1.shape[0]

    def start(s, which, block):
        row = pl.multiple_of((block[s] & 1) * BLK, BLK)
        for group in range(0, count, 4):

            @pl.when(block[s] >> 3 == group // 4)
            def _():
                for at in range(group, group + 4):

                    @pl.when(block[s] >> 1 == at)
                    def _():
                        pltpu.make_async_copy(
                            pieces[at].at[pl.ds(row, BLK), :],
                            got.at[which, s],
                            sems.at[which, s],
                        ).start()

    @pl.loop(0, slots)
    def _(s):
        for which, (block, used) in enumerate(((b1, m1), (b2, m2))):

            @pl.when(used[s] > 0)
            def _():
                start(s, which, block)

    def wait(s, which, used):
        @pl.when(used[s] > 0)
        def _():
            pltpu.make_async_copy(
                pieces[0].at[pl.ds(0, BLK), :], got.at[which, s], sems.at[which, s]
            ).wait()

    for s in range(slots):
        columns = pl.ds(s * BLK, BLK)
        used = m1[s] + m2[s] > 0

        @pl.when(used)
        def _():
            wait(s, 0, m1)
            wait(s, 1, m2)
            u1 = jnp.where(m1[s] > 0, got[0, s].astype(F32), 0.0)
            u2 = jnp.where(m2[s] > 0, got[1, s].astype(F32), 0.0)
            linked = mm(u1.astype(BF16), link_ref[...])
            out_ref[:width, columns] = (-u1).T.astype(BF16)
            out_ref[width:, columns] = (linked - u2).T.astype(BF16)

        @pl.when(jnp.logical_not(used))
        def _():
            out_ref[:, columns] = jnp.zeros((2 * width, BLK), BF16)


def place_slots(pieces, link, tables, first):
    width = link.shape[0]
    slots = tables[0].shape[0]
    vmem = pl.BlockSpec(memory_space=pltpu.VMEM)
    return pl.pallas_call(
        functools.partial(place_slots_body, len(pieces)),
        out_shape=jax.ShapeDtypeStruct((2 * width, slots * BLK), BF16),
        in_specs=[SCALARS] * 4 + [vmem] + [ANY] * (len(pieces) + len(first)),
        out_specs=vmem,
        scratch_shapes=[
            pltpu.VMEM((2, slots, BLK, width), BF16),
            pltpu.SemaphoreType.DMA((2, slots)),
        ],
        compiler_params=pltpu.CompilerParams(vmem_limit_bytes=56 * 2**20),
        cost_estimate=FREE,
        name="place_slots",
    )(*tables, link, *pieces, *first)


def pack_body(local, pair, a_ref, *refs):
    refs[-1][...] = a_ref[...]


def pack(ancestor, local, columns, pairs, first):
    wide = ancestor.shape[1] // pairs
    turns = columns.shape[0]
    return pl.pallas_call(
        pack_body,
        out_shape=jax.ShapeDtypeStruct((SLOTS * BLK, turns * wide), BF16),
        grid_spec=pltpu.PrefetchScalarGridSpec(
            num_scalar_prefetch=2,
            grid=(turns, SLOTS),
            in_specs=[pl.BlockSpec((BLK, wide), lambda t, s, l, p: (l[SLOTS + s], p[t]))]
            + [ANY] * len(first),
            out_specs=pl.BlockSpec((BLK, wide), lambda t, s, l, p: (s, t)),
        ),
        cost_estimate=FREE,
        name="pack_slots",
    )(local, columns, ancestor, *first)


def merge_body(local, meta, columns, a_ref, got_ref, *refs):
    mine = pl.program_id(1) < meta[0]
    half = pl.num_programs(0) // 2
    for first, out_ref in ((True, refs[-2]), (False, refs[-1])):
        here = (pl.program_id(0) < half) == first

        @pl.when(jnp.logical_and(here, mine))
        def _():
            out_ref[...] = a_ref[...]

        @pl.when(jnp.logical_and(here, jnp.logical_not(mine)))
        def _():
            out_ref[...] = got_ref[...]


def merge(ancestor, got, local, meta, columns, pairs):
    wide = ancestor.shape[1] // pairs
    turns = columns.shape[0]
    half = turns // 2
    shape = jax.ShapeDtypeStruct((SLOTS * BLK, half * wide), BF16)
    return pl.pallas_call(
        merge_body,
        out_shape=(shape, shape),
        grid_spec=pltpu.PrefetchScalarGridSpec(
            num_scalar_prefetch=3,
            grid=(turns, SLOTS),
            in_specs=[
                pl.BlockSpec((BLK, wide), lambda t, s, l, n, p: (l[s], p[t])),
                pl.BlockSpec(
                    (BLK, wide), lambda t, s, l, n, p: (jnp.clip(s - n[0], 0, SLOTS - 1), t)
                ),
            ],
            out_specs=(
                pl.BlockSpec(
                    (BLK, wide),
                    lambda t, s, l, n, p: (
                        jnp.where(t < half, s, SLOTS - 1), jnp.minimum(t, half - 1)
                    ),
                ),
                pl.BlockSpec(
                    (BLK, wide),
                    lambda t, s, l, n, p: (
                        jnp.where(t < half, 0, s), jnp.maximum(t - half, 0)
                    ),
                ),
            ),
        ),
        compiler_params=pltpu.CompilerParams(vmem_limit_bytes=56 * 2**20),
        cost_estimate=FREE,
        name="merge_slots",
    )(local, meta, columns, ancestor, got)


def lower_slots_body(groups, block_count, l1, l2, at, *refs):
    listed = groups * SLOTS
    tiles = (refs[:listed], refs[listed : 2 * listed])
    panel_refs, link_ref = refs[2 * listed : 2 * listed + 2], refs[2 * listed + 2]
    given_ref, kept_ref, linked_ref, total_ref = refs[-4:]
    width = link_ref.shape[0]
    half = width // 2

    @pl.when(pl.program_id(0) == 0)
    def _():
        linked_ref[...] = mm(panel_refs[0][...], link_ref[...]).astype(BF16)

    def picked(which, blocks):
        kept = []
        for k in range(listed):
            place = blocks[k] - at[0]
            inside = jnp.logical_and(place >= 0, place < block_count)
            kept.append(tiles[which][k][...] * jnp.where(inside, 1.0, 0.0).astype(BF16))
        return jnp.concatenate(kept, axis=1)

    picked1 = picked(0, l1)
    total_ref[:, :width] = -mm(picked1, panel_refs[0][...])
    second = mm(picked1, linked_ref[...]) - mm(picked(1, l2), panel_refs[1][...])
    total_ref[:, width:] = second

    for column, (own, other) in ((0, (kept_ref, given_ref)), (1, (given_ref, kept_ref))):

        @pl.when(at[1] == column)
        def _():
            for out, start in ((own, 0), (other, half)):
                out[:, :half] = total_ref[:, start : start + half].astype(BF16)
                second = total_ref[:, width + start : width + start + half]
                out[:, half:] = second.astype(BF16)


def lower_slots(ancestor, panels, link, list1, list2, first_block, column, first):
    rows, columns = ancestor.shape
    listed, width = list1.shape[0], link.shape[0]
    block_count = columns // BLK
    tile = largest_tile(rows, 512)
    at = jnp.stack([first_block, column]).astype(jnp.int32)

    def picked(which, k):
        def index(i, l1, l2, at):
            place = (l1, l2)[which][k] - at[0]
            inside = jnp.logical_and(place >= 0, place < block_count)
            return jnp.where(inside, i, 0), jnp.clip(place, 0, block_count - 1)

        return pl.BlockSpec((tile, BLK), index)

    specs = [picked(which, k) for which in (0, 1) for k in range(listed)]
    specs += [
        pl.BlockSpec((listed * BLK, width), lambda i, l1, l2, at: (0, 0)),
        pl.BlockSpec((listed * BLK, width), lambda i, l1, l2, at: (1, 0)),
        pl.BlockSpec((width, width), lambda i, l1, l2, at: (0, 0)),
    ]
    shape = jax.ShapeDtypeStruct((rows, width), BF16)
    return pl.pallas_call(
        functools.partial(lower_slots_body, listed // SLOTS, block_count),
        out_shape=(shape, shape),
        grid_spec=pltpu.PrefetchScalarGridSpec(
            num_scalar_prefetch=3,
            grid=(rows // tile,),
            in_specs=specs + [ANY] * len(first),
            out_specs=(pl.BlockSpec((tile, width), lambda i, l1, l2, at: (i, 0)),) * 2,
            scratch_shapes=[
                pltpu.VMEM((listed * BLK, width), BF16),
                pltpu.VMEM((tile, 2 * width), F32),
            ],
        ),
        compiler_params=pltpu.CompilerParams(vmem_limit_bytes=56 * 2**20),
        cost_estimate=FREE,
        name="lower_slots",
    )(list1, list2, at, *([ancestor] * (2 * listed)), panels, panels, link, *first)


def slots_body(adds, local, count, at, w_ref, arrived_ref, *refs):
    tiles = refs[:SLOTS]
    added = refs[SLOTS : SLOTS + adds]
    placed_ref, ancestor_ref = refs[SLOTS + adds : SLOTS + adds + 2]
    out_ref, rest_w, rest_a, sems = refs[-4:]
    first = [arrived_ref[...]] + [ref[...] for ref in tiles]
    total = mm(w_ref[...], jnp.concatenate(first, axis=0))
    for ref in added:
        total = total + ref[...].astype(F32)
    out_ref[...] = total.astype(BF16)

    @pl.when(count[0] > SLOTS)
    def _():
        tile = out_ref.shape[1]
        more = rest_a.shape[0] // BLK
        column = pl.multiple_of((at[0] + pl.program_id(0)) * tile, BLK)
        copies = [
            pltpu.make_async_copy(
                placed_ref.at[:, pl.ds(2 * SLOTS * BLK, more * BLK)], rest_w, sems.at[more]
            )
        ]
        for s in range(more):
            row = pl.multiple_of(local[SLOTS + s] * BLK, BLK)
            copies.append(
                pltpu.make_async_copy(
                    ancestor_ref.at[pl.ds(row, BLK), pl.ds(column, tile)],
                    rest_a.at[pl.ds(s * BLK, BLK), :],
                    sems.at[s],
                )
            )
        for copy in copies:
            copy.start()
        for copy in copies:
            copy.wait()
        again = mm(w_ref[...], jnp.concatenate(first, axis=0))
        again = again + mm(rest_w[...], rest_a[...])
        for ref in added:
            again = again + ref[...].astype(F32)
        out_ref[...] = again.astype(BF16)


def slots_product(
    ancestor, placed, arrived, local, count, strip, within, strips, added, first
):
    columns = ancestor.shape[1]
    strip_width = columns // strips
    height = placed.shape[0]
    tile = largest_tile(strip_width, 384)
    per = strip_width // tile
    more = placed.shape[1] // BLK - 2 * SLOTS
    where_at = jnp.stack([strip * per, within * per]).astype(jnp.int32)

    def own_block(slot):
        return lambda j, l, n, p: (l[slot], p[0] + j)

    return pl.pallas_call(
        functools.partial(slots_body, len(added)),
        out_shape=jax.ShapeDtypeStruct((height, strip_width), BF16),
        grid_spec=pltpu.PrefetchScalarGridSpec(
            num_scalar_prefetch=3,
            grid=(per,),
            in_specs=[pl.BlockSpec((height, 2 * SLOTS * BLK), lambda j, l, n, p: (0, 0))]
            + [pl.BlockSpec((SLOTS * BLK, tile), lambda j, l, n, p: (0, p[1] + j))]
            + [pl.BlockSpec((BLK, tile), own_block(slot)) for slot in range(SLOTS)]
            + [pl.BlockSpec((height, tile), lambda j, l, n, p: (0, j))] * len(added)
            + [ANY] * (2 + len(first)),
            out_specs=pl.BlockSpec((height, tile), lambda j, l, n, p: (0, j)),
            scratch_shapes=[
                pltpu.VMEM((height, more * BLK), BF16),
                pltpu.VMEM((more * BLK, tile), BF16),
                pltpu.SemaphoreType.DMA((more + 1,)),
            ],
        ),
        compiler_params=pltpu.CompilerParams(vmem_limit_bytes=56 * 2**20),
        cost_estimate=FREE,
        name="slots_product",
    )(
        local, jnp.reshape(count, (1,)), where_at, placed, arrived, *([ancestor] * SLOTS),
        *added, placed, ancestor, *first,
    )


def small_sums_body(local, count, w_ref, *refs):
    tiles, outs, totals = refs[: 2 * SLOTS], refs[-4:-2], refs[-2:]
    at = pl.program_id(0)
    width = w_ref.shape[0] // 2
    half = width // 2

    @pl.when(at == 0)
    def _():
        for total in totals:
            total[...] = jnp.zeros_like(total)

    @pl.when(at * SLOTS < count[0])
    def _():
        for which, total in enumerate(totals):
            group = tiles[which * SLOTS : (which + 1) * SLOTS]
            rows = jnp.concatenate([ref[...] for ref in group], axis=0)
            total[:, : 2 * half] += mm(w_ref[:width, :], rows)
            total[:, 2 * half :] += mm(w_ref[width:, :], rows[:, half:])

    @pl.when(at == pl.num_programs(0) - 1)
    def _():
        for out, total in zip(outs, totals):
            out[...] = total[...].astype(BF16)


def small_sums(placed, pieces, local, count, first):
    width = placed.shape[0] // 2
    wide = 3 * width // 2
    slots = local.shape[0]

    def row(k):
        def index(s, l, n):
            return l[jnp.where(s * SLOTS < n[0], s, 0) * SLOTS + k], 0

        return pl.BlockSpec((BLK, width), index)

    shape = jax.ShapeDtypeStruct((width, wide), BF16)
    return pl.pallas_call(
        small_sums_body,
        out_shape=(shape, shape),
        grid_spec=pltpu.PrefetchScalarGridSpec(
            num_scalar_prefetch=2,
            grid=(slots // SLOTS,),
            in_specs=[
                pl.BlockSpec(
                    (2 * width, SLOTS * BLK),
                    lambda s, l, n: (0, 1 + jnp.where(s * SLOTS < n[0], s, 0)),
                )
            ]
            + [row(k) for k in range(SLOTS)] * 2
            + [ANY] * len(first),
            out_specs=(pl.BlockSpec((width, wide), lambda s, l, n: (0, 0)),) * 2,
            scratch_shapes=[pltpu.VMEM((width, wide), F32)] * 2,
        ),
        compiler_params=pltpu.CompilerParams(vmem_limit_bytes=56 * 2**20),
        cost_estimate=FREE,
        name="small_sums",
    )(
        local, jnp.reshape(count, (1,)), placed, *([pieces[0]] * SLOTS),
        *([pieces[1]] * SLOTS), *first,
    )


def step_body(options, which, *refs):
    choices, arrived = refs[:options], refs[options : options + 2]
    outs = refs[-2:]
    for way in (0, 1):
        for option in range(options):

            @pl.when(which[way] == option)
            def _():
                came = arrived[way][...].astype(F32) * which[2 + way].astype(F32)
                outs[way][...] = (choices[option][...].astype(F32) + came).astype(BF16)


def level_step(choices, which, arrived, first):
    height, wide = choices[0].shape
    tile = height // 4
    block = (tile, wide)

    def choice(option):
        def index(i, w):
            return jnp.where(jnp.logical_or(w[0] == option, w[1] == option), i, 0), 0

        return pl.BlockSpec(block, index)

    def whole(i, w):
        return i, 0

    shape = jax.ShapeDtypeStruct((height, wide), BF16)
    return pl.pallas_call(
        functools.partial(step_body, len(choices)),
        out_shape=(shape, shape),
        grid_spec=pltpu.PrefetchScalarGridSpec(
            num_scalar_prefetch=1,
            grid=(height // tile,),
            in_specs=[choice(option) for option in range(len(choices))]
            + [pl.BlockSpec(block, whole)] * 2
            + [ANY] * len(first),
            out_specs=(pl.BlockSpec(block, whole),) * 2,
        ),
        compiler_params=pltpu.CompilerParams(vmem_limit_bytes=56 * 2**20),
        cost_estimate=FREE,
        name="level_step",
    )(which, *choices, *arrived, *first)


def last_body(own_ref, up_ref, down_ref, *refs):
    first_ref, second_ref = refs[-2:]
    width = first_ref.shape[1]
    total = own_ref[...].astype(F32) + up_ref[...].astype(F32) + down_ref[...].astype(F32)
    first_ref[...] = total[:width].T.astype(BF16)
    second_ref[...] = total[width:].T.astype(BF16)


def last_sum(own, up, down, first):
    height, wide = own.shape
    tile = largest_tile(wide, 256)
    width = height // 2
    shape = jax.ShapeDtypeStruct((wide, width), BF16)
    return pl.pallas_call(
        last_body,
        out_shape=(shape, shape),
        grid=(wide // tile,),
        in_specs=[pl.BlockSpec((height, tile), lambda j: (0, j))] * 3 + [ANY] * len(first),
        out_specs=(pl.BlockSpec((tile, width), lambda j: (j, 0)),) * 2,
        compiler_params=pltpu.CompilerParams(vmem_limit_bytes=56 * 2**20),
        cost_estimate=FREE,
        name="last_sum",
    )(own, up, down, *first)


def split_body(parts, at, left_ref, right_ref, *refs):
    outs = refs[-parts:]
    size = outs[0].shape[0]
    for shift in range(parts):
        start = pl.multiple_of(lax.rem(at[0] + shift, parts) * size, 16)
        rows = pl.ds(start, size)
        total = left_ref[rows, :].astype(F32) + right_ref[rows, :].astype(F32)
        outs[shift][...] = total.astype(BF16)


def split_sum(left, right, at, parts, first):
    rows, wide = left.shape
    shape = jax.ShapeDtypeStruct((rows // parts, wide), BF16)
    vmem = pl.BlockSpec(memory_space=pltpu.VMEM)
    return pl.pallas_call(
        functools.partial(split_body, parts),
        out_shape=(shape,) * parts,
        in_specs=[SCALARS, vmem, vmem] + [ANY] * len(first),
        out_specs=(vmem,) * parts,
        compiler_params=pltpu.CompilerParams(vmem_limit_bytes=56 * 2**20),
        cost_estimate=FREE,
        name="split_sum",
    )(jnp.reshape(at, (1,)).astype(jnp.int32), left, right, *first)


def pair_sum(pieces, first):
    vmem = pl.BlockSpec(memory_space=pltpu.VMEM)
    count = len(pieces)

    def kernel(*refs):
        total = refs[0][...].astype(F32)
        for ref in refs[1:count]:
            total = total + ref[...].astype(F32)
        refs[-1][...] = total.astype(BF16)

    return pl.pallas_call(
        kernel,
        out_shape=jax.ShapeDtypeStruct(pieces[0].shape, BF16),
        in_specs=[vmem] * count + [ANY] * len(first),
        out_specs=vmem,
        cost_estimate=FREE,
        name="pair_sum",
    )(*pieces, *first)


def left_over(seat, ancestor, pieces, link, lists, places, dropped):
    block_rows, columns = ancestor.shape
    width = link.shape[0]
    first_row = seat.row * block_rows
    shaped = jnp.concatenate(pieces).reshape(-1, BLK, width)
    u1, u2 = (
        rows_onto(
            jnp.take(shaped, place, axis=0).reshape(-1, width), blocks, first_row, block_rows
        )
        for blocks, place in zip(lists, places)
    )
    joined = jnp.concatenate([-u1.astype(F32), mm(u1, link) - u2.astype(F32)], axis=1)
    joined = jnp.where(jnp.repeat(dropped, BLK)[:, None], joined, 0.0).astype(BF16)
    wide = columns // (2 * seat.depth)
    partial = jnp.concatenate(
        [
            mm_first(
                joined,
                lax.dynamic_slice_in_dim(
                    ancestor, (2 * level + 1 - seat.side) * wide, wide, 1
                ),
            ).astype(BF16)
            for level in range(seat.depth)
        ],
        axis=1,
    )
    groups = [
        [4 * level + 2 * side + core for level in range(seat.depth) for core in range(2)]
        for side in range(2)
    ]
    own = lax.psum_scatter(
        partial, "rows", scatter_dimension=1, axis_index_groups=groups, tiled=True
    )
    return swapped(own, "rows", 2).astype(F32)


def gather_small(seat, value):
    for bit, at in ((2, seat.side), (1, seat.core)):
        other = swapped(value, "rows", bit)
        value = jnp.concatenate(
            [jnp.where(at == 0, value, other), jnp.where(at == 0, other, value)]
        )
    return value


def body_by_slots(
    ancestor,
    panel_below,
    panel_beside,
    inverse_lower,
    inverse_upper,
    list_below,
    list_beside,
    second_below,
    second_beside,
    linked_below,
    linked_beside,
    second_lower,
    second_upper,
    blocks_below,
    blocks_beside,
):
    seat = Seat()
    tile_rows, tile_cols = ancestor.shape
    block_count = tile_rows // BLK
    width = inverse_lower.shape[0]
    half = width // 2
    listed = list_below.shape[0]
    depth = seat.depth
    rows = 4 * depth
    pairs = 2 * depth
    at_first = seat.col == 0

    def either(first, second):
        return jnp.where(at_first, first, second)

    beside = mm_rows(either(panel_beside, second_beside), either(inverse_upper, second_upper))
    pieces = spread(beside.astype(BF16), depth)
    below = mm(either(panel_below, second_below), either(inverse_lower, second_lower))
    panels = lax.all_gather(below.astype(BF16), ("cols", "rows"), axis=0, tiled=True)
    link_below = mm(linked_below, second_lower).astype(BF16)
    link_beside = mm_rows(linked_beside, second_upper).astype(BF16)

    local, meta, *tables = plan_slots(
        seat.row, seat.col, list_beside, blocks_beside, block_count, rows
    )
    count = meta[0]
    order = [sorted(range(depth), key=lambda d: (-abs(d - z), d)) for z in range(depth)]
    place = [[order[z].index(d) for d in range(depth)] for z in range(depth)]
    order_table = jnp.array(order, jnp.int32)
    targets = [order_table[seat.level, turn] for turn in range(depth)]

    def own(matrix):
        return lax.dynamic_slice_in_dim(matrix, seat.col * half, half, 1)

    base = mm(inverse_upper, inverse_lower).astype(BF16)
    base_link = mm(base, own(link_below))
    added = jnp.concatenate(
        [
            mm(inverse_upper, own(inverse_lower)),
            -base_link,
            mm(second_upper, own(second_lower)) + mm_first(link_beside, base_link.astype(BF16)),
        ],
        axis=1,
    )
    added = lax.dynamic_slice_in_dim(
        added, (seat.core * 2 + seat.side) * (width // 4), width // 4, 0
    )

    columns = jnp.stack([target * 2 + 1 - seat.side for target in targets])
    passed = swapped(pack(ancestor, local, columns, pairs, pieces[:1]), "rows", 1)
    leaving = merge(ancestor, passed, local, meta, columns, pairs)
    arrived = [swapped(each, "rows", 2) for each in leaving]
    placed = place_slots(pieces, link_beside, tables, list(leaving))
    turns = depth // 2

    def strip(turn, part, added, first):
        pair = targets[turn] * 2 + seat.side
        return slots_product(
            ancestor, placed, arrived[turn // turns], local, count, pair * 2 + part,
            (turn % turns) * 2 + part, rows, added, first,
        )

    def far_strip(turn, first):
        return strip(turn, 1 - seat.core, [], first)

    def near_strip(turn, far, first):
        return strip(turn, seat.core, [swapped(far, "rows", 1)], first)

    def moved(values, step):
        gap = depth - 1 - step
        ways = []
        for way in (1, -1):
            senders = [z for z in range(depth) if 0 <= z + way * gap < depth]
            ways.append([(z * 4 + i, (z + way) * 4 + i) for z in senders for i in range(4)])
        if step == 0:
            return [lax.ppermute(values[0], "rows", ways[0] + ways[1])]
        return [lax.ppermute(value, "rows", way) for value, way in zip(values, ways)]

    def next_step(step, layer, moving, first):
        gap = depth - 1 - step
        which = [
            [place[z][z + way * gap] if 0 <= z + way * gap < depth else 0 for z in range(depth)]
            for way in (1, -1)
        ]
        options = 1 + max(max(each) for each in which)
        which = jnp.array(which, jnp.int32)[:, seat.level]
        takes = jnp.ones((2,), jnp.int32)
        if len(moving) == 1:
            takes = jnp.stack([seat.level == 1, seat.level == depth - 2]).astype(jnp.int32)
        which = jnp.concatenate([which, takes])
        return level_step(layer[:options], which, [moving[0], moving[-1]], first)

    fars = [far_strip(0, [])]
    fars.append(far_strip(1, fars[:1]))
    layer = [near_strip(0, fars[0], fars[1:])]
    moving = moved([layer[0]] * 2, 0)
    layer.append(near_strip(1, fars[1], layer[:1]))
    given, kept = lower_slots(
        ancestor, panels, link_below, list_below, blocks_below,
        seat.col * (tile_cols // BLK), seat.col, layer[-1:],
    )
    given_sums, kept_sums = small_sums(placed, (given, kept), local, count, [])
    got_sums = swapped(given_sums, "cols", 1)
    stepped = next_step(1, layer, moving, [given_sums])
    moving = moved(stepped, 1)
    for turn in range(2, depth):
        fars.append(far_strip(turn, stepped[:1] if turn == 2 else fars[-1:]))
    layer.append(near_strip(2, fars[2], fars[-1:]))
    sums = split_sum(kept_sums, got_sums, seat.core, 2, layer[-1:])
    sums = split_sum(sums[0], swapped(sums[1], "rows", 1), seat.side, 2, [])
    mine = pair_sum([sums[0], swapped(sums[1], "rows", 2)], [])
    bits = (depth - 1).bit_length()
    for bit in range(bits):
        base_now = [added] if bit == bits - 1 else []
        mine = pair_sum([mine, swapped(mine, "rows", 4 << bit)] + base_now, [])
    for step in range(2, depth - 1):
        stepped = next_step(step, layer, moving, [mine])
        moving = moved(stepped, step)
        layer.append(near_strip(step + 1, fars[step + 1], stepped[:1]))
    whole = gather_small(seat, mine)

    given = jnp.where(got_sums[0, 0] == got_sums[0, 0], given, jnp.zeros_like(given))
    piece = kept.astype(F32) + swapped(given, "cols", 1).astype(F32)
    new_lower = piece[:, :half].astype(BF16)
    next_lower = piece[:, half:].astype(BF16)
    link_part = whole[:, half : 2 * half]
    link_other = swapped(link_part, "cols", 1)
    next_link = jnp.concatenate(
        [either(link_part, link_other), either(link_other, link_part)], axis=1
    )

    def with_rest(own, up, down):
        own_at = jnp.arange(block_count, dtype=jnp.int32)
        slot_dropped = jnp.logical_and(
            own_at < count, own_at >= 2 * SLOTS - jnp.minimum(meta[1], SLOTS)
        )
        dropped = jnp.any(
            jnp.logical_and(slot_dropped[:, None], local[:, None] == own_at[None, :]), axis=0
        )
        places = spread_place(seat, listed, 0), spread_place(seat, listed, 1)
        total = own.astype(F32) + up.astype(F32) + down.astype(F32)
        total = total + left_over(
            seat, ancestor, pieces, link_beside, (list_beside, blocks_beside), places, dropped,
        )
        return total[:width].T.astype(BF16), total[width:].T.astype(BF16)

    def without_rest(own, up, down):
        return last_sum(own, up, down, [next_link, new_lower])

    new_upper, next_upper = lax.cond(
        meta[2] > 2 * SLOTS, with_rest, without_rest, layer[-1], *moving
    )
    return (
        new_lower, new_upper, whole[:, :half], next_lower, next_upper, next_link,
        whole[:, 2 * half :],
    )


def body(*arrays):
    ancestor, panel, list_beside = arrays[0], arrays[1], arrays[6]
    rows, cols = lax.axis_size("rows"), lax.axis_size("cols")
    by_slots = (
        cols == 2
        and rows % 4 == 0
        and rows >= 16
        and rows & (rows - 1) == 0
        and panel.shape[0] == BLK
        and list_beside.shape[0] == rows
        and ancestor.shape[0] % BLK == 0
        and ancestor.shape[0] // BLK >= 2 * SLOTS
        and ancestor.shape[0] // BLK % SLOTS == 0
        and ancestor.shape[1] % (rows * BLK) == 0
        and panel.shape[1] % (2 * rows) == 0
    )
    return (body_by_slots if by_slots else body_general)(*arrays)


def solution(mesh):
    return jax.shard_map(
        body,
        mesh=mesh,
        in_specs=(
            P("rows", "cols"),
            P("rows", None),
            P("rows", None),
            P(),
            P(),
            P(),
            P(),
            P("rows", None),
            P("rows", None),
            P(),
            P(),
            P(),
            P(),
            P(),
            P(),
        ),
        out_specs=(
            P("rows", "cols"),
            P(("cols", "rows"), None),
            P(None, "cols"),
            P("rows", "cols"),
            P(("cols", "rows"), None),
            P(),
            P(None, "cols"),
        ),
        check_vma=False,
    )
```

```python
import functools

import jax
import jax.numpy as jnp
from jax import lax
from jax.experimental import pallas as pl
from jax.experimental.pallas import tpu as pltpu
from jax.sharding import PartitionSpec as P

BLK = 128
F32 = jnp.float32
BF16 = jnp.bfloat16


def mm(left, right):
    return jnp.dot(left, right, preferred_element_type=F32)


def mm_rows(left, right):
    return lax.dot_general(left, right, (((1,), (1,)), ((), ())), preferred_element_type=F32)


def mm_first(left, right):
    return lax.dot_general(left, right, (((0,), (0,)), ((), ())), preferred_element_type=F32)


def largest_tile(size, limit):
    tile = min(limit, size)
    while size % tile:
        tile -= BLK
    return tile


def gather_pair(first, second, product):
    cols = lax.axis_size("cols")
    if cols == 2:
        at_first = lax.axis_index("cols") == 0
        mine = product(
            jnp.where(at_first, first[0], second[0]), jnp.where(at_first, first[1], second[1])
        ).astype(BF16)
        return lax.all_gather(mine, ("cols", "rows"), axis=0, tiled=True)
    return jnp.concatenate(
        [
            lax.all_gather(product(*each).astype(BF16), "rows", axis=0, tiled=True)
            for each in (first, second)
        ]
    )


def place_body(pos1, in1, pos2, in2, u1_ref, u2_ref, link_ref, out_ref):
    at = pl.program_id(0)
    width = u1_ref.shape[1]
    keep1 = in1[at].astype(F32)
    keep2 = in2[at].astype(F32)
    u1 = u1_ref[...]
    linked = mm(u1, link_ref[...])
    out_ref[:width, :] = (-u1.astype(F32) * keep1).T.astype(BF16)
    out_ref[width:, :] = (linked * keep1 - u2_ref[...].astype(F32) * keep2).T.astype(BF16)


def blocks_in_tile(blocks, first_block, block_count):
    ids = first_block + jnp.arange(block_count, dtype=jnp.int32)
    matches = ids[:, None] == blocks[None, :]
    places = jnp.sum(
        jnp.where(matches, jnp.arange(blocks.shape[0], dtype=jnp.int32)[None, :], 0), axis=1
    )
    return places.astype(jnp.int32), jnp.any(matches, axis=1).astype(jnp.int32)


def rows_onto(panel, blocks, first_row, row_count):
    global_rows = first_row + jnp.arange(row_count, dtype=jnp.int32)
    matches = (global_rows // BLK)[:, None] == blocks[None, :]
    places = jnp.sum(
        jnp.where(matches, jnp.arange(blocks.shape[0], dtype=jnp.int32)[None, :], 0), axis=1
    )
    picked = jnp.take(panel, places * BLK + global_rows % BLK, axis=0)
    return jnp.where(jnp.any(matches, axis=1)[:, None], picked, jnp.zeros_like(picked))


def place_panels(both, link, list1, list2, first_row, row_count):
    width = both.shape[1]
    listed = list1.shape[0]
    if row_count % BLK:
        u1 = rows_onto(both[: listed * BLK], list1, first_row, row_count)
        u2 = rows_onto(both[listed * BLK :], list2, first_row, row_count)
        joined = jnp.concatenate([-u1.astype(F32), mm(u1, link) - u2.astype(F32)], axis=1)
        return joined.T.astype(BF16)
    first_block = first_row // BLK
    block_count = row_count // BLK
    pos1, in1 = blocks_in_tile(list1, first_block, block_count)
    pos2, in2 = blocks_in_tile(list2, first_block, block_count)
    return pl.pallas_call(
        place_body,
        out_shape=jax.ShapeDtypeStruct((2 * width, block_count * BLK), BF16),
        grid_spec=pltpu.PrefetchScalarGridSpec(
            num_scalar_prefetch=4,
            grid=(block_count,),
            in_specs=[
                pl.BlockSpec((BLK, width), lambda b, p1, i1, p2, i2: (p1[b], 0)),
                pl.BlockSpec((BLK, width), lambda b, p1, i1, p2, i2: (listed + p2[b], 0)),
                pl.BlockSpec((width, width), lambda b, p1, i1, p2, i2: (0, 0)),
            ],
            out_specs=pl.BlockSpec((2 * width, BLK), lambda b, p1, i1, p2, i2: (0, b)),
        ),
        compiler_params=pltpu.CompilerParams(vmem_limit_bytes=24 * 2**20),
        cost_estimate=pl.CostEstimate(
            flops=2 * block_count * BLK * width * width,
            bytes_accessed=8 * block_count * BLK * width,
            transcendentals=0,
        ),
        name="place_panels",
    )(pos1, in1, pos2, in2, both, both, link)


def lower_body(listed, loc1, in1, loc2, in2, part, *refs):
    tiles1, tiles2 = refs[:listed], refs[listed : 2 * listed]
    l1_ref, v1_ref, l2_ref, out_ref = refs[2 * listed :]
    half = l1_ref.shape[1]
    picked1 = jnp.concatenate(
        [tiles1[k][...] * in1[k].astype(F32).astype(BF16) for k in range(listed)], axis=1
    )
    picked2 = jnp.concatenate(
        [tiles2[k][...] * in2[k].astype(F32).astype(BF16) for k in range(listed)], axis=1
    )
    out_ref[:, :half] = (-mm(picked1, l1_ref[...])).astype(BF16)
    out_ref[:, half:] = (mm(picked1, v1_ref[...]) - mm(picked2, l2_ref[...])).astype(BF16)


def lower_partial(ancestor, both, linked, list1, list2, first_block, part, parts):
    rows, columns = ancestor.shape
    width = both.shape[1]
    half = width // parts
    listed = list1.shape[0]
    depth = listed * BLK
    block_count = columns // BLK
    tile = largest_tile(rows, 512)

    def local(blocks):
        at = blocks - first_block
        inside = jnp.logical_and(at >= 0, at < block_count)
        return jnp.clip(at, 0, block_count - 1), inside.astype(jnp.int32)

    loc1, in1 = local(list1)
    loc2, in2 = local(list2)
    specs = [
        pl.BlockSpec((tile, BLK), functools.partial(lambda k, i, l1, i1, l2, i2, p: (i, l1[k]), k))
        for k in range(listed)
    ] + [
        pl.BlockSpec((tile, BLK), functools.partial(lambda k, i, l1, i1, l2, i2, p: (i, l2[k]), k))
        for k in range(listed)
    ]
    specs += [
        pl.BlockSpec((depth, half), lambda i, l1, i1, l2, i2, p: (0, p[0])),
        pl.BlockSpec((depth, half), lambda i, l1, i1, l2, i2, p: (0, p[0])),
        pl.BlockSpec((depth, half), lambda i, l1, i1, l2, i2, p: (1, p[0])),
    ]
    return pl.pallas_call(
        functools.partial(lower_body, listed),
        out_shape=jax.ShapeDtypeStruct((rows, 2 * half), BF16),
        grid_spec=pltpu.PrefetchScalarGridSpec(
            num_scalar_prefetch=5,
            grid=(rows // tile,),
            in_specs=specs,
            out_specs=pl.BlockSpec((tile, 2 * half), lambda i, l1, i1, l2, i2, p: (i, 0)),
        ),
        compiler_params=pltpu.CompilerParams(vmem_limit_bytes=40 * 2**20),
        cost_estimate=pl.CostEstimate(
            flops=6 * rows * depth * half,
            bytes_accessed=4 * rows * depth + 6 * depth * half,
            transcendentals=0,
        ),
        name="lower_partial",
    )(
        loc1, in1, loc2, in2, jnp.reshape(part, (1,)).astype(jnp.int32),
        *([ancestor] * (2 * listed)), both, linked, both,
    )


def strip_body(strip, w_ref, a_ref, *refs):
    total = mm(w_ref[...], a_ref[...])
    for ref in refs[:-1]:
        total = total + ref[...].astype(F32)
    refs[-1][...] = total.astype(BF16)


def strip_product(ancestor, placed, strip, strips, *added):
    rows, columns = ancestor.shape
    strip_width = columns // strips
    height = placed.shape[0]
    if strip_width % BLK:
        total = mm(
            placed, lax.dynamic_slice_in_dim(ancestor, strip * strip_width, strip_width, 1)
        )
        for each in added:
            total = total + each.astype(F32)
        return total.astype(BF16)
    tile = largest_tile(strip_width, 256)
    per = strip_width // tile
    return pl.pallas_call(
        strip_body,
        out_shape=jax.ShapeDtypeStruct((height, strip_width), BF16),
        grid_spec=pltpu.PrefetchScalarGridSpec(
            num_scalar_prefetch=1,
            grid=(per,),
            in_specs=[
                pl.BlockSpec((height, rows), lambda j, s: (0, 0)),
                pl.BlockSpec((rows, tile), lambda j, s: (0, s[0] * per + j)),
            ]
            + [pl.BlockSpec((height, tile), lambda j, s: (0, j))] * len(added),
            out_specs=pl.BlockSpec((height, tile), lambda j, s: (0, j)),
        ),
        compiler_params=pltpu.CompilerParams(vmem_limit_bytes=40 * 2**20),
        cost_estimate=pl.CostEstimate(
            flops=2 * height * rows * strip_width,
            bytes_accessed=2 * (rows * strip_width + height * rows)
            + 2 * (1 + len(added)) * height * strip_width,
            transcendentals=0,
        ),
        name="strip_product",
    )(jnp.reshape(strip, (1,)).astype(jnp.int32), placed, ancestor, *added)


def add_pair(left, right):
    return (left.astype(F32) + right.astype(F32)).astype(BF16)


def upper_sums(ancestor, placed):
    strips = lax.axis_size("rows")
    row_at = lax.axis_index("rows")
    inner = 4 if strips % 4 == 0 else 1
    if inner == 1:
        whole = strip_product(ancestor, placed, 0, 1)
        return lax.psum_scatter(whole.astype(F32), "rows", scatter_dimension=1, tiled=True)
    depth = strips // inner
    core, side, level = row_at % 2, (row_at // 2) % 2, row_at // 4
    to_core = [(i, i ^ 1) for i in range(strips)]
    to_side = [(i, i ^ 2) for i in range(strips)]
    order = [sorted(range(depth), key=lambda d: (-abs(d - z), d)) for z in range(depth)]
    place = [[order[z].index(d) for d in range(depth)] for z in range(depth)]
    order_table = jnp.array(order, jnp.int32)

    def strip_of(target, x, c):
        return (target * 2 + x) * 2 + c

    layer = []
    for turn in range(depth):
        target = order_table[level, turn]
        far = strip_product(ancestor, placed, strip_of(target, 1 - side, 1 - core), strips)
        far = lax.ppermute(far, "rows", to_core)
        near = strip_product(ancestor, placed, strip_of(target, side, 1 - core), strips)
        near = lax.ppermute(near, "rows", to_core)
        far = strip_product(ancestor, placed, strip_of(target, 1 - side, core), strips, far)
        far = lax.ppermute(far, "rows", to_side)
        layer.append(
            strip_product(ancestor, placed, strip_of(target, side, core), strips, near, far)
        )

    def own_part(step, way):
        gap = depth - 1 - step
        chosen = None
        for z in range(depth):
            target = z + way * gap
            if 0 <= target < depth:
                value = layer[place[z][target]]
                chosen = value if chosen is None else jnp.where(level == z, value, chosen)
        return chosen

    arrived = {1: None, -1: None}
    for step in range(depth - 1):
        gap = depth - 1 - step
        for way in (1, -1):
            senders = [z for z in range(depth) if 0 <= z + way * gap < depth]
            pairs = [
                (z * inner + i, (z + way) * inner + i) for z in senders for i in range(inner)
            ]
            value = own_part(step, way)
            if arrived[way] is not None:
                value = add_pair(value, arrived[way])
            arrived[way] = lax.ppermute(value, "rows", pairs)
    total = layer[-1].astype(F32)
    for way in (1, -1):
        if arrived[way] is not None:
            total = total + arrived[way].astype(F32)
    return total


def body_general(
    ancestor,
    panel_below,
    panel_beside,
    inverse_lower,
    inverse_upper,
    list_below,
    list_beside,
    second_below,
    second_beside,
    linked_below,
    linked_beside,
    second_lower,
    second_upper,
    blocks_below,
    blocks_beside,
):
    row_at = lax.axis_index("rows")
    col_at = lax.axis_index("cols")
    cols = lax.axis_size("cols")
    tile_rows, tile_cols = ancestor.shape
    width = inverse_lower.shape[0]
    half = width // cols

    beside = gather_pair((panel_beside, inverse_upper), (second_beside, second_upper), mm_rows)
    below = gather_pair((panel_below, inverse_lower), (second_below, second_lower), mm)
    link_below = mm(linked_below, second_lower).astype(BF16)
    link_beside = mm_rows(linked_beside, second_upper).astype(BF16)

    placed = place_panels(
        beside, link_beside, list_beside, blocks_beside,
        row_at * tile_rows, tile_rows,
    )
    upper = upper_sums(ancestor, placed)
    new_upper = upper[:width].T.astype(BF16)
    next_upper = upper[width:].T.astype(BF16)

    depth = below.shape[0] // 2
    linked = mm(below[:depth], link_below).astype(BF16)
    lower_total = None
    sums_total = None
    for shift in reversed(range(cols)):
        part = (col_at + shift) % cols
        piece = lower_partial(
            ancestor, below, linked, list_below, blocks_below,
            col_at * (tile_cols // BLK), part, cols,
        )
        sums = jnp.concatenate(
            [mm(placed[:width], piece), mm(placed[width:], piece[:, half:])], axis=1
        )
        if shift:
            pairs = [(i, (i + shift) % cols) for i in range(cols)]
            piece = lax.ppermute(piece, "cols", pairs)
            sums = lax.ppermute(sums, "cols", pairs)
        piece = piece.astype(F32)
        lower_total = piece if lower_total is None else lower_total + piece
        sums_total = sums if sums_total is None else sums_total + sums
    new_lower = lower_total[:, :half].astype(BF16)
    next_lower = lower_total[:, half:].astype(BF16)

    sums = lax.psum(sums_total, "rows")

    def own(matrix):
        return lax.dynamic_slice_in_dim(matrix, col_at * half, half, 1)

    base = mm(inverse_upper, inverse_lower).astype(BF16)
    base_link = mm(base, own(link_below))
    new_diagonal = (mm(inverse_upper, own(inverse_lower)) + sums[:, :half]).astype(BF16)
    link_part = (sums[:, half : 2 * half] - base_link).astype(BF16)
    next_link = lax.all_gather(link_part, "cols", axis=1, tiled=True)
    next_diagonal = (
        mm(second_upper, own(second_lower))
        + mm_first(link_beside, base_link.astype(BF16))
        + sums[:, 2 * half :]
    ).astype(BF16)
    return (new_lower, new_upper, new_diagonal, next_lower, next_upper, next_link, next_diagonal)


SLOTS = 4
FREE = pl.CostEstimate(flops=0, bytes_accessed=0, transcendentals=0)
ANY = pl.BlockSpec(memory_space=pl.ANY)
SCALARS = pl.BlockSpec(memory_space=pltpu.SMEM)


def swapped(value, axis, bit):
    size = lax.axis_size(axis)
    return lax.ppermute(value, axis, [(i, i ^ bit) for i in range(size)])


def from_levels(value, shift):
    size = lax.axis_size("rows")
    return lax.ppermute(value, "rows", [(i, (i + 4 * shift) % size) for i in range(size)])


class Seat:
    def __init__(self):
        row_at = lax.axis_index("rows")
        self.row = row_at
        self.core, self.side, self.level = row_at % 2, (row_at // 2) % 2, row_at // 4
        self.depth = lax.axis_size("rows") // 4
        self.col = lax.axis_index("cols")


def spread(item, depth):
    pair = jnp.concatenate([item, swapped(item, "rows", 2)])
    near = [pair] + [from_levels(pair, shift) for shift in range(1, depth)]
    beyond = [swapped(each, "cols", 1) for each in near]
    return (
        near + [swapped(each, "rows", 1) for each in near]
        + beyond + [swapped(each, "rows", 1) for each in beyond]
    )


def spread_place(seat, listed, which):
    at = jnp.arange(listed, dtype=jnp.int32)
    core, side, level = at % 2, (at // 2) % 2, at // 4
    apart = (seat.col ^ which) * 2 + (seat.core ^ core)
    return (apart * seat.depth + (seat.level - level) % seat.depth) * 2 + (seat.side ^ side)


def plan_body(block_count, row, l1, l2, local, meta, b1, m1, b2, m2, at1, at2):
    listed = l1.shape[0]
    tiles = at1.shape[0] // block_count
    depth = listed // 4
    own, column = row[0], row[1]

    def place_of(k, which):
        apart = (own >> 2) - (k >> 2)
        apart = jnp.where(apart < 0, apart + depth, apart)
        half = (column ^ which) * 2 + ((own ^ k) & 1)
        return (half * depth + apart) * 2 + (((own ^ k) >> 1) & 1)

    @pl.loop(0, at1.shape[0])
    def _(i):
        at1[i] = 0
        at2[i] = 0

    @pl.loop(0, listed)
    def _(k):
        at1[l1[k]] = k + 1
        at2[l2[k]] = k + 1

    @pl.loop(0, b1.shape[0])
    def _(s):
        b1[s] = 0
        m1[s] = 0
        b2[s] = 0
        m2[s] = 0

    def scan(tile, put):
        def step(b, rank):
            g = tile * block_count + b
            here = jnp.where(at1[g] + at2[g] > 0, 1, 0)
            put(rank, b, g, here)
            return rank + here

        return lax.fori_loop(0, block_count, step, jnp.int32(0))

    def place(slot, g):
        b1[slot] = place_of(jnp.maximum(at1[g] - 1, 0), 0)
        m1[slot] = jnp.where(at1[g] > 0, 1, 0)
        b2[slot] = place_of(jnp.maximum(at2[g] - 1, 0), 1)
        m2[slot] = jnp.where(at2[g] > 0, 1, 0)

    def put_own(rank, b, g, here):
        local[rank] = b
        place(SLOTS + rank, g)

    def put_facing(rank, b, g, here):
        @pl.when(jnp.logical_and(here > 0, rank < SLOTS))
        def _():
            place(rank, g)

    def nothing(rank, b, g, here):
        return None

    @pl.loop(0, block_count)
    def _(s):
        local[s] = 0

    meta[0] = scan(own, put_own)
    meta[1] = scan(own ^ 1, nothing)
    facing = scan(own ^ 2, put_facing)

    def put_beyond(rank, b, g, here):
        slot = facing + rank - SLOTS

        @pl.when(jnp.logical_and(here > 0, jnp.logical_and(rank >= SLOTS, slot < SLOTS)))
        def _():
            place(slot, g)

    scan(own ^ 3, put_beyond)

    def most(chip, found):
        count = scan(2 * chip, nothing) + scan(2 * chip + 1, nothing)
        return jnp.maximum(found, count)

    meta[2] = lax.fori_loop(0, tiles // 2, most, jnp.int32(0))


def plan_slots(row, column, list1, list2, block_count, tiles):
    def numbers(count):
        return jax.ShapeDtypeStruct((count,), jnp.int32)

    slots = SLOTS + block_count
    return pl.pallas_call(
        functools.partial(plan_body, block_count),
        out_shape=(numbers(block_count), numbers(3)) + (numbers(slots),) * 4,
        in_specs=[SCALARS] * 3,
        out_specs=(SCALARS,) * 6,
        scratch_shapes=[pltpu.SMEM((tiles * block_count,), jnp.int32)] * 2,
        name="plan_slots",
    )(jnp.stack([row, column]).astype(jnp.int32), list1, list2)


def place_slots_body(count, b1, m1, b2, m2, link_ref, *refs):
    pieces = refs[:count]
    out_ref, got, sems = refs[-3:]
    width = link_ref.shape[0]
    slots = b1.shape[0]

    def start(s, which, block):
        row = pl.multiple_of((block[s] & 1) * BLK, BLK)
        for group in range(0, count, 4):

            @pl.when(block[s] >> 3 == group // 4)
            def _():
                for at in range(group, group + 4):

                    @pl.when(block[s] >> 1 == at)
                    def _():
                        pltpu.make_async_copy(
                            pieces[at].at[pl.ds(row, BLK), :],
                            got.at[which, s],
                            sems.at[which, s],
                        ).start()

    @pl.loop(0, slots)
    def _(s):
        for which, (block, used) in enumerate(((b1, m1), (b2, m2))):

            @pl.when(used[s] > 0)
            def _():
                start(s, which, block)

    def wait(s, which, used):
        @pl.when(used[s] > 0)
        def _():
            pltpu.make_async_copy(
                pieces[0].at[pl.ds(0, BLK), :], got.at[which, s], sems.at[which, s]
            ).wait()

    for s in range(slots):
        columns = pl.ds(s * BLK, BLK)
        used = m1[s] + m2[s] > 0

        @pl.when(used)
        def _():
            wait(s, 0, m1)
            wait(s, 1, m2)
            u1 = jnp.where(m1[s] > 0, got[0, s].astype(F32), 0.0)
            u2 = jnp.where(m2[s] > 0, got[1, s].astype(F32), 0.0)
            linked = mm(u1.astype(BF16), link_ref[...])
            out_ref[:width, columns] = (-u1).T.astype(BF16)
            out_ref[width:, columns] = (linked - u2).T.astype(BF16)

        @pl.when(jnp.logical_not(used))
        def _():
            out_ref[:, columns] = jnp.zeros((2 * width, BLK), BF16)


def place_slots(pieces, link, tables, first):
    width = link.shape[0]
    slots = tables[0].shape[0]
    vmem = pl.BlockSpec(memory_space=pltpu.VMEM)
    return pl.pallas_call(
        functools.partial(place_slots_body, len(pieces)),
        out_shape=jax.ShapeDtypeStruct((2 * width, slots * BLK), BF16),
        in_specs=[SCALARS] * 4 + [vmem] + [ANY] * (len(pieces) + len(first)),
        out_specs=vmem,
        scratch_shapes=[
            pltpu.VMEM((2, slots, BLK, width), BF16),
            pltpu.SemaphoreType.DMA((2, slots)),
        ],
        compiler_params=pltpu.CompilerParams(vmem_limit_bytes=56 * 2**20),
        cost_estimate=FREE,
        name="place_slots",
    )(*tables, link, *pieces, *first)


def pack_body(local, pair, a_ref, *refs):
    refs[-1][...] = a_ref[...]


def pack(ancestor, local, columns, pairs, first):
    wide = ancestor.shape[1] // pairs
    turns = columns.shape[0]
    return pl.pallas_call(
        pack_body,
        out_shape=jax.ShapeDtypeStruct((SLOTS * BLK, turns * wide), BF16),
        grid_spec=pltpu.PrefetchScalarGridSpec(
            num_scalar_prefetch=2,
            grid=(turns, SLOTS),
            in_specs=[pl.BlockSpec((BLK, wide), lambda t, s, l, p: (l[SLOTS + s], p[t]))]
            + [ANY] * len(first),
            out_specs=pl.BlockSpec((BLK, wide), lambda t, s, l, p: (s, t)),
        ),
        cost_estimate=FREE,
        name="pack_slots",
    )(local, columns, ancestor, *first)


def merge_body(local, meta, columns, a_ref, got_ref, *refs):
    mine = pl.program_id(1) < meta[0]
    out_ref = refs[-1]

    @pl.when(mine)
    def _():
        out_ref[...] = a_ref[...]

    @pl.when(jnp.logical_not(mine))
    def _():
        out_ref[...] = got_ref[...]


def merge(ancestor, got, local, meta, columns, pairs):
    wide = ancestor.shape[1] // pairs
    turns = columns.shape[0]
    return pl.pallas_call(
        merge_body,
        out_shape=jax.ShapeDtypeStruct((SLOTS * BLK, turns * wide), BF16),
        grid_spec=pltpu.PrefetchScalarGridSpec(
            num_scalar_prefetch=3,
            grid=(turns, SLOTS),
            in_specs=[
                pl.BlockSpec((BLK, wide), lambda t, s, l, n, p: (l[s], p[t])),
                pl.BlockSpec(
                    (BLK, wide), lambda t, s, l, n, p: (jnp.clip(s - n[0], 0, SLOTS - 1), t)
                ),
            ],
            out_specs=pl.BlockSpec((BLK, wide), lambda t, s, l, n, p: (s, t)),
        ),
        compiler_params=pltpu.CompilerParams(vmem_limit_bytes=56 * 2**20),
        cost_estimate=FREE,
        name="merge_slots",
    )(local, meta, columns, ancestor, got)


def lower_slots_body(groups, block_count, l1, l2, at, *refs):
    listed = groups * SLOTS
    tiles = (refs[:listed], refs[listed : 2 * listed])
    panel_refs, link_ref = refs[2 * listed : 2 * listed + 2], refs[2 * listed + 2]
    given_ref, kept_ref, linked_ref, total_ref = refs[-4:]
    width = link_ref.shape[0]
    half = width // 2

    @pl.when(pl.program_id(0) == 0)
    def _():
        linked_ref[...] = mm(panel_refs[0][...], link_ref[...]).astype(BF16)

    def picked(which, blocks):
        kept = []
        for k in range(listed):
            place = blocks[k] - at[0]
            inside = jnp.logical_and(place >= 0, place < block_count)
            kept.append(tiles[which][k][...] * jnp.where(inside, 1.0, 0.0).astype(BF16))
        return jnp.concatenate(kept, axis=1)

    picked1 = picked(0, l1)
    total_ref[:, :width] = -mm(picked1, panel_refs[0][...])
    second = mm(picked1, linked_ref[...]) - mm(picked(1, l2), panel_refs[1][...])
    total_ref[:, width:] = second

    for column, (own, other) in ((0, (kept_ref, given_ref)), (1, (given_ref, kept_ref))):

        @pl.when(at[1] == column)
        def _():
            for out, start in ((own, 0), (other, half)):
                out[:, :half] = total_ref[:, start : start + half].astype(BF16)
                second = total_ref[:, width + start : width + start + half]
                out[:, half:] = second.astype(BF16)


def lower_slots(ancestor, panels, link, list1, list2, first_block, column, first):
    rows, columns = ancestor.shape
    listed, width = list1.shape[0], link.shape[0]
    block_count = columns // BLK
    tile = largest_tile(rows, 512)
    at = jnp.stack([first_block, column]).astype(jnp.int32)

    def picked(which, k):
        def index(i, l1, l2, at):
            place = (l1, l2)[which][k] - at[0]
            inside = jnp.logical_and(place >= 0, place < block_count)
            return jnp.where(inside, i, 0), jnp.clip(place, 0, block_count - 1)

        return pl.BlockSpec((tile, BLK), index)

    specs = [picked(which, k) for which in (0, 1) for k in range(listed)]
    specs += [
        pl.BlockSpec((listed * BLK, width), lambda i, l1, l2, at: (0, 0)),
        pl.BlockSpec((listed * BLK, width), lambda i, l1, l2, at: (1, 0)),
        pl.BlockSpec((width, width), lambda i, l1, l2, at: (0, 0)),
    ]
    shape = jax.ShapeDtypeStruct((rows, width), BF16)
    return pl.pallas_call(
        functools.partial(lower_slots_body, listed // SLOTS, block_count),
        out_shape=(shape, shape),
        grid_spec=pltpu.PrefetchScalarGridSpec(
            num_scalar_prefetch=3,
            grid=(rows // tile,),
            in_specs=specs + [ANY] * len(first),
            out_specs=(pl.BlockSpec((tile, width), lambda i, l1, l2, at: (i, 0)),) * 2,
            scratch_shapes=[
                pltpu.VMEM((listed * BLK, width), BF16),
                pltpu.VMEM((tile, 2 * width), F32),
            ],
        ),
        compiler_params=pltpu.CompilerParams(vmem_limit_bytes=56 * 2**20),
        cost_estimate=FREE,
        name="lower_slots",
    )(list1, list2, at, *([ancestor] * (2 * listed)), panels, panels, link, *first)


def slots_body(adds, local, count, at, w_ref, arrived_ref, *refs):
    tiles = refs[:SLOTS]
    added = refs[SLOTS : SLOTS + adds]
    placed_ref, ancestor_ref = refs[SLOTS + adds : SLOTS + adds + 2]
    out_ref, rest_w, rest_a, sems = refs[-4:]

    def store(total):
        for ref in added:
            total = total + ref[...].astype(F32)
        out_ref[...] = total.astype(BF16)

    def product():
        first = [arrived_ref[...]] + [ref[...] for ref in tiles]
        return mm(w_ref[...], jnp.concatenate(first, axis=0))

    @pl.when(count[0] <= SLOTS)
    def _():
        store(product())

    @pl.when(count[0] > SLOTS)
    def _():
        tile = out_ref.shape[1]
        more = rest_a.shape[0] // BLK
        column = pl.multiple_of((at[0] + pl.program_id(0)) * tile, BLK)
        copies = [
            pltpu.make_async_copy(
                placed_ref.at[:, pl.ds(2 * SLOTS * BLK, more * BLK)], rest_w, sems.at[more]
            )
        ]
        for s in range(more):
            row = pl.multiple_of(local[SLOTS + s] * BLK, BLK)
            copies.append(
                pltpu.make_async_copy(
                    ancestor_ref.at[pl.ds(row, BLK), pl.ds(column, tile)],
                    rest_a.at[pl.ds(s * BLK, BLK), :],
                    sems.at[s],
                )
            )
        for copy in copies:
            copy.start()
        total = product()
        for copy in copies:
            copy.wait()
        store(total + mm(rest_w[...], rest_a[...]))


def slots_product(
    ancestor, placed, arrived, local, count, strip, within, strips, added, first
):
    columns = ancestor.shape[1]
    strip_width = columns // strips
    height = placed.shape[0]
    tile = largest_tile(strip_width, 384)
    per = strip_width // tile
    more = placed.shape[1] // BLK - 2 * SLOTS
    where_at = jnp.stack([strip * per, within * per]).astype(jnp.int32)

    def own_block(slot):
        return lambda j, l, n, p: (l[slot], p[0] + j)

    return pl.pallas_call(
        functools.partial(slots_body, len(added)),
        out_shape=jax.ShapeDtypeStruct((height, strip_width), BF16),
        grid_spec=pltpu.PrefetchScalarGridSpec(
            num_scalar_prefetch=3,
            grid=(per,),
            in_specs=[pl.BlockSpec((height, 2 * SLOTS * BLK), lambda j, l, n, p: (0, 0))]
            + [pl.BlockSpec((SLOTS * BLK, tile), lambda j, l, n, p: (0, p[1] + j))]
            + [pl.BlockSpec((BLK, tile), own_block(slot)) for slot in range(SLOTS)]
            + [pl.BlockSpec((height, tile), lambda j, l, n, p: (0, j))] * len(added)
            + [ANY] * (2 + len(first)),
            out_specs=pl.BlockSpec((height, tile), lambda j, l, n, p: (0, j)),
            scratch_shapes=[
                pltpu.VMEM((height, more * BLK), BF16),
                pltpu.VMEM((more * BLK, tile), BF16),
                pltpu.SemaphoreType.DMA((more + 1,)),
            ],
        ),
        compiler_params=pltpu.CompilerParams(vmem_limit_bytes=56 * 2**20),
        cost_estimate=FREE,
        name="slots_product",
    )(
        local, jnp.reshape(count, (1,)), where_at, placed, arrived, *([ancestor] * SLOTS),
        *added, placed, ancestor, *first,
    )


def small_sums_body(local, count, w_ref, *refs):
    tiles, outs, totals = refs[: 2 * SLOTS], refs[-4:-2], refs[-2:]
    at = pl.program_id(0)
    width = w_ref.shape[0] // 2
    half = width // 2

    @pl.when(at == 0)
    def _():
        for total in totals:
            total[...] = jnp.zeros_like(total)

    @pl.when(at * SLOTS < count[0])
    def _():
        for which, total in enumerate(totals):
            group = tiles[which * SLOTS : (which + 1) * SLOTS]
            rows = jnp.concatenate([ref[...] for ref in group], axis=0)
            total[:, : 2 * half] += mm(w_ref[:width, :], rows)
            total[:, 2 * half :] += mm(w_ref[width:, :], rows[:, half:])

    @pl.when(at == pl.num_programs(0) - 1)
    def _():
        for out, total in zip(outs, totals):
            out[...] = total[...].astype(BF16)


def small_sums(placed, pieces, local, count, first):
    width = placed.shape[0] // 2
    wide = 3 * width // 2
    slots = local.shape[0]

    def row(k):
        def index(s, l, n):
            return l[jnp.where(s * SLOTS < n[0], s, 0) * SLOTS + k], 0

        return pl.BlockSpec((BLK, width), index)

    shape = jax.ShapeDtypeStruct((width, wide), BF16)
    return pl.pallas_call(
        small_sums_body,
        out_shape=(shape, shape),
        grid_spec=pltpu.PrefetchScalarGridSpec(
            num_scalar_prefetch=2,
            grid=(slots // SLOTS,),
            in_specs=[
                pl.BlockSpec(
                    (2 * width, SLOTS * BLK),
                    lambda s, l, n: (0, 1 + jnp.where(s * SLOTS < n[0], s, 0)),
                )
            ]
            + [row(k) for k in range(SLOTS)] * 2
            + [ANY] * len(first),
            out_specs=(pl.BlockSpec((width, wide), lambda s, l, n: (0, 0)),) * 2,
            scratch_shapes=[pltpu.VMEM((width, wide), F32)] * 2,
        ),
        compiler_params=pltpu.CompilerParams(vmem_limit_bytes=56 * 2**20),
        cost_estimate=FREE,
        name="small_sums",
    )(
        local, jnp.reshape(count, (1,)), placed, *([pieces[0]] * SLOTS),
        *([pieces[1]] * SLOTS), *first,
    )


def step_body(options, which, *refs):
    choices, arrived = refs[:options], refs[options : options + 2]
    outs = refs[-2:]
    for way in (0, 1):
        for option in range(options):

            @pl.when(which[way] == option)
            def _():
                came = arrived[way][...].astype(F32) * which[2 + way].astype(F32)
                outs[way][...] = (choices[option][...].astype(F32) + came).astype(BF16)


def level_step(choices, which, arrived, first):
    height, wide = choices[0].shape
    tile = height // 4
    block = (tile, wide)

    def choice(option):
        def index(i, w):
            return jnp.where(jnp.logical_or(w[0] == option, w[1] == option), i, 0), 0

        return pl.BlockSpec(block, index)

    def whole(i, w):
        return i, 0

    shape = jax.ShapeDtypeStruct((height, wide), BF16)
    return pl.pallas_call(
        functools.partial(step_body, len(choices)),
        out_shape=(shape, shape),
        grid_spec=pltpu.PrefetchScalarGridSpec(
            num_scalar_prefetch=1,
            grid=(height // tile,),
            in_specs=[choice(option) for option in range(len(choices))]
            + [pl.BlockSpec(block, whole)] * 2
            + [ANY] * len(first),
            out_specs=(pl.BlockSpec(block, whole),) * 2,
        ),
        compiler_params=pltpu.CompilerParams(vmem_limit_bytes=56 * 2**20),
        cost_estimate=FREE,
        name="level_step",
    )(which, *choices, *arrived, *first)


def last_body(own_ref, up_ref, down_ref, *refs):
    first_ref, second_ref = refs[-2:]
    width = first_ref.shape[1]
    total = own_ref[...].astype(F32) + up_ref[...].astype(F32) + down_ref[...].astype(F32)
    first_ref[...] = total[:width].T.astype(BF16)
    second_ref[...] = total[width:].T.astype(BF16)


def last_sum(own, up, down, first):
    height, wide = own.shape
    tile = largest_tile(wide, 256)
    width = height // 2
    shape = jax.ShapeDtypeStruct((wide, width), BF16)
    return pl.pallas_call(
        last_body,
        out_shape=(shape, shape),
        grid=(wide // tile,),
        in_specs=[pl.BlockSpec((height, tile), lambda j: (0, j))] * 3 + [ANY] * len(first),
        out_specs=(pl.BlockSpec((tile, width), lambda j: (j, 0)),) * 2,
        compiler_params=pltpu.CompilerParams(vmem_limit_bytes=56 * 2**20),
        cost_estimate=FREE,
        name="last_sum",
    )(own, up, down, *first)


def split_body(parts, at, left_ref, right_ref, *refs):
    outs = refs[-parts:]
    size = outs[0].shape[0]
    for shift in range(parts):
        start = pl.multiple_of(lax.rem(at[0] + shift, parts) * size, 16)
        rows = pl.ds(start, size)
        total = left_ref[rows, :].astype(F32) + right_ref[rows, :].astype(F32)
        outs[shift][...] = total.astype(BF16)


def split_sum(left, right, at, parts, first):
    rows, wide = left.shape
    shape = jax.ShapeDtypeStruct((rows // parts, wide), BF16)
    vmem = pl.BlockSpec(memory_space=pltpu.VMEM)
    return pl.pallas_call(
        functools.partial(split_body, parts),
        out_shape=(shape,) * parts,
        in_specs=[SCALARS, vmem, vmem] + [ANY] * len(first),
        out_specs=(vmem,) * parts,
        compiler_params=pltpu.CompilerParams(vmem_limit_bytes=56 * 2**20),
        cost_estimate=FREE,
        name="split_sum",
    )(jnp.reshape(at, (1,)).astype(jnp.int32), left, right, *first)


def pair_sum(pieces, first):
    vmem = pl.BlockSpec(memory_space=pltpu.VMEM)
    count = len(pieces)

    def kernel(*refs):
        total = refs[0][...].astype(F32)
        for ref in refs[1:count]:
            total = total + ref[...].astype(F32)
        refs[-1][...] = total.astype(BF16)

    return pl.pallas_call(
        kernel,
        out_shape=jax.ShapeDtypeStruct(pieces[0].shape, BF16),
        in_specs=[vmem] * count + [ANY] * len(first),
        out_specs=vmem,
        cost_estimate=FREE,
        name="pair_sum",
    )(*pieces, *first)


def left_over(seat, ancestor, pieces, link, lists, places, dropped):
    block_rows, columns = ancestor.shape
    width = link.shape[0]
    first_row = seat.row * block_rows
    shaped = jnp.concatenate(pieces).reshape(-1, BLK, width)
    u1, u2 = (
        rows_onto(
            jnp.take(shaped, place, axis=0).reshape(-1, width), blocks, first_row, block_rows
        )
        for blocks, place in zip(lists, places)
    )
    joined = jnp.concatenate([-u1.astype(F32), mm(u1, link) - u2.astype(F32)], axis=1)
    joined = jnp.where(jnp.repeat(dropped, BLK)[:, None], joined, 0.0).astype(BF16)
    wide = columns // (2 * seat.depth)
    partial = jnp.concatenate(
        [
            mm_first(
                joined,
                lax.dynamic_slice_in_dim(
                    ancestor, (2 * level + 1 - seat.side) * wide, wide, 1
                ),
            ).astype(BF16)
            for level in range(seat.depth)
        ],
        axis=1,
    )
    groups = [
        [4 * level + 2 * side + core for level in range(seat.depth) for core in range(2)]
        for side in range(2)
    ]
    own = lax.psum_scatter(
        partial, "rows", scatter_dimension=1, axis_index_groups=groups, tiled=True
    )
    return swapped(own, "rows", 2).astype(F32)


def gather_small(seat, value):
    for bit, at in ((2, seat.side), (1, seat.core)):
        other = swapped(value, "rows", bit)
        value = jnp.concatenate(
            [jnp.where(at == 0, value, other), jnp.where(at == 0, other, value)]
        )
    return value


def body_by_slots(
    ancestor,
    panel_below,
    panel_beside,
    inverse_lower,
    inverse_upper,
    list_below,
    list_beside,
    second_below,
    second_beside,
    linked_below,
    linked_beside,
    second_lower,
    second_upper,
    blocks_below,
    blocks_beside,
):
    seat = Seat()
    tile_rows, tile_cols = ancestor.shape
    block_count = tile_rows // BLK
    width = inverse_lower.shape[0]
    half = width // 2
    listed = list_below.shape[0]
    depth = seat.depth
    rows = 4 * depth
    pairs = 2 * depth
    at_first = seat.col == 0

    def either(first, second):
        return jnp.where(at_first, first, second)

    beside = mm_rows(either(panel_beside, second_beside), either(inverse_upper, second_upper))
    pieces = spread(beside.astype(BF16), depth)
    below = mm(either(panel_below, second_below), either(inverse_lower, second_lower))
    panels = lax.all_gather(below.astype(BF16), ("cols", "rows"), axis=0, tiled=True)
    link_below = mm(linked_below, second_lower).astype(BF16)
    link_beside = mm_rows(linked_beside, second_upper).astype(BF16)

    local, meta, *tables = plan_slots(
        seat.row, seat.col, list_beside, blocks_beside, block_count, rows
    )
    count = meta[0]
    order = [sorted(range(depth), key=lambda d: (-abs(d - z), d)) for z in range(depth)]
    place = [[order[z].index(d) for d in range(depth)] for z in range(depth)]
    order_table = jnp.array(order, jnp.int32)
    targets = [order_table[seat.level, turn] for turn in range(depth)]

    def own(matrix):
        return lax.dynamic_slice_in_dim(matrix, seat.col * half, half, 1)

    base = mm(inverse_upper, inverse_lower).astype(BF16)
    base_link = mm(base, own(link_below))
    added = jnp.concatenate(
        [
            mm(inverse_upper, own(inverse_lower)),
            -base_link,
            mm(second_upper, own(second_lower)) + mm_first(link_beside, base_link.astype(BF16)),
        ],
        axis=1,
    )
    added = lax.dynamic_slice_in_dim(
        added, (seat.core * 2 + seat.side) * (width // 4), width // 4, 0
    )

    columns = jnp.stack([target * 2 + 1 - seat.side for target in targets])
    turns = depth // 2
    leaving = []
    for group in range(0, depth, turns):
        near = columns[group : group + turns]
        packed = pack(ancestor, local, near, pairs, leaving or pieces[:1])
        leaving.append(merge(ancestor, swapped(packed, "rows", 1), local, meta, near, pairs))
    arrived = [swapped(each, "rows", 2) for each in leaving]
    placed = place_slots(pieces, link_beside, tables, leaving)

    def strip(turn, part, added, first):
        pair = targets[turn] * 2 + seat.side
        return slots_product(
            ancestor, placed, arrived[turn // turns], local, count, pair * 2 + part,
            (turn % turns) * 2 + part, rows, added, first,
        )

    def far_strip(turn, first):
        return strip(turn, 1 - seat.core, [], first)

    def near_strip(turn, far, first):
        return strip(turn, seat.core, [swapped(far, "rows", 1)], first)

    def moved(values, step):
        gap = depth - 1 - step
        ways = []
        for way in (1, -1):
            senders = [z for z in range(depth) if 0 <= z + way * gap < depth]
            ways.append([(z * 4 + i, (z + way) * 4 + i) for z in senders for i in range(4)])
        if step == 0:
            return [lax.ppermute(values[0], "rows", ways[0] + ways[1])]
        return [lax.ppermute(value, "rows", way) for value, way in zip(values, ways)]

    def next_step(step, layer, moving, first):
        gap = depth - 1 - step
        which = [
            [place[z][z + way * gap] if 0 <= z + way * gap < depth else 0 for z in range(depth)]
            for way in (1, -1)
        ]
        options = 1 + max(max(each) for each in which)
        which = jnp.array(which, jnp.int32)[:, seat.level]
        takes = jnp.ones((2,), jnp.int32)
        if len(moving) == 1:
            takes = jnp.stack([seat.level == 1, seat.level == depth - 2]).astype(jnp.int32)
        which = jnp.concatenate([which, takes])
        return level_step(layer[:options], which, [moving[0], moving[-1]], first)

    fars = [far_strip(0, [])]
    fars.append(far_strip(1, fars[:1]))
    layer = [near_strip(0, fars[0], fars[1:])]
    moving = moved([layer[0]] * 2, 0)
    layer.append(near_strip(1, fars[1], layer[:1]))
    given, kept = lower_slots(
        ancestor, panels, link_below, list_below, blocks_below,
        seat.col * (tile_cols // BLK), seat.col, layer[-1:],
    )
    given_sums, kept_sums = small_sums(placed, (given, kept), local, count, [])
    got_sums = swapped(given_sums, "cols", 1)
    stepped = next_step(1, layer, moving, [given_sums])
    moving = moved(stepped, 1)
    fars.append(far_strip(2, stepped[:1]))
    sums = split_sum(kept_sums, got_sums, seat.core, 2, fars[-1:])
    for turn in range(3, depth):
        fars.append(far_strip(turn, [sums[0]]))
    sums = split_sum(sums[0], swapped(sums[1], "rows", 1), seat.side, 2, fars[-1:])
    layer.append(near_strip(2, fars[2], [sums[0]]))
    mine = pair_sum([sums[0], swapped(sums[1], "rows", 2)], layer[-1:])
    bits = (depth - 1).bit_length()
    for bit in range(bits):
        base_now = [added] if bit == bits - 1 else []
        mine = pair_sum([mine, swapped(mine, "rows", 4 << bit)] + base_now, [])
    for step in range(2, depth - 1):
        stepped = next_step(step, layer, moving, [mine])
        moving = moved(stepped, step)
        layer.append(near_strip(step + 1, fars[step + 1], stepped[:1]))
    whole = gather_small(seat, mine)

    piece = kept.astype(F32) + swapped(given, "cols", 1).astype(F32)
    new_lower = piece[:, :half].astype(BF16)
    next_lower = piece[:, half:].astype(BF16)
    link_part = whole[:, half : 2 * half]
    link_other = swapped(link_part, "cols", 1)
    next_link = jnp.concatenate(
        [either(link_part, link_other), either(link_other, link_part)], axis=1
    )

    def with_rest(own, up, down):
        own_at = jnp.arange(block_count, dtype=jnp.int32)
        slot_dropped = jnp.logical_and(
            own_at < count, own_at >= 2 * SLOTS - jnp.minimum(meta[1], SLOTS)
        )
        dropped = jnp.any(
            jnp.logical_and(slot_dropped[:, None], local[:, None] == own_at[None, :]), axis=0
        )
        places = spread_place(seat, listed, 0), spread_place(seat, listed, 1)
        total = own.astype(F32) + up.astype(F32) + down.astype(F32)
        total = total + left_over(
            seat, ancestor, pieces, link_beside, (list_beside, blocks_beside), places, dropped,
        )
        return total[:width].T.astype(BF16), total[width:].T.astype(BF16)

    def without_rest(own, up, down):
        return last_sum(own, up, down, [next_link, new_lower])

    new_upper, next_upper = lax.cond(
        meta[2] > 2 * SLOTS, with_rest, without_rest, layer[-1], *moving
    )
    return (
        new_lower, new_upper, whole[:, :half], next_lower, next_upper, next_link,
        whole[:, 2 * half :],
    )


def body(*arrays):
    ancestor, panel, list_beside = arrays[0], arrays[1], arrays[6]
    rows, cols = lax.axis_size("rows"), lax.axis_size("cols")
    by_slots = (
        cols == 2
        and rows % 4 == 0
        and rows >= 16
        and rows & (rows - 1) == 0
        and panel.shape[0] == BLK
        and list_beside.shape[0] == rows
        and ancestor.shape[0] % BLK == 0
        and ancestor.shape[0] // BLK >= 2 * SLOTS
        and ancestor.shape[0] // BLK % SLOTS == 0
        and ancestor.shape[1] % (rows * BLK) == 0
        and panel.shape[1] % (2 * rows) == 0
    )
    return (body_by_slots if by_slots else body_general)(*arrays)


def solution(mesh):
    return jax.shard_map(
        body,
        mesh=mesh,
        in_specs=(
            P("rows", "cols"),
            P("rows", None),
            P("rows", None),
            P(),
            P(),
            P(),
            P(),
            P("rows", None),
            P("rows", None),
            P(),
            P(),
            P(),
            P(),
            P(),
            P(),
        ),
        out_specs=(
            P("rows", "cols"),
            P(("cols", "rows"), None),
            P(None, "cols"),
            P("rows", "cols"),
            P(("cols", "rows"), None),
            P(),
            P(None, "cols"),
        ),
        check_vma=False,
    )
```

```python
import functools

import jax
import jax.numpy as jnp
from jax import lax
from jax.experimental import pallas as pl
from jax.experimental.pallas import tpu as pltpu
from jax.sharding import PartitionSpec as P

BLK = 128
F32 = jnp.float32
BF16 = jnp.bfloat16


def mm(left, right):
    return jnp.dot(left, right, preferred_element_type=F32)


def mm_rows(left, right):
    return lax.dot_general(left, right, (((1,), (1,)), ((), ())), preferred_element_type=F32)


def mm_first(left, right):
    return lax.dot_general(left, right, (((0,), (0,)), ((), ())), preferred_element_type=F32)


def largest_tile(size, limit):
    tile = min(limit, size)
    while size % tile:
        tile -= BLK
    return tile


def gather_pair(first, second, product):
    cols = lax.axis_size("cols")
    if cols == 2:
        at_first = lax.axis_index("cols") == 0
        mine = product(
            jnp.where(at_first, first[0], second[0]), jnp.where(at_first, first[1], second[1])
        ).astype(BF16)
        return lax.all_gather(mine, ("cols", "rows"), axis=0, tiled=True)
    return jnp.concatenate(
        [
            lax.all_gather(product(*each).astype(BF16), "rows", axis=0, tiled=True)
            for each in (first, second)
        ]
    )


def place_body(pos1, in1, pos2, in2, u1_ref, u2_ref, link_ref, out_ref):
    at = pl.program_id(0)
    width = u1_ref.shape[1]
    keep1 = in1[at].astype(F32)
    keep2 = in2[at].astype(F32)
    u1 = u1_ref[...]
    linked = mm(u1, link_ref[...])
    out_ref[:width, :] = (-u1.astype(F32) * keep1).T.astype(BF16)
    out_ref[width:, :] = (linked * keep1 - u2_ref[...].astype(F32) * keep2).T.astype(BF16)


def blocks_in_tile(blocks, first_block, block_count):
    ids = first_block + jnp.arange(block_count, dtype=jnp.int32)
    matches = ids[:, None] == blocks[None, :]
    places = jnp.sum(
        jnp.where(matches, jnp.arange(blocks.shape[0], dtype=jnp.int32)[None, :], 0), axis=1
    )
    return places.astype(jnp.int32), jnp.any(matches, axis=1).astype(jnp.int32)


def rows_onto(panel, blocks, first_row, row_count):
    global_rows = first_row + jnp.arange(row_count, dtype=jnp.int32)
    matches = (global_rows // BLK)[:, None] == blocks[None, :]
    places = jnp.sum(
        jnp.where(matches, jnp.arange(blocks.shape[0], dtype=jnp.int32)[None, :], 0), axis=1
    )
    picked = jnp.take(panel, places * BLK + global_rows % BLK, axis=0)
    return jnp.where(jnp.any(matches, axis=1)[:, None], picked, jnp.zeros_like(picked))


def place_panels(both, link, list1, list2, first_row, row_count):
    width = both.shape[1]
    listed = list1.shape[0]
    if row_count % BLK:
        u1 = rows_onto(both[: listed * BLK], list1, first_row, row_count)
        u2 = rows_onto(both[listed * BLK :], list2, first_row, row_count)
        joined = jnp.concatenate([-u1.astype(F32), mm(u1, link) - u2.astype(F32)], axis=1)
        return joined.T.astype(BF16)
    first_block = first_row // BLK
    block_count = row_count // BLK
    pos1, in1 = blocks_in_tile(list1, first_block, block_count)
    pos2, in2 = blocks_in_tile(list2, first_block, block_count)
    return pl.pallas_call(
        place_body,
        out_shape=jax.ShapeDtypeStruct((2 * width, block_count * BLK), BF16),
        grid_spec=pltpu.PrefetchScalarGridSpec(
            num_scalar_prefetch=4,
            grid=(block_count,),
            in_specs=[
                pl.BlockSpec((BLK, width), lambda b, p1, i1, p2, i2: (p1[b], 0)),
                pl.BlockSpec((BLK, width), lambda b, p1, i1, p2, i2: (listed + p2[b], 0)),
                pl.BlockSpec((width, width), lambda b, p1, i1, p2, i2: (0, 0)),
            ],
            out_specs=pl.BlockSpec((2 * width, BLK), lambda b, p1, i1, p2, i2: (0, b)),
        ),
        compiler_params=pltpu.CompilerParams(vmem_limit_bytes=24 * 2**20),
        cost_estimate=pl.CostEstimate(
            flops=2 * block_count * BLK * width * width,
            bytes_accessed=8 * block_count * BLK * width,
            transcendentals=0,
        ),
        name="place_panels",
    )(pos1, in1, pos2, in2, both, both, link)


SLOTS = 4
FREE = pl.CostEstimate(flops=0, bytes_accessed=0, transcendentals=0)
ANY = pl.BlockSpec(memory_space=pl.ANY)


def lower_slots_body(groups, block_count, l1, l2, at, *refs):
    listed = groups * SLOTS
    tiles = (refs[:listed], refs[listed : 2 * listed])
    panel_refs, link_ref = refs[2 * listed : 2 * listed + 2], refs[2 * listed + 2]
    given_ref, kept_ref, linked_ref, total_ref = refs[-4:]
    width = link_ref.shape[0]
    half = width // 2

    @pl.when(pl.program_id(0) == 0)
    def _():
        linked_ref[...] = mm(panel_refs[0][...], link_ref[...]).astype(BF16)

    def picked(which, blocks):
        kept = []
        for k in range(listed):
            place = blocks[k] - at[0]
            inside = jnp.logical_and(place >= 0, place < block_count)
            kept.append(tiles[which][k][...] * jnp.where(inside, 1.0, 0.0).astype(BF16))
        return jnp.concatenate(kept, axis=1)

    picked1 = picked(0, l1)
    total_ref[:, :width] = -mm(picked1, panel_refs[0][...])
    second = mm(picked1, linked_ref[...]) - mm(picked(1, l2), panel_refs[1][...])
    total_ref[:, width:] = second

    for column, (own, other) in ((0, (kept_ref, given_ref)), (1, (given_ref, kept_ref))):

        @pl.when(at[1] == column)
        def _():
            for out, start in ((own, 0), (other, half)):
                out[:, :half] = total_ref[:, start : start + half].astype(BF16)
                second = total_ref[:, width + start : width + start + half]
                out[:, half:] = second.astype(BF16)


def lower_slots(ancestor, panels, link, list1, list2, first_block, column, first):
    rows, columns = ancestor.shape
    listed, width = list1.shape[0], link.shape[0]
    block_count = columns // BLK
    tile = largest_tile(rows, 512)
    at = jnp.stack([first_block, column]).astype(jnp.int32)

    def picked(which, k):
        def index(i, l1, l2, at):
            place = (l1, l2)[which][k] - at[0]
            inside = jnp.logical_and(place >= 0, place < block_count)
            return jnp.where(inside, i, 0), jnp.clip(place, 0, block_count - 1)

        return pl.BlockSpec((tile, BLK), index)

    specs = [picked(which, k) for which in (0, 1) for k in range(listed)]
    specs += [
        pl.BlockSpec((listed * BLK, width), lambda i, l1, l2, at: (0, 0)),
        pl.BlockSpec((listed * BLK, width), lambda i, l1, l2, at: (1, 0)),
        pl.BlockSpec((width, width), lambda i, l1, l2, at: (0, 0)),
    ]
    shape = jax.ShapeDtypeStruct((rows, width), BF16)
    return pl.pallas_call(
        functools.partial(lower_slots_body, listed // SLOTS, block_count),
        out_shape=(shape, shape),
        grid_spec=pltpu.PrefetchScalarGridSpec(
            num_scalar_prefetch=3,
            grid=(rows // tile,),
            in_specs=specs + [ANY] * len(first),
            out_specs=(pl.BlockSpec((tile, width), lambda i, l1, l2, at: (i, 0)),) * 2,
            scratch_shapes=[
                pltpu.VMEM((listed * BLK, width), BF16),
                pltpu.VMEM((tile, 2 * width), F32),
            ],
        ),
        compiler_params=pltpu.CompilerParams(vmem_limit_bytes=56 * 2**20),
        cost_estimate=FREE,
        name="lower_slots",
    )(list1, list2, at, *([ancestor] * (2 * listed)), panels, panels, link, *first)


def strip_body(strip, w_ref, a_ref, *refs):
    total = mm(w_ref[...], a_ref[...])
    for ref in refs[:-1]:
        total = total + ref[...].astype(F32)
    refs[-1][...] = total.astype(BF16)


def strip_product(ancestor, placed, strip, strips, *added):
    rows, columns = ancestor.shape
    strip_width = columns // strips
    height = placed.shape[0]
    if strip_width % BLK:
        total = mm(
            placed, lax.dynamic_slice_in_dim(ancestor, strip * strip_width, strip_width, 1)
        )
        for each in added:
            total = total + each.astype(F32)
        return total.astype(BF16)
    tile = largest_tile(strip_width, 256)
    per = strip_width // tile
    return pl.pallas_call(
        strip_body,
        out_shape=jax.ShapeDtypeStruct((height, strip_width), BF16),
        grid_spec=pltpu.PrefetchScalarGridSpec(
            num_scalar_prefetch=1,
            grid=(per,),
            in_specs=[
                pl.BlockSpec((height, rows), lambda j, s: (0, 0)),
                pl.BlockSpec((rows, tile), lambda j, s: (0, s[0] * per + j)),
            ]
            + [pl.BlockSpec((height, tile), lambda j, s: (0, j))] * len(added),
            out_specs=pl.BlockSpec((height, tile), lambda j, s: (0, j)),
        ),
        compiler_params=pltpu.CompilerParams(vmem_limit_bytes=40 * 2**20),
        cost_estimate=pl.CostEstimate(
            flops=2 * height * rows * strip_width,
            bytes_accessed=2 * (rows * strip_width + height * rows)
            + 2 * (1 + len(added)) * height * strip_width,
            transcendentals=0,
        ),
        name="strip_product",
    )(jnp.reshape(strip, (1,)).astype(jnp.int32), placed, ancestor, *added)


def add_pair(left, right):
    return (left.astype(F32) + right.astype(F32)).astype(BF16)


def upper_sums(ancestor, placed):
    strips = lax.axis_size("rows")
    row_at = lax.axis_index("rows")
    inner = 4 if strips % 4 == 0 else 1
    if inner == 1:
        whole = strip_product(ancestor, placed, 0, 1)
        whole = whole.astype(F32)
        return lax.psum_scatter(whole, "rows", scatter_dimension=1, tiled=True), []
    depth = strips // inner
    core, side, level = row_at % 2, (row_at // 2) % 2, row_at // 4
    to_core = [(i, i ^ 1) for i in range(strips)]
    to_side = [(i, i ^ 2) for i in range(strips)]
    order = [sorted(range(depth), key=lambda d: (-abs(d - z), d)) for z in range(depth)]
    place = [[order[z].index(d) for d in range(depth)] for z in range(depth)]
    order_table = jnp.array(order, jnp.int32)

    def strip_of(target, x, c):
        return (target * 2 + x) * 2 + c

    layer, marks = [], []
    for turn in range(depth):
        target = order_table[level, turn]
        far = strip_product(ancestor, placed, strip_of(target, 1 - side, 1 - core), strips)
        far = lax.ppermute(far, "rows", to_core)
        near = strip_product(ancestor, placed, strip_of(target, side, 1 - core), strips)
        near = lax.ppermute(near, "rows", to_core)
        far = strip_product(ancestor, placed, strip_of(target, 1 - side, core), strips, far)
        marks.append(far)
        far = lax.ppermute(far, "rows", to_side)
        layer.append(
            strip_product(ancestor, placed, strip_of(target, side, core), strips, near, far)
        )

    def own_part(step, way):
        gap = depth - 1 - step
        chosen = None
        for z in range(depth):
            target = z + way * gap
            if 0 <= target < depth:
                value = layer[place[z][target]]
                chosen = value if chosen is None else jnp.where(level == z, value, chosen)
        return chosen

    arrived = {1: None, -1: None}
    for step in range(depth - 1):
        gap = depth - 1 - step
        for way in (1, -1):
            senders = [z for z in range(depth) if 0 <= z + way * gap < depth]
            pairs = [
                (z * inner + i, (z + way) * inner + i) for z in senders for i in range(inner)
            ]
            value = own_part(step, way)
            if arrived[way] is not None:
                value = add_pair(value, arrived[way])
            arrived[way] = lax.ppermute(value, "rows", pairs)
    total = layer[-1].astype(F32)
    for way in (1, -1):
        if arrived[way] is not None:
            total = total + arrived[way].astype(F32)
    return total, marks[:2]


def body(
    ancestor,
    panel_below,
    panel_beside,
    inverse_lower,
    inverse_upper,
    list_below,
    list_beside,
    second_below,
    second_beside,
    linked_below,
    linked_beside,
    second_lower,
    second_upper,
    blocks_below,
    blocks_beside,
):
    row_at = lax.axis_index("rows")
    col_at = lax.axis_index("cols")
    cols = lax.axis_size("cols")
    tile_rows, tile_cols = ancestor.shape
    width = inverse_lower.shape[0]
    half = width // cols

    beside = gather_pair((panel_beside, inverse_upper), (second_beside, second_upper), mm_rows)
    below = gather_pair((panel_below, inverse_lower), (second_below, second_lower), mm)
    link_below = mm(linked_below, second_lower).astype(BF16)
    link_beside = mm_rows(linked_beside, second_upper).astype(BF16)

    placed = place_panels(
        beside, link_beside, list_beside, blocks_beside,
        row_at * tile_rows, tile_rows,
    )
    upper, marks = upper_sums(ancestor, placed)
    new_upper = upper[:width].T.astype(BF16)
    next_upper = upper[width:].T.astype(BF16)

    given, kept = lower_slots(
        ancestor, below, link_below, list_below, blocks_below,
        col_at * (tile_cols // BLK), col_at, marks,
    )

    def small_sums(piece):
        return jnp.concatenate(
            [mm(placed[:width], piece), mm(placed[width:], piece[:, half:])], axis=1
        )

    def other_column(value):
        return lax.ppermute(value, "cols", [(i, i ^ 1) for i in range(cols)])

    sums_total = small_sums(kept) + other_column(small_sums(given).astype(BF16)).astype(F32)
    lower_total = kept.astype(F32) + other_column(given).astype(F32)
    new_lower = lower_total[:, :half].astype(BF16)
    next_lower = lower_total[:, half:].astype(BF16)

    sums = lax.psum(sums_total, "rows")

    def own(matrix):
        return lax.dynamic_slice_in_dim(matrix, col_at * half, half, 1)

    base = mm(inverse_upper, inverse_lower).astype(BF16)
    base_link = mm(base, own(link_below))
    new_diagonal = (mm(inverse_upper, own(inverse_lower)) + sums[:, :half]).astype(BF16)
    link_part = (sums[:, half : 2 * half] - base_link).astype(BF16)
    next_link = lax.all_gather(link_part, "cols", axis=1, tiled=True)
    next_diagonal = (
        mm(second_upper, own(second_lower))
        + mm_first(link_beside, base_link.astype(BF16))
        + sums[:, 2 * half :]
    ).astype(BF16)
    return (new_lower, new_upper, new_diagonal, next_lower, next_upper, next_link, next_diagonal)


def solution(mesh):
    return jax.shard_map(
        body,
        mesh=mesh,
        in_specs=(
            P("rows", "cols"),
            P("rows", None),
            P("rows", None),
            P(),
            P(),
            P(),
            P(),
            P("rows", None),
            P("rows", None),
            P(),
            P(),
            P(),
            P(),
            P(),
            P(),
        ),
        out_specs=(
            P("rows", "cols"),
            P(("cols", "rows"), None),
            P(None, "cols"),
            P("rows", "cols"),
            P(("cols", "rows"), None),
            P(),
            P(None, "cols"),
        ),
        check_vma=False,
    )
```
